32 devices in a mesh: gx: 4 (over y, x), gy: 4 (over z), gz: 2 (over core).
Axes of the slice: x: 2, y: 2, z: 4, core: 2. Of those that a mesh axis runs over, the one named last changes fastest.
Arguments:
- point_feats: bfloat16 [32, 262144], P(None, ('gx', 'gy', 'gz')), may hold values from -40 to 40
- voxel_ids: int32 [262144], P(('gx', 'gy', 'gz')), may hold values from 0 to 4095
- send_counts: int32 [32, 32], P(('gx', 'gy', 'gz')), may hold values from 0 to 256, as said below
- active: int32 [16, 16, 512], P('gx', 'gy', 'gz'), may hold values from 0 to 1
- w_sub: bfloat16 [64, 864], replicated, may hold values from -0.21875 to 0.21875
- w_down: bfloat16 [64, 512], replicated, may hold values from -0.25 to 0.25
- bn_gain: float32 [64], replicated, may hold values from 0.4 to 1.6
- bn_shift: float32 [64], replicated, may hold values from -2.5 to 2.5
- cotangent: bfloat16 [64, 8, 8, 256], P(None, 'gx', 'gy', 'gz'), may hold values from -6 to 6
Outputs:
- coarse_out: bfloat16 [64, 8, 8, 256], P(None, 'gx', 'gy', 'gz')
- grad_points: bfloat16 [32, 262144], P(None, ('gx', 'gy', 'gz'))
- grad_sub: float32 [64, 864], replicated
- grad_down: float32 [64, 512], replicated
- grad_gain: float32 [64], replicated
- grad_shift: float32 [64], replicated
The draws below stay inside these ranges and needn't reach their ends.
Inputs may be any that keep to these rules, and one draw needn't show every extreme that they name: The slots for destination d are the 256 slots from d * 256 on; the first send_counts[src, d] of them hold points. Some destination device gets 256 points from every source device.
All inputs are finite; a program needn't handle non-finite values.
Results may differ from the reference program's by a relative error of at most 0.009.
Values may be sent and summed in bfloat16 or wider, within the bound.
No kernel may reach another device: no remote copies, remote signals or barrier semaphores. Data moves between devices by JAX's collectives and lax.ppermute only.
A program may use at most 192 MiB of HBM per device.

```python
import math
import jax
import jax.numpy as jnp
from jax import lax

CIN = 32
COUT = 64
BX = 4
BY = 4
BZ = 256
SLOTS = 8192
CAP = 256
NX = 16
NY = 16
NZ = 512
N_GY = 4
N_GZ = 2
DEVICES = 32


def draw_point_feats(key, part):
    keys = jax.random.split(key, 3)
    chan_scale = jnp.exp(jax.random.uniform(keys[0], (CIN, 1), jnp.float32, 0.0, math.log(10.0)))
    dest_scale = jnp.exp(jax.random.uniform(keys[1], (DEVICES,), jnp.float32, 0.0, math.log(10.0)))
    destination = jnp.arange(DEVICES * SLOTS, dtype=jnp.int32) % SLOTS // CAP
    base = jnp.clip(jax.random.normal(keys[2], (CIN, DEVICES * SLOTS), jnp.float32), -4.0, 4.0)
    values = base * chan_scale * dest_scale[destination][None, :] * 0.1
    return values.astype(jnp.bfloat16)


def draw_send_counts(key, part):
    keys = jax.random.split(key, 4)
    busy = jax.random.randint(keys[0], (1, DEVICES), 0, 4) == 0
    heavy = jax.random.randint(keys[1], (DEVICES, DEVICES), CAP // 2, CAP + 1)
    light = jax.random.randint(keys[2], (DEVICES, DEVICES), CAP // 8, CAP // 2 + 1)
    filled = jax.random.randint(keys[3], (1, 1), 0, DEVICES)
    counts = jnp.where(busy, heavy, light)
    column = jnp.arange(DEVICES, dtype=jnp.int32)[None, :]
    return jnp.where(column == filled, CAP, counts).astype(jnp.int32)


def draw_active(key, part):
    level_x = jnp.arange(NX, dtype=jnp.int32) * 4 // NX
    level_y = jnp.arange(NY, dtype=jnp.int32) * 4 // NY
    level_z = jnp.arange(NZ, dtype=jnp.int32) * 4 // NZ
    level = level_x[:, None, None] + level_y[None, :, None] + level_z[None, None, :]
    threshold = 256 + 512 * level // 9
    drawn = jax.random.randint(key, (NX, NY, NZ), 0, 1024)
    return (drawn < threshold).astype(jnp.int32)


def draw_cotangent(key, part):
    keys = jax.random.split(key, 2)
    shape = (COUT, NX // 2, NY // 2, NZ // 2)
    offset = 0.8 * jnp.clip(jax.random.normal(keys[0], (COUT, 1, 1, 1), jnp.float32), -2.5, 2.5)
    base = jnp.clip(jax.random.normal(keys[1], shape, jnp.float32), -3.5, 3.5)
    return (base + offset).astype(jnp.bfloat16)


def with_ends(array, key, low, high):
    spot = [jax.random.randint(jax.random.fold_in(key, axis), (), 0, length) for axis, length in enumerate(array.shape)]
    widest = array.shape.index(max(array.shape))
    beside = spot[:widest] + [(spot[widest] + 1) % array.shape[widest]] + spot[widest + 1:]
    return array.at[tuple(spot)].set(low).at[tuple(beside)].set(high)


def bell_draw(own_key, dims, scale, reach, kind=jnp.bfloat16):
    entries = jax.random.normal(own_key, dims, jnp.float32) * scale
    return jnp.minimum(jnp.maximum(entries, -reach), reach).astype(kind)


def setup_inputs(seed: int = 0) -> dict:
    seeds = jax.random.split(jax.random.key(seed), 10)
    point_feats = draw_point_feats(jax.random.fold_in(seeds[9], 71), 0)
    voxel_ids = with_ends(jax.random.randint(seeds[1], (DEVICES * SLOTS,), 0, BX * BY * BZ), jax.random.fold_in(seeds[1], 1), 0, (BX * BY * BZ) - 1).astype(jnp.int32)
    send_counts = draw_send_counts(jax.random.fold_in(seeds[9], 71), 0)
    active = draw_active(jax.random.fold_in(seeds[9], 71), 0)
    w_sub = bell_draw(seeds[4], (COUT, 27 * CIN), (27 * CIN) ** -0.5, 0.21875)
    w_down = bell_draw(seeds[5], (COUT, 8 * COUT), (8 * COUT) ** -0.5, 0.25)
    bn_gain = jnp.clip(1.0 + 0.12 * jax.random.normal(seeds[6], (COUT,), jnp.float32), 0.4, 1.6)
    bn_shift = bell_draw(seeds[7], (COUT,), 0.5, 2.5, jnp.float32)
    cotangent = draw_cotangent(jax.random.fold_in(seeds[9], 71), 0)
    return {"point_feats": point_feats, "voxel_ids": voxel_ids, "send_counts": send_counts, "active": active, "w_sub": w_sub, "w_down": w_down, "bn_gain": bn_gain, "bn_shift": bn_shift, "cotangent": cotangent}


EPS = 1e-05
NUMBERS = ('NCDHW', 'OIDHW', 'NCDHW')

def sub_conv(field_in, kernel):
    return lax.conv_general_dilated(field_in[None], kernel, (1, 1, 1), [(1, 1), (1, 1), (1, 1)], dimension_numbers=NUMBERS, precision=lax.Precision.HIGHEST)[0]

def reference(point_feats, voxel_ids, send_counts, active, w_sub, w_down, bn_gain, bn_shift, cotangent):
    slot_rank = jnp.arange(CAP, dtype=jnp.int32)
    usable = (slot_rank[None, None, :] < send_counts[:, :, None]).reshape(-1)
    destination = jnp.tile(jnp.repeat(jnp.arange(DEVICES, dtype=jnp.int32), CAP), DEVICES)
    dest_x = destination // (N_GY * N_GZ)
    dest_y = destination // N_GZ % N_GY
    dest_z = destination % N_GZ
    local_x = voxel_ids // (BY * BZ)
    local_y = voxel_ids // BZ % BY
    local_z = voxel_ids % BZ
    flat_index = (((dest_x * BX + local_x) * NY + dest_y * BY + local_y) * NZ + dest_z * BZ + local_z).astype(jnp.int32)
    features = jnp.where(usable[None, :], point_feats.astype(jnp.float32), 0.0)
    summed = jax.ops.segment_sum(features.T, flat_index, num_segments=NX * NY * NZ)
    summed = summed.reshape(NX, NY, NZ, CIN).transpose(3, 0, 1, 2)
    activity = active.astype(jnp.float32)
    grid_in = (summed * activity[None]).astype(jnp.bfloat16)
    kernel = w_sub.astype(jnp.float32).reshape(COUT, 3, 3, 3, CIN).transpose(0, 4, 1, 2, 3)
    raw_hidden, conv_back = jax.vjp(sub_conv, grid_in.astype(jnp.float32), kernel)
    hidden = raw_hidden * activity[None]
    active_count = jnp.sum(activity)
    average = lax.optimization_barrier(jnp.sum(hidden, axis=(1, 2, 3))) / active_count
    centred = (hidden - average[:, None, None, None]) * activity[None]
    variance = lax.optimization_barrier(jnp.sum(centred * centred, axis=(1, 2, 3))) / active_count
    inverse = lax.rsqrt(variance + EPS)
    normed = (hidden - average[:, None, None, None]) * inverse[:, None, None, None]
    pre_act = bn_gain[:, None, None, None] * normed + bn_shift[:, None, None, None]
    gelu_val, gelu_back = jax.vjp(jax.nn.gelu, pre_act)
    fine_out = (gelu_val * activity[None]).astype(jnp.bfloat16)
    half_x, half_y, half_z = (NX // 2, NY // 2, NZ // 2)
    coarse_active = active.reshape(half_x, 2, half_y, 2, half_z, 2).max(axis=(1, 3, 5)).reshape(1, -1)
    fine_stack = fine_out.reshape(COUT, half_x, 2, half_y, 2, half_z, 2).transpose(2, 4, 6, 0, 1, 3, 5).reshape(8 * COUT, -1)
    coarse_sum = jnp.dot(w_down, fine_stack, preferred_element_type=jnp.float32) * coarse_active.astype(jnp.float32)
    coarse_out = coarse_sum.astype(jnp.bfloat16).reshape(COUT, half_x, half_y, half_z)
    grad_c = cotangent.reshape(COUT, -1) * coarse_active.astype(jnp.bfloat16)
    raw_down = lax.dot_general(grad_c, fine_stack, (((1,), (1,)), ((), ())), preferred_element_type=jnp.float32)
    grad_stack = jnp.dot(w_down.T, grad_c, preferred_element_type=jnp.float32)
    grad_fine = grad_stack.reshape(2, 2, 2, COUT, half_x, half_y, half_z).transpose(3, 4, 0, 5, 1, 6, 2).reshape(COUT, NX, NY, NZ)
    grad_pre = gelu_back(grad_fine * activity[None])[0]
    raw_shift = lax.optimization_barrier(jnp.sum(grad_pre, axis=(1, 2, 3)))
    raw_gain = lax.optimization_barrier(jnp.sum(grad_pre * normed, axis=(1, 2, 3)))
    grad_hidden = activity[None] * (bn_gain * inverse)[:, None, None, None] * (grad_pre - (raw_shift[:, None, None, None] + normed * raw_gain[:, None, None, None]) / active_count)
    grad_hidden = grad_hidden.astype(jnp.bfloat16)
    grad_field, grad_kernel = conv_back(grad_hidden.astype(jnp.float32))
    raw_sub = grad_kernel.transpose(0, 2, 3, 4, 1).reshape(COUT, 27 * CIN)
    grad_grid = (grad_field * activity[None]).astype(jnp.bfloat16)
    grad_points = jnp.where(usable[None, :], grad_grid.reshape(CIN, -1)[:, flat_index], jnp.zeros((), jnp.bfloat16))
    grad_scale = lax.rsqrt(active_count)
    return (coarse_out, grad_points, raw_sub * grad_scale, raw_down * grad_scale, raw_gain * grad_scale, raw_shift * grad_scale)
```

```python
import functools

import jax
import jax.numpy as jnp
from jax import lax
from jax.experimental import pallas as pl
from jax.experimental.pallas import tpu as pltpu
from jax.sharding import PartitionSpec as P

EPS = 1e-05
AXES = ("gx", "gy", "gz")
LANES = 128
GELU_SCALE = 0.7978845608028654
GELU_CUBE = 0.044715
F32 = jnp.float32
BF16 = jnp.bfloat16
NT = (((1,), (1,)), ((), ()))


def local_call(kernel, outs, *args, scratch=(), smem=(), limit=40, flops=0, moved=0):
    vmem = pl.BlockSpec(memory_space=pltpu.VMEM)
    scalar = pl.BlockSpec(memory_space=pltpu.SMEM)
    return pl.pallas_call(
        kernel,
        out_shape=[jax.ShapeDtypeStruct(shape, kind) for shape, kind in outs],
        in_specs=[scalar if i in smem else vmem for i in range(len(args))],
        out_specs=[vmem] * len(outs),
        scratch_shapes=[pltpu.VMEM(shape, kind) for shape, kind in scratch],
        compiler_params=pltpu.CompilerParams(vmem_limit_bytes=limit * 1024 * 1024),
        cost_estimate=pl.CostEstimate(
            flops=int(flops), bytes_accessed=int(moved), transcendentals=0
        ),
    )(*args)


def neighbours(axis, step):
    count = lax.axis_size(axis)
    return [(i, i + step) for i in range(count) if 0 <= i + step < count]


def exchange(low, high, axis):
    return (
        lax.ppermute(high, axis, neighbours(axis, 1)),
        lax.ppermute(low, axis, neighbours(axis, -1)),
    )


def z_exchange(low, high, swap):
    if lax.axis_size("gz") != 2:
        return exchange(low, high, "gz")
    got = lax.ppermute(swap, "gz", [(0, 1), (1, 0)])
    return got, got


def everyone(block):
    return lax.all_to_all(block, AXES, split_axis=0, concat_axis=0, tiled=True)


def pack_kernel(halves, groups, depth, counts_ref, feats_ref, ids_ref, out_ref):
    devices = out_ref.shape[0]
    chan = feats_ref.shape[0]
    rank = lax.broadcasted_iota(jnp.int32, (halves, LANES), 0) * LANES + lax.broadcasted_iota(
        jnp.int32, (halves, LANES), 1
    )
    blank = jnp.zeros((8 - 2 * halves, LANES), F32)
    for d in range(devices):
        for h in range(halves):
            first = (d * halves + h) * LANES
            out_ref[d, h * chan : (h + 1) * chan, :] = feats_ref[:, first : first + LANES]
        ids = ids_ref[d * halves : (d + 1) * halves, :]
        usable = rank < counts_ref[0, d]
        group = jnp.where(usable, ids // depth, groups).astype(F32)
        place = (ids % depth).astype(F32)
        tags = jnp.concatenate([group, place, blank], axis=0)
        out_ref[d, halves * chan :, :] = tags.astype(BF16)


def pack_plain(feats, ids, counts, groups, depth):
    chan, total = feats.shape
    devices = counts.shape[1]
    cap = total // devices
    ids = ids.reshape(devices, 1, cap)
    rank = jnp.arange(cap, dtype=jnp.int32)[None, None, :]
    group = jnp.where(rank < counts.reshape(devices, 1, 1), ids // depth, groups)
    tags = jnp.concatenate([group, ids % depth], axis=1).astype(BF16)
    rows = feats.reshape(chan, devices, cap).transpose(1, 0, 2)
    return jnp.concatenate([rows, jnp.pad(tags, ((0, 0), (0, 6), (0, 0)))], axis=1)


def scatter_kernel(halves, chan, size_y, recv_ref, act_ref, low_ref, high_ref, acc, masked, hot):
    chunks = recv_ref.shape[0]
    groups, depth = act_ref.shape
    per_step = masked.shape[1] // (halves * LANES)
    steps = chunks // per_step
    place = lax.broadcasted_iota(jnp.int32, (depth, LANES), 0).astype(F32)

    def step(s, carry):
        for j in range(per_step):
            block = recv_ref[s * per_step + j]
            tags = block[halves * chan :, :].astype(F32)
            for h in range(halves):
                feats = block[h * chan : (h + 1) * chan, :]
                col = (j * halves + h) * LANES
                group = jnp.broadcast_to(tags[h : h + 1, :], (chan, LANES)).astype(BF16)
                for k in range(groups):
                    masked[k * chan : (k + 1) * chan, col : col + LANES] = jnp.where(
                        group == k, feats, jnp.zeros_like(feats)
                    )
                low = tags[halves + h : halves + h + 1, :]
                hot[:, col : col + LANES] = jnp.where(place == low, 1.0, 0.0).astype(BF16)
        part = lax.dot_general(masked[...], hot[...], NT, preferred_element_type=F32)

        @pl.when(s == 0)
        def _():
            acc[...] = part

        @pl.when(s > 0)
        def _():
            acc[...] += part

        return carry

    lax.fori_loop(0, steps, step, 0)
    half = size_y // 2
    for k in range(groups):
        p, q = k // size_y, k % size_y
        out_ref = low_ref if p < 2 else high_ref
        row = ((q // half) * 4 + (p % 2) * 2 + q % half) * chan
        out_ref[row : row + chan, :] = (
            acc[k * chan : (k + 1) * chan, :] * act_ref[k : k + 1, :]
        ).astype(BF16)


def coarse_kernel(act_ref, cot_ref, low_ref, high_ref, grad_ref, mask_ref):
    depth = act_ref.shape[1]
    chan = cot_ref.shape[2]
    fine = lax.broadcasted_iota(jnp.int32, (depth, LANES), 0) // 2
    pair = (fine == lax.broadcasted_iota(jnp.int32, (depth, LANES), 1)).astype(BF16)
    acts = act_ref[...]
    sums = jnp.dot(acts.astype(BF16), pair, preferred_element_type=F32)
    masks = []
    for x in range(2):
        for y in range(2):
            rows = [sums[(2 * x + a) * 4 + 2 * y + b] for a in range(2) for b in range(2)]
            any_row = (rows[0] + rows[1] + rows[2] + rows[3])[None, :]
            mask = jnp.where(any_row > 0.5, 1.0, 0.0)
            masks.append(mask)
            grad = (cot_ref[x, y].astype(F32) * mask).astype(BF16)
            first = (x * 2 + y) * chan
            grad_ref[first : first + chan, :] = grad
            out_ref = low_ref if x == 0 else high_ref
            out_ref[y * chan : (y + 1) * chan, :] = grad
    mask_ref[...] = jnp.concatenate(masks + [jnp.zeros((4, LANES), F32)], axis=0)
    blank = jnp.zeros((8, LANES), F32)
    for out_ref, p in ((low_ref, 0), (high_ref, 3)):
        rows = acts[4 * p : 4 * p + 4]
        tail = jnp.concatenate([rows[:, :LANES], rows[:, LANES:], blank], axis=0)
        out_ref[2 * chan :, :] = tail.astype(BF16)


def coarse_rows_kernel(act_ref, grad_ref, before_ref, after_ref, low_ref, high_ref):
    chan = grad_ref.shape[0] // 4
    for out_ref, y, q in ((low_ref, 0, 0), (high_ref, 1, 3)):
        out_ref[0:chan, :] = before_ref[y * chan : (y + 1) * chan, :]
        out_ref[chan : 2 * chan, :] = grad_ref[y * chan : (y + 1) * chan, :]
        out_ref[2 * chan : 3 * chan, :] = grad_ref[(2 + y) * chan : (3 + y) * chan, :]
        out_ref[3 * chan : 4 * chan, :] = after_ref[y * chan : (y + 1) * chan, :]
        before = before_ref[2 * chan :, :].astype(F32)
        after = after_ref[2 * chan :, :].astype(F32)
        acts = act_ref[...]
        rows = [before[q : q + 1], before[4 + q : 5 + q]]
        for p in range(4):
            rows += [acts[4 * p + q : 4 * p + q + 1, :LANES], acts[4 * p + q : 4 * p + q + 1, LANES:]]
        rows += [after[q : q + 1], after[4 + q : 5 + q], jnp.zeros((4, LANES), F32)]
        out_ref[4 * chan :, :] = jnp.concatenate(rows, axis=0).astype(BF16)


def fine_grad_kernel(
    act_ref, grad_ref, xb_ref, xa_ref, yb_ref, ya_ref, down_ref, fine_ref, acts_ref, up
):
    chan = grad_ref.shape[0] // 4
    depth = act_ref.shape[1]
    acts = act_ref[...]
    xb = xb_ref[2 * chan :, :].astype(F32)
    xa = xa_ref[2 * chan :, :].astype(F32)
    yb = yb_ref[4 * chan :, :].astype(F32)
    ya = ya_ref[4 * chan :, :].astype(F32)
    rows = []
    for p in range(6):
        rows.append(jnp.concatenate([yb[2 * p : 2 * p + 1], yb[2 * p + 1 : 2 * p + 2]], axis=1))
        for q in range(4):
            if p in (0, 5):
                got = xb if p == 0 else xa
                rows.append(jnp.concatenate([got[q : q + 1], got[4 + q : 5 + q]], axis=1))
            else:
                rows.append(acts[4 * (p - 1) + q : 4 * (p - 1) + q + 1])
        rows.append(jnp.concatenate([ya[2 * p : 2 * p + 1], ya[2 * p + 1 : 2 * p + 2]], axis=1))
    rows.append(jnp.zeros((4, depth), F32))
    acts_ref[...] = jnp.concatenate(rows, axis=0)
    coarse = lax.broadcasted_iota(jnp.int32, (LANES, depth), 0)
    fine = lax.broadcasted_iota(jnp.int32, (LANES, depth), 1)
    spread = [(2 * coarse + c == fine).astype(BF16) for c in range(2)]
    for x in range(4):
        for y in range(4):
            if y in (0, 3):
                got = yb_ref if y == 0 else ya_ref
                block = got[x * chan : (x + 1) * chan, :]
            elif x in (0, 3):
                got = xb_ref if x == 0 else xa_ref
                block = got[(y - 1) * chan : y * chan, :]
            else:
                first = ((x - 1) * 2 + y - 1) * chan
                block = grad_ref[first : first + chan, :]
            for c in range(2):
                up[c * chan : (c + 1) * chan, :] = jnp.dot(
                    block, spread[c], preferred_element_type=F32
                ).astype(BF16)
            for a in range(2):
                p = 2 * x + a - 1
                for b in range(2):
                    q = 2 * y + b - 1
                    if 0 <= p < 6 and 0 <= q < 6:
                        first = (a * 2 + b) * chan
                        row = (p * 6 + q) * chan
                        fine_ref[row : row + chan, :] = jnp.dot(
                            down_ref[first : first + chan, :], up[...], preferred_element_type=F32
                        )


def bands_kernel(front_ref, back_ref, bands_ref, back_bands_ref):
    rows, width = front_ref.shape[0], front_ref.shape[1] // 9
    back_rows, back_width = back_ref.shape[0], back_ref.shape[1] // 9
    for t in range(9):
        block = front_ref[:, t * width : (t + 1) * width].astype(F32)
        for q in range(6):
            moved = pltpu.roll(block, q * back_rows, 1) if q else block
            bands_ref[q * rows : (q + 1) * rows, t * width : (t + 1) * width] = moved.astype(BF16)
        block = back_ref[:, t * back_width : (t + 1) * back_width].astype(F32)
        for q in range(4):
            moved = pltpu.roll(block, q * rows, 1) if q else block
            back_bands_ref[
                q * back_rows : (q + 1) * back_rows, t * back_width : (t + 1) * back_width
            ] = moved.astype(BF16)


def band_inputs(w_sub, in_chan):
    out_chan = w_sub.shape[0]
    taps = w_sub.reshape(out_chan, 3, 3, 3, in_chan)
    front = taps.transpose(0, 1, 3, 2, 4).reshape(out_chan, 9, 3 * in_chan)
    front = jnp.pad(front, ((0, 0), (0, 0), (0, 5 * in_chan)))
    back = taps[:, ::-1, ::-1].transpose(4, 1, 3, 2, 0).reshape(in_chan, 9, 3 * out_chan)
    back = jnp.pad(back, ((0, 0), (0, 0), (0, 3 * out_chan)))
    return front.reshape(out_chan, -1), back.reshape(in_chan, -1)


def rows_kernel(b_ref, low_ref, high_ref, a_ref, out_low_ref, out_high_ref):
    half = b_ref.shape[0] // 2
    for n, ref in enumerate((b_ref, low_ref, high_ref, a_ref)):
        out_low_ref[n * half : (n + 1) * half, :] = ref[:half, :]
        out_high_ref[n * half : (n + 1) * half, :] = ref[half:, :]


def columns_kernel(
    chan, place_ref, b_ref, low_ref, high_ref, a_ref, yb_ref, ya_ref, front_ref, rear_ref, swap_ref
):
    for n, ref in enumerate((b_ref, low_ref, high_ref, a_ref)):
        for p in range(2):
            for y in range(8):
                if y in (0, 1, 6, 7):
                    got = yb_ref if y < 2 else ya_ref
                    row = (n * 4 + p * 2 + y % 2) * chan
                else:
                    got = ref
                    row = (((y - 2) // 2) * 4 + p * 2 + y % 2) * chan
                block = got[row : row + chan, :]
                to = ((n * 2 + p) * 8 + y) * chan
                front_ref[to : to + chan, :] = block[:, :LANES]
                rear_ref[to : to + chan, :] = block[:, LANES:]

    @pl.when(place_ref[0] == 0)
    def _():
        swap_ref[...] = rear_ref[...]

    @pl.when(place_ref[0] != 0)
    def _():
        swap_ref[...] = front_ref[...]


def shifted(low, high, before, after, step):
    lane = lax.broadcasted_iota(jnp.int32, low.shape, 1)
    if step > 0:
        turned = [pltpu.roll(tile.astype(F32), LANES - 1, 1) for tile in (low, high, after)]
        edge = lane == LANES - 1
        tiles = [jnp.where(edge, turned[1], turned[0]), jnp.where(edge, turned[2], turned[1])]
    else:
        turned = [pltpu.roll(tile.astype(F32), 1, 1) for tile in (before, low, high)]
        edge = lane == 0
        tiles = [jnp.where(edge, turned[0], turned[1]), jnp.where(edge, turned[1], turned[2])]
    return tiles[0].astype(BF16), tiles[1].astype(BF16)


def keep(tile, wanted):
    return jnp.where(wanted, tile, jnp.zeros_like(tile))


def to_rows(columns):
    lane = lax.broadcasted_iota(jnp.int32, (LANES, LANES), 1)
    wide = jnp.zeros((LANES, LANES), F32)
    for n, column in enumerate(columns):
        tall = jnp.concatenate([column, jnp.zeros((LANES - column.shape[0], 1), F32)], axis=0)
        wide = jnp.where(lane == n, tall, wide)
    return wide.T[:8, :]


def to_columns(rows, chan):
    wide = jnp.concatenate(rows + [jnp.zeros((LANES - len(rows), LANES), F32)], axis=0).T
    return [wide[:chan, n : n + 1] for n in range(len(rows))]


def conv_kernel(
    only_two, place_ref, low_ref, high_ref, before_ref, after_ref, bands_ref, acts_ref,
    hidden_ref, stack_ref, stats_ref,
):
    rows = low_ref.shape[0] // 8
    depth = acts_ref.shape[1]
    wide = bands_ref.shape[0]
    chan = wide // 6
    has_before = place_ref[0] != 0 if only_two else True
    has_after = place_ref[0] == 0 if only_two else True
    for x in range(8):
        own = slice(x * rows, (x + 1) * rows)
        low, high = low_ref[own, :], high_ref[own, :]
        before, after = before_ref[own, :], after_ref[own, :]
        if only_two:
            before, after = keep(before, has_before), keep(after, has_after)
        for n, step in enumerate((-1, 0, 1)):
            tiles = (low, high) if step == 0 else shifted(low, high, before, after, step)
            to = slice((x * 3 + n) * rows, (x * 3 + n + 1) * rows)
            stack_ref[to, :LANES] = tiles[0]
            stack_ref[to, LANES:] = tiles[1]
    total = jnp.zeros((chan, depth), F32)
    for p in range(6):
        first = p * 3 * rows
        out = jnp.dot(
            bands_ref[...], stack_ref[first : first + 9 * rows, :], preferred_element_type=F32
        )
        for q in range(6):
            block = out[q * chan : (q + 1) * chan] * acts_ref[p * 6 + q : p * 6 + q + 1, :]
            hidden_ref[p * wide + q * chan : p * wide + (q + 1) * chan, :] = block
            if 1 <= p <= 4 and 1 <= q <= 4:
                total = total + block
    count = jnp.zeros((1, depth), F32)
    for p in range(1, 5):
        for q in range(1, 5):
            count = count + acts_ref[p * 6 + q : p * 6 + q + 1, :]
    count = jnp.sum(count, axis=1, keepdims=True)
    total = jnp.sum(total, axis=1, keepdims=True)
    mean = total / jnp.maximum(count, 1.0)
    squares = jnp.zeros((chan, depth), F32)
    for p in range(1, 5):
        for q in range(1, 5):
            row = p * wide + q * chan
            centred = (hidden_ref[row : row + chan, :] - mean) * acts_ref[
                p * 6 + q : p * 6 + q + 1, :
            ]
            squares = squares + centred * centred
    squares = jnp.sum(squares, axis=1, keepdims=True)
    packed = to_rows([total, squares, jnp.broadcast_to(count, (chan, 1))])
    for d in range(stats_ref.shape[0]):
        stats_ref[d] = packed


def merged_stats(stats_ref):
    totals, squares, counts = stats_ref[:, 0, :], stats_ref[:, 1, :], stats_ref[:, 2, :]
    count = jnp.sum(counts, axis=0, keepdims=True)
    average = jnp.sum(totals, axis=0, keepdims=True) / count
    off = totals / jnp.maximum(counts, 1.0) - average
    spread = jnp.sum(squares + counts * off * off, axis=0, keepdims=True)
    return count, average, lax.rsqrt(spread / count + EPS)


def norm_kernel(
    stats_ref, gain_ref, shift_ref, hidden_ref, fine_ref, acts_ref, pre_ref, out_ref, sums_ref
):
    chan = gain_ref.shape[0]
    depth = acts_ref.shape[1]
    count, average, inverse = merged_stats(stats_ref)
    average, inverse = to_columns([average, inverse], chan)
    full = (chan, LANES)
    average, inverse = jnp.broadcast_to(average, full), jnp.broadcast_to(inverse, full)
    gain, shift = jnp.broadcast_to(gain_ref[...], full), jnp.broadcast_to(shift_ref[...], full)
    sum_shift = jnp.zeros((chan, LANES), F32)
    sum_gain = jnp.zeros((chan, LANES), F32)
    for p in range(6):
        for q in range(6):
            row = (p * 6 + q) * chan
            for half in range(depth // LANES):
                lanes = slice(half * LANES, (half + 1) * LANES)
                act = acts_ref[p * 6 + q : p * 6 + q + 1, lanes]
                normed = (hidden_ref[row : row + chan, lanes] - average) * inverse
                x = gain * normed + shift
                square = x * x
                bent = jnp.tanh(GELU_SCALE * (x + GELU_CUBE * (square * x)))
                cdf = 0.5 + 0.5 * bent
                slope = cdf + (0.5 * x) * (1.0 - bent * bent) * (
                    GELU_SCALE + (3.0 * GELU_CUBE * GELU_SCALE) * square
                )
                grad = (act * slope) * fine_ref[row : row + chan, lanes]
                pre_ref[row : row + chan, lanes] = grad
                if 1 <= p <= 4 and 1 <= q <= 4:
                    sum_shift = sum_shift + grad
                    sum_gain = sum_gain + grad * normed
                    to = ((p - 1) * 4 + q - 1) * chan
                    out_ref[to : to + chan, lanes] = (x * cdf * act).astype(BF16)
    sums = to_rows(
        [jnp.sum(sum_shift, axis=1, keepdims=True), jnp.sum(sum_gain, axis=1, keepdims=True)]
    )
    for d in range(sums_ref.shape[0]):
        sums_ref[d] = sums


def down_kernel(out_ref, grad_ref, mask_ref, down_ref, coarse_ref, raw_ref, stack):
    depth = out_ref.shape[1]
    chan = grad_ref.shape[0] // 4
    source = lax.broadcasted_iota(jnp.int32, (depth, depth), 0)
    target = lax.broadcasted_iota(jnp.int32, (depth, depth), 1)
    wanted = jnp.where(target < LANES, 2 * target, 2 * (target - LANES) + 1)
    sort = (source == wanted).astype(BF16)
    for x in range(2):
        for y in range(2):
            for a in range(2):
                for b in range(2):
                    row = ((2 * x + a) * 4 + 2 * y + b) * chan
                    parted = jnp.dot(
                        out_ref[row : row + chan, :], sort, preferred_element_type=F32
                    ).astype(BF16)
                    lanes = slice((x * 2 + y) * LANES, (x * 2 + y + 1) * LANES)
                    to = (a * 4 + b * 2) * chan
                    stack[to : to + chan, lanes] = parted[:, :LANES]
                    stack[to + chan : to + 2 * chan, lanes] = parted[:, LANES:]
    sums = jnp.dot(down_ref[...], stack[...], preferred_element_type=F32)
    for n in range(4):
        coarse_ref[n] = (sums[:, n * LANES : (n + 1) * LANES] * mask_ref[n : n + 1, :]).astype(
            BF16
        )
    grads = jnp.concatenate([grad_ref[n * chan : (n + 1) * chan, :] for n in range(4)], axis=1)
    raw = lax.dot_general(grads, stack[...], NT, preferred_element_type=F32)
    for n in range(4):
        raw_ref[n * chan : (n + 1) * chan, :] = raw[:, n * LANES : (n + 1) * LANES]


def hidden_grad_kernel(
    place_ref, stats_ref, sums_ref, gain_ref, hidden_ref, pre_ref, acts_ref,
    front_ref, rear_ref, swap_ref, small_ref,
):
    chan = gain_ref.shape[0]
    count, average, inverse = merged_stats(stats_ref)
    raw_shift = jnp.sum(sums_ref[:, 0, :], axis=0, keepdims=True)
    raw_gain = jnp.sum(sums_ref[:, 1, :], axis=0, keepdims=True)
    scale = lax.rsqrt(count)
    small_ref[...] = jnp.concatenate(
        [raw_shift * scale, raw_gain * scale, scale, jnp.zeros((5, LANES), F32)], axis=0
    )
    columns = to_columns([average, inverse, raw_shift / count, raw_gain / count], chan)
    average, inverse, mean_shift, mean_gain = [
        jnp.broadcast_to(column, (chan, LANES)) for column in columns
    ]
    weight = jnp.broadcast_to(gain_ref[...], (chan, LANES)) * inverse
    for n in range(36):
        row = n * chan
        for half, out_ref in enumerate((front_ref, rear_ref)):
            lanes = slice(half * LANES, (half + 1) * LANES)
            act = acts_ref[n : n + 1, lanes]
            normed = (hidden_ref[row : row + chan, lanes] - average) * inverse
            grad = pre_ref[row : row + chan, lanes] - (mean_shift + normed * mean_gain)
            out_ref[row : row + chan, :] = ((act * weight) * grad).astype(BF16)

    @pl.when(place_ref[0] == 0)
    def _():
        swap_ref[...] = rear_ref[...]

    @pl.when(place_ref[0] != 0)
    def _():
        swap_ref[...] = front_ref[...]


def weight_grad_kernel(in_chan, stack_ref, front_ref, rear_ref, raw_ref, out_ref, acc):
    chan = front_ref.shape[0] // 36
    rows = stack_ref.shape[0] // 8
    band = rows // 3
    for p in range(4):
        own = slice(((p + 1) * 6 + 1) * chan, ((p + 1) * 6 + 5) * chan)
        grads = jnp.concatenate([front_ref[own, :], rear_ref[own, :]], axis=1)
        for dx in range(3):
            first = (p + 1 + dx) * rows
            part = lax.dot_general(
                stack_ref[first : first + rows, :], grads, NT, preferred_element_type=F32
            )
            if p == 0:
                acc[dx] = part
            else:
                acc[dx] += part
    low = lax.broadcasted_iota(jnp.int32, (in_chan, LANES), 1) < chan
    for dx in range(3):
        for dy in range(3):
            for dz in range(3):
                blocks = []
                for q in range(4):
                    row = dz * band + (q + 1 + dy) * in_chan
                    lanes = slice((q // 2) * LANES, (q // 2 + 1) * LANES)
                    blocks.append(acc[dx, row : row + in_chan, lanes])
                both = jnp.where(low, blocks[0] + blocks[2], blocks[1] + blocks[3])
                folded = both + pltpu.roll(both, chan, 1)
                tap = (dx * 3 + dy) * 3 + dz
                if tap < 16:
                    out_ref[tap * in_chan : (tap + 1) * in_chan, :chan] = folded[:, :chan]
                else:
                    to = (tap - 16) * in_chan
                    out_ref[to : to + in_chan, chan:] = folded[:, chan:]
    out_ref[11 * in_chan : 16 * in_chan, chan:] = jnp.zeros((5 * in_chan, LANES - chan), F32)
    tail = 16 * in_chan
    out_ref[tail : tail + 4 * chan, :] = raw_ref[...]
    if tail + 4 * chan < out_ref.shape[0]:
        out_ref[tail + 4 * chan :, :] = jnp.zeros(
            (out_ref.shape[0] - tail - 4 * chan, LANES), F32
        )


def point_grad_kernel(
    only_two, halves, chan, place_ref, front_ref, rear_ref, before_ref, after_ref, bands_ref, act_ref,
    recv_ref, out_ref, stack, cells,
):
    rows = front_ref.shape[0] // 6
    groups, depth = act_ref.shape
    has_before = place_ref[0] != 0 if only_two else True
    has_after = place_ref[0] == 0 if only_two else True
    for x in range(6):
        own = slice(x * rows, (x + 1) * rows)
        low, high = front_ref[own, :], rear_ref[own, :]
        before, after = before_ref[own, :], after_ref[own, :]
        if only_two:
            before, after = keep(before, has_before), keep(after, has_after)
        for n, step in enumerate((1, 0, -1)):
            tiles = (low, high) if step == 0 else shifted(low, high, before, after, step)
            to = slice((x * 3 + n) * rows, (x * 3 + n + 1) * rows)
            stack[to, :LANES] = tiles[0]
            stack[to, LANES:] = tiles[1]
    for p in range(4):
        first = p * 3 * rows
        grid = jnp.dot(
            bands_ref[...], stack[first : first + 9 * rows, :], preferred_element_type=F32
        )
        for q in range(4):
            k = p * 4 + q
            cells[k * chan : (k + 1) * chan, :] = (
                grid[q * chan : (q + 1) * chan] * act_ref[k : k + 1, :]
            ).astype(BF16)
    place = lax.broadcasted_iota(jnp.int32, (depth, LANES), 0).astype(F32)

    def step(d, carry):
        tags = recv_ref[d][halves * chan :, :].astype(F32)
        for h in range(halves):
            group = jnp.broadcast_to(tags[h : h + 1, :], (chan, LANES))
            low = tags[halves + h : halves + h + 1, :]
            hot = jnp.where(place == low, 1.0, 0.0).astype(BF16)
            found = jnp.dot(cells[...], hot, preferred_element_type=F32)
            out = jnp.zeros((chan, LANES), F32)
            for k in range(groups):
                out = jnp.where(group == k, found[k * chan : (k + 1) * chan], out)
            out_ref[d, h * chan : (h + 1) * chan, :] = out.astype(BF16)
        return carry

    lax.fori_loop(0, recv_ref.shape[0], step, 0)


def piece_kernel(parts_ref, points_ref, out_ref):
    rows = points_ref.shape[1]
    piece = jnp.sum(parts_ref[...], axis=0).astype(BF16)
    for d in range(out_ref.shape[0]):
        out_ref[d, :rows, :] = points_ref[d]
        out_ref[d, rows:, :] = piece


def sum_kernel(parts_ref, out_ref):
    piece = jnp.sum(parts_ref[...], axis=0).astype(BF16)
    for d in range(out_ref.shape[0]):
        out_ref[d] = piece


def weights_out(rows, small_ref, in_chan, sub_ref, down_ref):
    chan = down_ref.shape[0]
    scale = small_ref[2:3, 0:1]
    for n in range(4):
        turned = rows(n).T * scale
        sub_ref[:, n * LANES : (n + 1) * LANES] = turned[:chan]
        left = sub_ref.shape[1] - 16 * in_chan - n * LANES
        if left > 0:
            width = min(left, LANES)
            first = 16 * in_chan + n * LANES
            sub_ref[:, first : first + width] = turned[chan:, :width]
    for n in range(2):
        both = rows(4 + n) * scale
        down_ref[:, 2 * n * LANES : (2 * n + 1) * LANES] = both[:chan]
        down_ref[:, (2 * n + 1) * LANES : (2 * n + 2) * LANES] = both[chan:]


def last_kernel(halves, chan, got_ref, small_ref, points_ref, sub_ref, down_ref, flat):
    devices = got_ref.shape[0]
    piece = got_ref.shape[1] - halves * chan
    for d in range(devices):
        block = got_ref[d]
        for h in range(halves):
            first = (d * halves + h) * LANES
            points_ref[:, first : first + LANES] = block[h * chan : (h + 1) * chan, :]
        flat[d * piece : (d + 1) * piece, :] = block[halves * chan :, :].astype(F32)
    weights_out(lambda n: flat[n * LANES : (n + 1) * LANES, :], small_ref, chan, sub_ref, down_ref)


def weights_kernel(chan, got_ref, small_ref, sub_ref, down_ref, flat):
    piece = got_ref.shape[1]
    for d in range(got_ref.shape[0]):
        flat[d * piece : (d + 1) * piece, :] = got_ref[d].astype(F32)
    weights_out(lambda n: flat[n * LANES : (n + 1) * LANES, :], small_ref, chan, sub_ref, down_ref)


def on_device(
    point_feats, voxel_ids, send_counts, active, w_sub, w_down, bn_gain, bn_shift, cotangent
):
    in_chan, slot_total = point_feats.shape
    devices = send_counts.shape[1]
    slot_cap = slot_total // devices
    size_x, size_y, size_z = active.shape
    groups = size_x * size_y
    out_chan = w_sub.shape[0]
    only_two = lax.axis_size("gz") == 2
    place = lax.axis_index("gz").astype(jnp.int32).reshape(1)
    aligned = slot_cap % LANES == 0
    halves = slot_cap // LANES if aligned else 1

    if aligned:
        payload = local_call(
            functools.partial(pack_kernel, halves, groups, size_z),
            [((devices, halves * in_chan + 8, LANES), BF16)],
            send_counts, point_feats, voxel_ids.reshape(-1, LANES),
            smem=(0,), moved=2e6,
        )[0]
        recv = everyone(payload)
    else:
        payload = pack_plain(point_feats, voxel_ids, send_counts, groups, size_z)
        together = LANES // slot_cap
        recv = everyone(payload)
        recv = recv.reshape(devices // together, together, in_chan + 8, slot_cap)
        recv = recv.transpose(0, 2, 1, 3).reshape(devices // together, in_chan + 8, LANES)
    chunks = recv.shape[0]

    acts = active.reshape(groups, size_z).astype(F32)
    front, back = band_inputs(w_sub, in_chan)
    wide, back_wide = 6 * out_chan, 4 * in_chan
    bands, back_bands = local_call(
        bands_kernel,
        [((wide, 9 * 8 * in_chan), BF16), ((back_wide, 9 * 6 * out_chan), BF16)],
        front, back, moved=4e6,
    )
    cot = cotangent.transpose(1, 2, 0, 3)
    cot_low, cot_high, grad_c, coarse_mask = local_call(
        coarse_kernel,
        [((2 * out_chan + 16, LANES), BF16)] * 2
        + [((4 * out_chan, LANES), BF16), ((8, LANES), F32)],
        acts, cot, moved=2e5,
    )
    cot_xb, cot_xa = exchange(cot_low, cot_high, "gx")
    cot_low, cot_high = local_call(
        coarse_rows_kernel,
        [((4 * out_chan + 16, LANES), BF16)] * 2,
        acts, grad_c, cot_xb, cot_xa, moved=2e5,
    )
    cot_yb, cot_ya = exchange(cot_low, cot_high, "gy")
    by_child = (
        w_down.reshape(out_chan, 4, 2, out_chan)
        .transpose(1, 3, 2, 0)
        .reshape(4 * out_chan, 2 * out_chan)
    )
    fine_grad, acts_wide = local_call(
        fine_grad_kernel,
        [((36 * out_chan, size_z), F32), ((40, size_z), F32)],
        acts, grad_c, cot_xb, cot_xa, cot_yb, cot_ya, by_child,
        scratch=[((2 * out_chan, size_z), BF16)], moved=3e6,
    )

    per_step = min(chunks, 16 // halves)
    low, high = local_call(
        functools.partial(scatter_kernel, halves, in_chan, size_y),
        [((groups // 2 * in_chan, size_z), BF16)] * 2,
        recv, acts,
        scratch=[
            ((groups * in_chan, size_z), F32),
            ((groups * in_chan, per_step * halves * LANES), BF16),
            ((size_z, per_step * halves * LANES), BF16),
        ],
        moved=2e7,
    )
    below, above = exchange(low, high, "gx")
    row_low, row_high = local_call(
        rows_kernel,
        [((groups * in_chan, size_z), BF16)] * 2,
        below, low, high, above, moved=1e6,
    )
    left, right = exchange(row_low, row_high, "gy")
    all_rows = 64 * in_chan
    tile_low, tile_high, swap = local_call(
        functools.partial(columns_kernel, in_chan),
        [((all_rows, LANES), BF16)] * 3,
        place, below, low, high, above, left, right, smem=(0,), moved=3e6,
    )
    before, after = z_exchange(tile_low, tile_high, swap)

    hidden, stack, stats = local_call(
        functools.partial(conv_kernel, only_two),
        [((6 * wide, size_z), F32), ((3 * all_rows, size_z), BF16), ((devices, 8, LANES), F32)],
        place, tile_low, tile_high, before, after, bands, acts_wide, smem=(0,), moved=2e7,
    )
    stats = everyone(stats)
    gain, shift = bn_gain.reshape(-1, 1), bn_shift.reshape(-1, 1)
    grad_pre, fine_out, sums = local_call(
        norm_kernel,
        [
            ((6 * wide, size_z), F32),
            ((groups * out_chan, size_z), BF16),
            ((devices, 8, LANES), F32),
        ],
        stats, gain, shift, hidden, fine_grad, acts_wide, moved=1e7,
    )
    sums = everyone(sums)
    coarse, raw_down = local_call(
        down_kernel,
        [((4, out_chan, LANES), BF16), ((4 * out_chan, LANES), F32)],
        fine_out, grad_c, coarse_mask, w_down,
        scratch=[((8 * out_chan, 4 * LANES), BF16)], moved=5e6,
    )
    half_x, half_y, half_z = size_x // 2, size_y // 2, size_z // 2
    coarse_out = coarse.reshape(half_x, half_y, out_chan, half_z).transpose(2, 0, 1, 3)

    grad_low, grad_high, grad_swap, small = local_call(
        hidden_grad_kernel,
        [((6 * wide, LANES), BF16)] * 3 + [((8, LANES), F32)],
        place, stats, sums, gain, hidden, grad_pre, acts_wide, smem=(0,), moved=5e6,
    )
    grad_before, grad_after = z_exchange(grad_low, grad_high, grad_swap)
    piece = -(-(16 * in_chan + 4 * out_chan) // devices)
    piece = -(-piece // 8) * 8
    parts = local_call(
        functools.partial(weight_grad_kernel, in_chan),
        [((devices * piece, LANES), F32)],
        stack, grad_low, grad_high, raw_down,
        scratch=[((3, 24 * in_chan, 4 * out_chan), F32)], moved=1e7,
    )[0]
    parts = everyone(parts.reshape(devices, piece, LANES))

    points = local_call(
        functools.partial(point_grad_kernel, only_two, halves, in_chan),
        [((chunks, halves * in_chan, LANES), BF16)],
        place, grad_low, grad_high, grad_before, grad_after, back_bands, acts, recv,
        scratch=[((18 * wide, size_z), BF16), ((groups * in_chan, size_z), BF16)],
        smem=(0,), moved=2e7,
    )[0]
    shapes = [((out_chan, 27 * in_chan), F32), ((out_chan, 8 * out_chan), F32)]
    flat = [((devices * piece, LANES), F32)]
    if aligned:
        both = local_call(
            piece_kernel,
            [((devices, halves * in_chan + piece, LANES), BF16)],
            parts, points, moved=2e6,
        )[0]
        returned, raw_sub, raw_down = local_call(
            functools.partial(last_kernel, halves, in_chan),
            [((in_chan, slot_total), BF16)] + shapes,
            everyone(both), small, scratch=flat, moved=2e6,
        )
    else:
        points = points.reshape(chunks, in_chan, together, slot_cap).transpose(0, 2, 1, 3)
        returned = everyone(points.reshape(devices, in_chan, slot_cap))
        returned = returned.transpose(1, 0, 2).reshape(in_chan, slot_total)
        whole = local_call(sum_kernel, [((devices, piece, LANES), BF16)], parts)[0]
        raw_sub, raw_down = local_call(
            functools.partial(weights_kernel, in_chan), shapes, everyone(whole), small, scratch=flat
        )
    return (
        coarse_out,
        returned,
        raw_sub,
        raw_down,
        small[1, :out_chan],
        small[0, :out_chan],
    )


def solution(mesh):
    in_specs = (
        P(None, AXES),
        P(AXES),
        P(AXES, None),
        P("gx", "gy", "gz"),
        P(),
        P(),
        P(),
        P(),
        P(None, "gx", "gy", "gz"),
    )
    out_specs = (P(None, "gx", "gy", "gz"), P(None, AXES), P(), P(), P(), P())
    return jax.shard_map(
        on_device, mesh=mesh, in_specs=in_specs, out_specs=out_specs, check_vma=False
    )
```

```python
import functools
import math

import jax
import jax.numpy as jnp
from jax import lax
from jax.experimental import pallas as pl
from jax.experimental.pallas import tpu as pltpu
from jax.sharding import PartitionSpec as P

EPS = 1e-05
AXES = ("gx", "gy", "gz")
LANES = 128
GELU_SCALE = 0.7978845608028654
GELU_CUBE = 0.044715
F32 = jnp.float32
BF16 = jnp.bfloat16
NT = (((1,), (1,)), ((), ()))


def local_call(kernel, outs, *args, scratch=(), smem=(), hbm=(), hbm_outs=(), copies=0, moved=0):
    held = sum(math.prod(shape) * jnp.dtype(kind).itemsize for shape, kind in scratch)
    limit = held // 2**20 + 6
    vmem = pl.BlockSpec(memory_space=pltpu.VMEM)
    scalar = pl.BlockSpec(memory_space=pltpu.SMEM)
    far = pl.BlockSpec(memory_space=pltpu.HBM)
    args = [
        pltpu.with_memory_space_constraint(arg, pltpu.HBM) if i in hbm else arg
        for i, arg in enumerate(args)
    ]
    held = [pltpu.VMEM(shape, kind) for shape, kind in scratch]
    if copies:
        held.append(pltpu.SemaphoreType.DMA((copies,)))
    return pl.pallas_call(
        kernel,
        out_shape=[
            pltpu.HBM(shape, kind) if i in hbm_outs else jax.ShapeDtypeStruct(shape, kind)
            for i, (shape, kind) in enumerate(outs)
        ],
        in_specs=[
            scalar if i in smem else far if i in hbm else vmem for i in range(len(args))
        ],
        out_specs=[far if i in hbm_outs else vmem for i in range(len(outs))],
        scratch_shapes=held,
        compiler_params=pltpu.CompilerParams(vmem_limit_bytes=limit * 1024 * 1024),
        cost_estimate=pl.CostEstimate(flops=0, bytes_accessed=int(moved), transcendentals=0),
    )(*args)


def started(source, target, semaphore):
    copy = pltpu.make_async_copy(source, target, semaphore)
    copy.start()
    return copy


def rows_of(n, count):
    return pl.ds(n * count, count)


def neighbours(axis, step):
    count = lax.axis_size(axis)
    return [(i, i + step) for i in range(count) if 0 <= i + step < count]


def swaps(first, second, axis):
    count = lax.axis_size(axis)
    got = []
    for block, begin in ((first, 0), (second, 1)):
        pairs = [(i, i + 1) for i in range(begin, count - 1, 2)]
        got.append(lax.ppermute(block, axis, pairs + [(j, i) for i, j in pairs]))
    return got


def sided(odd, first, second):
    return jnp.where(odd, first, second), jnp.where(odd, second, first)


def z_exchange(low, high, swap):
    if lax.axis_size("gz") != 2:
        return (
            lax.ppermute(high, "gz", neighbours("gz", 1)),
            lax.ppermute(low, "gz", neighbours("gz", -1)),
        )
    got = lax.ppermute(swap, "gz", [(0, 1), (1, 0)])
    return got, got


def everyone(block):
    return lax.all_to_all(block, AXES, split_axis=0, concat_axis=0, tiled=True)


def pack_kernel(
    halves, groups, depth, counts_ref, feats_ref, ids_ref, out_ref, feats, ids, sems
):
    devices = out_ref.shape[0]
    chan = feats_ref.shape[0]
    parts = 4
    width = feats.shape[1] // parts
    got_ids = started(ids_ref, ids, sems.at[parts])
    got = []
    for n in range(parts):
        lanes = pl.ds(n * width, width)
        got.append(started(feats_ref.at[:, lanes], feats.at[:, lanes], sems.at[n]))
    got_ids.wait()
    rank = lax.broadcasted_iota(jnp.int32, (halves, LANES), 0) * LANES + lax.broadcasted_iota(
        jnp.int32, (halves, LANES), 1
    )
    blank = jnp.zeros((8 - 2 * halves, LANES), F32)
    for d in range(devices):
        those = ids[d * halves : (d + 1) * halves, :]
        usable = rank < counts_ref[0, d]
        group = jnp.where(usable, those // depth, groups).astype(F32)
        place = (those % depth).astype(F32)
        tags = jnp.concatenate([group, place, blank], axis=0)
        out_ref[d, halves * chan :, :] = tags.astype(BF16)
    for d in range(devices):
        if d * parts % devices == 0:
            got[d * parts // devices].wait()
        for h in range(halves):
            first = (d * halves + h) * LANES
            out_ref[d, h * chan : (h + 1) * chan, :] = feats[:, first : first + LANES]


def pack_plain(feats, ids, counts, groups, depth):
    chan, total = feats.shape
    devices = counts.shape[1]
    cap = total // devices
    ids = ids.reshape(devices, 1, cap)
    rank = jnp.arange(cap, dtype=jnp.int32)[None, None, :]
    group = jnp.where(rank < counts.reshape(devices, 1, 1), ids // depth, groups)
    tags = jnp.concatenate([group, ids % depth], axis=1).astype(BF16)
    rows = feats.reshape(chan, devices, cap).transpose(1, 0, 2)
    return jnp.concatenate([rows, jnp.pad(tags, ((0, 0), (0, 6), (0, 0)))], axis=1)


def scatter_kernel(
    halves, chan, size_y, sides_ref, recv_ref, act_ref, first_ref, second_ref, tags_ref,
    acc, masked, hot, tags_held, sems,
):
    chunks = recv_ref.shape[0]
    groups, depth = act_ref.shape
    per_step = masked.shape[1] // (halves * LANES)
    steps = chunks // per_step
    place = lax.broadcasted_iota(jnp.int32, (depth, LANES), 0).astype(F32)
    tags_held[...] = recv_ref[:, halves * chan :, :].astype(F32)
    kept = started(tags_held, tags_ref, sems.at[0])

    def step(s, carry):
        for j in range(per_step):
            block = recv_ref[s * per_step + j]
            tags = tags_held[s * per_step + j]
            for h in range(halves):
                feats = block[h * chan : (h + 1) * chan, :]
                col = (j * halves + h) * LANES
                group = jnp.broadcast_to(tags[h : h + 1, :], (chan, LANES)).astype(BF16)
                for k in range(groups):
                    masked[k * chan : (k + 1) * chan, col : col + LANES] = jnp.where(
                        group == k, feats, jnp.zeros_like(feats)
                    )
                low = tags[halves + h : halves + h + 1, :]
                hot[:, col : col + LANES] = jnp.where(place == low, 1.0, 0.0).astype(BF16)
        part = lax.dot_general(masked[...], hot[...], NT, preferred_element_type=F32)

        @pl.when(s == 0)
        def _():
            acc[...] = part

        @pl.when(s > 0)
        def _():
            acc[...] += part

        return carry

    lax.fori_loop(0, steps, step, 0)
    odd = sides_ref[0] != 0
    half = size_y // 2
    for k in range(groups // 2):
        p, q = k // size_y, k % size_y
        row = ((q // half) * 4 + p * 2 + q % half) * chan
        blocks = []
        for n in (k, k + groups // 2):
            block = acc[n * chan : (n + 1) * chan, :] * act_ref[n : n + 1, :]
            blocks.append(block.astype(BF16))
        first_ref[row : row + chan, :], second_ref[row : row + chan, :] = sided(odd, *blocks)
    kept.wait()


def coarse_kernel(sides_ref, act_ref, cot_ref, first_ref, second_ref, grad_ref, mask_ref):
    depth = act_ref.shape[1]
    chan = cot_ref.shape[2]
    odd = sides_ref[0] != 0
    fine = lax.broadcasted_iota(jnp.int32, (depth, LANES), 0) // 2
    pair = (fine == lax.broadcasted_iota(jnp.int32, (depth, LANES), 1)).astype(BF16)
    acts = act_ref[...]
    sums = jnp.dot(acts.astype(BF16), pair, preferred_element_type=F32)
    masks, grads = [], []
    for x in range(2):
        for y in range(2):
            rows = [sums[(2 * x + a) * 4 + 2 * y + b] for a in range(2) for b in range(2)]
            any_row = (rows[0] + rows[1] + rows[2] + rows[3])[None, :]
            mask = jnp.where(any_row > 0.5, 1.0, 0.0)
            masks.append(mask)
            grads.append((cot_ref[x, y].astype(F32) * mask).astype(BF16))
    for n, grad in enumerate(grads):
        grad_ref[n * chan : (n + 1) * chan, :] = grad
    for y in range(2):
        own = slice(y * chan, (y + 1) * chan)
        first_ref[own, :], second_ref[own, :] = sided(odd, grads[y], grads[2 + y])
    mask_ref[...] = jnp.concatenate(masks + [jnp.zeros((4, LANES), F32)], axis=0)
    blank = jnp.zeros((8, LANES), F32)
    tails = []
    for p in (0, 3):
        rows = acts[4 * p : 4 * p + 4]
        tails.append(jnp.concatenate([rows[:, :LANES], rows[:, LANES:], blank], axis=0))
    tails = sided(odd, *tails)
    for out_ref, tail in zip((first_ref, second_ref), tails):
        out_ref[2 * chan :, :] = tail.astype(BF16)


def coarse_rows_kernel(sides_ref, act_ref, grad_ref, xf_ref, xs_ref, first_ref, second_ref):
    chan = grad_ref.shape[0] // 4
    odd_x, odd_y = sides_ref[0] != 0, sides_ref[1] != 0
    before, after = sided(odd_x, xf_ref[...], xs_ref[...])
    acts = act_ref[...]
    before_acts = before[2 * chan :, :].astype(F32)
    after_acts = after[2 * chan :, :].astype(F32)
    ends = []
    for y, q in ((0, 0), (1, 3)):
        own = slice(y * chan, (y + 1) * chan)
        columns = [before[own], grad_ref[own, :]]
        columns += [grad_ref[(2 + y) * chan : (3 + y) * chan, :], after[own]]
        rows = [before_acts[q : q + 1], before_acts[4 + q : 5 + q]]
        for p in range(4):
            row = acts[4 * p + q : 4 * p + q + 1]
            rows += [row[:, :LANES], row[:, LANES:]]
        rows += [after_acts[q : q + 1], after_acts[4 + q : 5 + q], jnp.zeros((4, LANES), F32)]
        ends.append(columns + [jnp.concatenate(rows, axis=0).astype(BF16)])
    row = 0
    for low, high in zip(*ends):
        own = slice(row, row + low.shape[0])
        first_ref[own, :], second_ref[own, :] = sided(odd_y, low, high)
        row += low.shape[0]


def wide_kernel(
    sides_ref, act_ref, grad_ref, xf_ref, xs_ref, yf_ref, ys_ref, wide_ref, acts_ref
):
    chan = grad_ref.shape[0] // 4
    depth = act_ref.shape[1]
    acts = act_ref[...]
    x_ends = sided(sides_ref[0] != 0, xf_ref[...], xs_ref[...])
    y_ends = sided(sides_ref[1] != 0, yf_ref[...], ys_ref[...])
    xb, xa = [end[2 * chan :, :].astype(F32) for end in x_ends]
    yb, ya = [end[4 * chan :, :].astype(F32) for end in y_ends]
    rows = []
    for p in range(6):
        rows.append(jnp.concatenate([yb[2 * p : 2 * p + 1], yb[2 * p + 1 : 2 * p + 2]], axis=1))
        for q in range(4):
            if p in (0, 5):
                got = xb if p == 0 else xa
                rows.append(jnp.concatenate([got[q : q + 1], got[4 + q : 5 + q]], axis=1))
            else:
                rows.append(acts[4 * (p - 1) + q : 4 * (p - 1) + q + 1])
        rows.append(jnp.concatenate([ya[2 * p : 2 * p + 1], ya[2 * p + 1 : 2 * p + 2]], axis=1))
    rows.append(jnp.zeros((4, depth), F32))
    acts_ref[...] = jnp.concatenate(rows, axis=0)
    for x in range(4):
        for y in range(4):
            if y in (0, 3):
                block = y_ends[y // 3][x * chan : (x + 1) * chan, :]
            elif x in (0, 3):
                block = x_ends[x // 3][(y - 1) * chan : y * chan, :]
            else:
                first = ((x - 1) * 2 + y - 1) * chan
                block = grad_ref[first : first + chan, :]
            wide_ref[(x * 4 + y) * chan : (x * 4 + y + 1) * chan, :] = block


def bands_kernel(front_ref, back_ref, bands_ref, back_bands_ref):
    rows, width = front_ref.shape[0], front_ref.shape[1] // 9
    back_rows, back_width = back_ref.shape[0], back_ref.shape[1] // 9
    for t in range(9):
        block = front_ref[:, t * width : (t + 1) * width].astype(F32)
        for q in range(6):
            moved = pltpu.roll(block, q * back_rows, 1) if q else block
            bands_ref[q * rows : (q + 1) * rows, t * width : (t + 1) * width] = moved.astype(BF16)
        block = back_ref[:, t * back_width : (t + 1) * back_width].astype(F32)
        for q in range(4):
            moved = pltpu.roll(block, q * rows, 1) if q else block
            back_bands_ref[
                q * back_rows : (q + 1) * back_rows, t * back_width : (t + 1) * back_width
            ] = moved.astype(BF16)


def band_inputs(w_sub, in_chan):
    out_chan = w_sub.shape[0]
    taps = w_sub.reshape(out_chan, 3, 3, 3, in_chan)
    front = taps.transpose(0, 1, 3, 2, 4).reshape(out_chan, 9, 3 * in_chan)
    front = jnp.pad(front, ((0, 0), (0, 0), (0, 5 * in_chan)))
    back = taps[:, ::-1, ::-1].transpose(4, 1, 3, 2, 0).reshape(in_chan, 9, 3 * out_chan)
    back = jnp.pad(back, ((0, 0), (0, 0), (0, 3 * out_chan)))
    return front.reshape(out_chan, -1), back.reshape(in_chan, -1)


def rows_kernel(sides_ref, first_ref, second_ref, gf_ref, gs_ref, out_first_ref, out_second_ref):
    odd_x, odd_y = sides_ref[0] != 0, sides_ref[1] != 0
    half = first_ref.shape[0] // 2
    low, high = sided(odd_x, first_ref[...], second_ref[...])
    below, above = sided(odd_x, gf_ref[...], gs_ref[...])
    for n, block in enumerate((below, low, high, above)):
        own = slice(n * half, (n + 1) * half)
        out_first_ref[own, :], out_second_ref[own, :] = sided(odd_y, block[:half], block[half:])


def columns_kernel(
    chan, sides_ref, first_ref, second_ref, gf_ref, gs_ref, yf_ref, ys_ref, front_ref, rear_ref, swap_ref
):
    odd_x, odd_y, place = sides_ref[0] != 0, sides_ref[1] != 0, sides_ref[2]
    low, high = sided(odd_x, first_ref[...], second_ref[...])
    below, above = sided(odd_x, gf_ref[...], gs_ref[...])
    left, right = sided(odd_y, yf_ref[...], ys_ref[...])
    for n, own in enumerate((below, low, high, above)):
        for p in range(2):
            for y in range(8):
                if y in (0, 1, 6, 7):
                    got = left if y < 2 else right
                    row = (n * 4 + p * 2 + y % 2) * chan
                else:
                    got = own
                    row = (((y - 2) // 2) * 4 + p * 2 + y % 2) * chan
                block = got[row : row + chan]
                to = ((n * 2 + p) * 8 + y) * chan
                front_ref[to : to + chan, :] = block[:, :LANES]
                rear_ref[to : to + chan, :] = block[:, LANES:]
                swap_ref[to : to + chan, :] = jnp.where(
                    place == 0, block[:, LANES:], block[:, :LANES]
                )


def shifted(low, high, before, after, step):
    lane = lax.broadcasted_iota(jnp.int32, low.shape, 1)
    if step > 0:
        turned = [pltpu.roll(tile.astype(F32), LANES - 1, 1) for tile in (low, high, after)]
        edge = lane == LANES - 1
        tiles = [jnp.where(edge, turned[1], turned[0]), jnp.where(edge, turned[2], turned[1])]
    else:
        turned = [pltpu.roll(tile.astype(F32), 1, 1) for tile in (before, low, high)]
        edge = lane == 0
        tiles = [jnp.where(edge, turned[0], turned[1]), jnp.where(edge, turned[1], turned[2])]
    return tiles[0].astype(BF16), tiles[1].astype(BF16)


def keep(tile, wanted):
    return jnp.where(wanted, tile, jnp.zeros_like(tile))


def to_rows(columns):
    lane = lax.broadcasted_iota(jnp.int32, (LANES, LANES), 1)
    wide = jnp.zeros((LANES, LANES), F32)
    for n, column in enumerate(columns):
        tall = jnp.concatenate([column, jnp.zeros((LANES - column.shape[0], 1), F32)], axis=0)
        wide = jnp.where(lane == n, tall, wide)
    return wide.T[:8, :]


def to_columns(rows, chan):
    wide = jnp.concatenate(rows + [jnp.zeros((LANES - len(rows), LANES), F32)], axis=0).T
    return [wide[:chan, n : n + 1] for n in range(len(rows))]


def conv_kernel(
    only_two, sides_ref, low_ref, high_ref, before_ref, after_ref, bands_ref, acts_ref,
    hidden_ref, stack_ref, stats_ref, hidden, stack, sems,
):
    rows = low_ref.shape[0] // 8
    depth = acts_ref.shape[1]
    wide = bands_ref.shape[0]
    chan = wide // 6
    place = sides_ref[2]
    kept = []
    for x in range(8):
        own = slice(x * rows, (x + 1) * rows)
        low, high = low_ref[own, :], high_ref[own, :]
        before, after = before_ref[own, :], after_ref[own, :]
        if only_two:
            before, after = keep(before, place != 0), keep(after, place == 0)
        for n, step in enumerate((-1, 0, 1)):
            tiles = (low, high) if step == 0 else shifted(low, high, before, after, step)
            to = slice((x * 3 + n) * rows, (x * 3 + n + 1) * rows)
            stack[to, :LANES] = tiles[0]
            stack[to, LANES:] = tiles[1]
        if 1 <= x <= 6:
            kept.append(
                started(
                    stack.at[rows_of(x, 3 * rows), :],
                    stack_ref.at[rows_of(x - 1, 3 * rows), :],
                    sems.at[x - 1],
                )
            )
    total = jnp.zeros((chan, depth), F32)
    for p in range(6):
        first = p * 3 * rows
        out = jnp.dot(
            bands_ref[...], stack[first : first + 9 * rows, :], preferred_element_type=F32
        )
        for q in range(6):
            block = out[q * chan : (q + 1) * chan] * acts_ref[p * 6 + q : p * 6 + q + 1, :]
            hidden[p * wide + q * chan : p * wide + (q + 1) * chan, :] = block
            if 1 <= p <= 4 and 1 <= q <= 4:
                total = total + block
        own = rows_of(p, wide)
        kept.append(started(hidden.at[own, :], hidden_ref.at[own, :], sems.at[6 + p]))
    count = jnp.zeros((1, depth), F32)
    for p in range(1, 5):
        for q in range(1, 5):
            count = count + acts_ref[p * 6 + q : p * 6 + q + 1, :]
    count = jnp.sum(count, axis=1, keepdims=True)
    total = jnp.sum(total, axis=1, keepdims=True)
    mean = total / jnp.maximum(count, 1.0)
    squares = jnp.zeros((chan, depth), F32)
    for p in range(1, 5):
        for q in range(1, 5):
            row = p * wide + q * chan
            centred = (hidden[row : row + chan, :] - mean) * acts_ref[p * 6 + q : p * 6 + q + 1, :]
            squares = squares + centred * centred
    squares = jnp.sum(squares, axis=1, keepdims=True)
    packed = to_rows([total, squares, jnp.broadcast_to(count, (chan, 1))])
    for d in range(stats_ref.shape[0]):
        stats_ref[d] = packed
    for copy in kept:
        copy.wait()


def merged_stats(stats_ref):
    totals, squares, counts = stats_ref[:, 0, :], stats_ref[:, 1, :], stats_ref[:, 2, :]
    count = jnp.sum(counts, axis=0, keepdims=True)
    average = jnp.sum(totals, axis=0, keepdims=True) / count
    off = totals / jnp.maximum(counts, 1.0) - average
    spread = jnp.sum(squares + counts * off * off, axis=0, keepdims=True)
    return count, average, lax.rsqrt(spread / count + EPS)


def norm_kernel(
    stats_ref, params_ref, hidden_ref, wide_ref, acts_ref, down_ref, pre_ref, out_ref, sums_ref,
    hidden, wide, acts, up, fine, pre, outs, sems,
):
    chan = hidden.shape[0] // 36
    depth = acts.shape[1]
    got_acts = started(acts_ref, acts, sems.at[0])
    got_wide = started(wide_ref, wide, sems.at[1])
    got = []
    for p in range(6):
        own = rows_of(p, 6 * chan)
        got.append(started(hidden_ref.at[own, :], hidden.at[own, :], sems.at[2 + p]))
    coarse_z = lax.broadcasted_iota(jnp.int32, (LANES, 2 * depth), 0)
    fine_z = lax.broadcasted_iota(jnp.int32, (LANES, 2 * depth), 1)
    child = jnp.where(fine_z < depth, 0, 1)
    spread = (2 * coarse_z + child == fine_z - child * depth).astype(BF16)
    got_wide.wait()
    up[...] = jnp.dot(wide[...], spread, preferred_element_type=F32).astype(BF16)
    for x in range(4):
        for y in range(4):
            own = slice((x * 4 + y) * chan, (x * 4 + y + 1) * chan)
            both = jnp.concatenate([up[own, :depth], up[own, depth:]], axis=0)
            for a in range(2):
                p = 2 * x + a - 1
                if not 0 <= p < 6:
                    continue
                cols = [b for b in range(2) if 0 <= 2 * y + b - 1 < 6]
                first = (a * 2 + cols[0]) * chan
                grads = jnp.dot(
                    down_ref[first : first + len(cols) * chan, :], both, preferred_element_type=F32
                )
                row = (p * 6 + 2 * y + cols[0] - 1) * chan
                fine[row : row + len(cols) * chan, :] = grads
    count, average, inverse = merged_stats(stats_ref)
    full = (chan, LANES)
    average, inverse, gain, shift = [
        jnp.broadcast_to(column, full)
        for column in to_columns([average, inverse, params_ref[0:1, :], params_ref[1:2, :]], chan)
    ]
    sum_shift = jnp.zeros((chan, LANES), F32)
    sum_gain = jnp.zeros((chan, LANES), F32)
    kept = []
    got_acts.wait()
    for p in range(6):
        got[p].wait()
        for q in range(6):
            row = (p * 6 + q) * chan
            for half in range(depth // LANES):
                lanes = slice(half * LANES, (half + 1) * LANES)
                act = acts[p * 6 + q : p * 6 + q + 1, lanes]
                normed = (hidden[row : row + chan, lanes] - average) * inverse
                x = gain * normed + shift
                square = x * x
                bent = jnp.tanh(GELU_SCALE * (x + GELU_CUBE * (square * x)))
                cdf = 0.5 + 0.5 * bent
                slope = cdf + (0.5 * x) * (1.0 - bent * bent) * (
                    GELU_SCALE + (3.0 * GELU_CUBE * GELU_SCALE) * square
                )
                grad = (act * slope) * fine[row : row + chan, lanes]
                pre[row : row + chan, lanes] = grad
                if 1 <= p <= 4 and 1 <= q <= 4:
                    sum_shift = sum_shift + grad
                    sum_gain = sum_gain + grad * normed
                    to = ((p - 1) * 4 + q - 1) * chan
                    outs[to : to + chan, lanes] = (x * cdf * act).astype(BF16)
        own = rows_of(p, 6 * chan)
        kept.append(started(pre.at[own, :], pre_ref.at[own, :], sems.at[8 + p]))
    kept.append(started(outs, out_ref, sems.at[14]))
    sums = to_rows(
        [jnp.sum(sum_shift, axis=1, keepdims=True), jnp.sum(sum_gain, axis=1, keepdims=True)]
    )
    for d in range(sums_ref.shape[0]):
        sums_ref[d] = sums
    for copy in kept:
        copy.wait()


def down_kernel(out_ref, grad_ref, mask_ref, down_ref, coarse_ref, raw_ref, stack):
    depth = out_ref.shape[1]
    chan = grad_ref.shape[0] // 4
    source = lax.broadcasted_iota(jnp.int32, (depth, depth), 0)
    target = lax.broadcasted_iota(jnp.int32, (depth, depth), 1)
    wanted = jnp.where(target < LANES, 2 * target, 2 * (target - LANES) + 1)
    sort = (source == wanted).astype(BF16)
    for x in range(2):
        for y in range(2):
            for a in range(2):
                for b in range(2):
                    row = ((2 * x + a) * 4 + 2 * y + b) * chan
                    parted = jnp.dot(
                        out_ref[row : row + chan, :], sort, preferred_element_type=F32
                    ).astype(BF16)
                    lanes = slice((x * 2 + y) * LANES, (x * 2 + y + 1) * LANES)
                    to = (a * 4 + b * 2) * chan
                    stack[to : to + chan, lanes] = parted[:, :LANES]
                    stack[to + chan : to + 2 * chan, lanes] = parted[:, LANES:]
    sums = jnp.dot(down_ref[...], stack[...], preferred_element_type=F32)
    for n in range(4):
        coarse_ref[n] = (sums[:, n * LANES : (n + 1) * LANES] * mask_ref[n : n + 1, :]).astype(
            BF16
        )
    grads = jnp.concatenate([grad_ref[n * chan : (n + 1) * chan, :] for n in range(4)], axis=1)
    raw = lax.dot_general(grads, stack[...], NT, preferred_element_type=F32)
    for n in range(4):
        raw_ref[n * chan : (n + 1) * chan, :] = raw[:, n * LANES : (n + 1) * LANES]


def hidden_grad_kernel(
    in_chan, sides_ref, stats_ref, sums_ref, params_ref, hidden_ref, pre_ref, acts_ref, stack_ref,
    raw_ref, front_ref, rear_ref, swap_ref, small_ref, out_ref,
    stats, hidden, pre, acts, stack, raw, front, rear, acc, sems,
):
    chan = hidden.shape[0] // 36
    place = sides_ref[2]
    got_stats = started(stats_ref, stats, sems.at[0])
    got_acts = started(acts_ref, acts, sems.at[1])
    got = []
    for p in range(6):
        own = rows_of(p, 6 * chan)
        got.append(
            (
                started(hidden_ref.at[own, :], hidden.at[own, :], sems.at[4 + p]),
                started(pre_ref.at[own, :], pre.at[own, :], sems.at[10 + p]),
            )
        )
    got_stack = started(stack_ref, stack, sems.at[2])
    got_raw = started(raw_ref, raw, sems.at[3])
    raw_shift = jnp.sum(sums_ref[:, 0, :], axis=0, keepdims=True)
    raw_gain = jnp.sum(sums_ref[:, 1, :], axis=0, keepdims=True)
    got_stats.wait()
    count, average, inverse = merged_stats(stats)
    scale = lax.rsqrt(count)
    small_ref[...] = jnp.concatenate(
        [raw_shift * scale, raw_gain * scale, scale, jnp.zeros((5, LANES), F32)], axis=0
    )
    columns = [average, inverse, raw_shift / count, raw_gain / count, params_ref[0:1, :]]
    average, inverse, mean_shift, mean_gain, gain = [
        jnp.broadcast_to(column, (chan, LANES)) for column in to_columns(columns, chan)
    ]
    weight = gain * inverse
    got_acts.wait()
    kept = []
    for p in range(6):
        for copy in got[p]:
            copy.wait()
        for n in range(6 * p, 6 * p + 6):
            row = n * chan
            tiles = []
            for half, held in enumerate((front, rear)):
                lanes = slice(half * LANES, (half + 1) * LANES)
                act = acts[n : n + 1, lanes]
                normed = (hidden[row : row + chan, lanes] - average) * inverse
                grad = pre[row : row + chan, lanes] - (mean_shift + normed * mean_gain)
                tiles.append(((act * weight) * grad).astype(BF16))
                held[row : row + chan, :] = tiles[-1]
            swap_ref[row : row + chan, :] = jnp.where(place == 0, tiles[1], tiles[0])
        own = rows_of(p, 6 * chan)
        kept.append(started(front.at[own, :], front_ref.at[own, :], sems.at[16 + p]))
        kept.append(started(rear.at[own, :], rear_ref.at[own, :], sems.at[22 + p]))
    got_stack.wait()
    got_raw.wait()
    rows = stack.shape[0] // 6
    band = rows // 3
    for p in range(4):
        own = slice(((p + 1) * 6 + 1) * chan, ((p + 1) * 6 + 5) * chan)
        grads = jnp.concatenate([front[own, :], rear[own, :]], axis=1)
        for dx in range(3):
            first = (p + dx) * rows
            part = lax.dot_general(
                stack[first : first + rows, :], grads, NT, preferred_element_type=F32
            )
            if p == 0:
                acc[dx] = part
            else:
                acc[dx] += part
    low = lax.broadcasted_iota(jnp.int32, (in_chan, LANES), 1) < chan
    for dx in range(3):
        for dy in range(3):
            for dz in range(3):
                blocks = []
                for q in range(4):
                    row = dz * band + (q + 1 + dy) * in_chan
                    lanes = slice((q // 2) * LANES, (q // 2 + 1) * LANES)
                    blocks.append(acc[dx, row : row + in_chan, lanes])
                both = jnp.where(low, blocks[0] + blocks[2], blocks[1] + blocks[3])
                folded = (both + pltpu.roll(both, chan, 1)).astype(out_ref.dtype)
                tap = (dx * 3 + dy) * 3 + dz
                if tap < 16:
                    out_ref[tap * in_chan : (tap + 1) * in_chan, :chan] = folded[:, :chan]
                else:
                    to = (tap - 16) * in_chan
                    out_ref[to : to + in_chan, chan:] = folded[:, chan:]
    out_ref[11 * in_chan : 16 * in_chan, chan:] = jnp.zeros(
        (5 * in_chan, LANES - chan), out_ref.dtype
    )
    tail = 16 * in_chan
    out_ref[tail : tail + 4 * chan, :] = raw[...].astype(out_ref.dtype)
    left = out_ref.shape[0] - tail - 4 * chan
    if left:
        out_ref[tail + 4 * chan :, :] = jnp.zeros((left, LANES), out_ref.dtype)
    for copy in kept:
        copy.wait()


def point_grad_kernel(
    only_two, halves, chan, sides_ref, front_ref, rear_ref, before_ref, after_ref, bands_ref, act_ref,
    tags_ref, out_ref, front, rear, bands, acts, tags_held, stack, cells, sems,
):
    rows = front.shape[0] // 6
    groups, depth = acts.shape
    place_z = sides_ref[2]
    got = []
    for x in range(6):
        own = rows_of(x, rows)
        got.append(
            (
                started(front_ref.at[own, :], front.at[own, :], sems.at[3 + x]),
                started(rear_ref.at[own, :], rear.at[own, :], sems.at[9 + x]),
            )
        )
    late = [
        started(bands_ref, bands, sems.at[0]),
        started(act_ref, acts, sems.at[1]),
        started(tags_ref, tags_held, sems.at[2]),
    ]
    for x in range(6):
        for copy in got[x]:
            copy.wait()
        own = slice(x * rows, (x + 1) * rows)
        low, high = front[own, :], rear[own, :]
        before, after = before_ref[own, :], after_ref[own, :]
        if only_two:
            before, after = keep(before, place_z != 0), keep(after, place_z == 0)
        for n, step in enumerate((1, 0, -1)):
            tiles = (low, high) if step == 0 else shifted(low, high, before, after, step)
            to = slice((x * 3 + n) * rows, (x * 3 + n + 1) * rows)
            stack[to, :LANES] = tiles[0]
            stack[to, LANES:] = tiles[1]
    for copy in late:
        copy.wait()
    for p in range(4):
        first = p * 3 * rows
        grid = jnp.dot(
            bands[...], stack[first : first + 9 * rows, :], preferred_element_type=F32
        )
        for q in range(4):
            k = p * 4 + q
            cells[k * chan : (k + 1) * chan, :] = (
                grid[q * chan : (q + 1) * chan] * acts[k : k + 1, :]
            ).astype(BF16)
    place = lax.broadcasted_iota(jnp.int32, (depth, LANES), 0).astype(F32)

    def from_cells(d):
        tags = tags_held[d]
        lows = [tags[halves + h : halves + h + 1, :] for h in range(halves)]
        hot = [jnp.where(place == low, 1.0, 0.0).astype(BF16) for low in lows]
        hot = jnp.concatenate(hot, axis=1)
        found = jnp.dot(cells[...], hot, preferred_element_type=F32)
        for h in range(halves):
            group = jnp.broadcast_to(tags[h : h + 1, :], (chan, LANES))
            lanes = slice(h * LANES, (h + 1) * LANES)
            out = jnp.zeros((chan, LANES), F32)
            for k in range(groups):
                out = jnp.where(group == k, found[k * chan : (k + 1) * chan, lanes], out)
            out_ref[d, h * chan : (h + 1) * chan, :] = out.astype(BF16)

    def step(s, carry):
        for j in range(4):
            from_cells(4 * s + j)
        return carry

    lax.fori_loop(0, tags_held.shape[0] // 4, step, 0)


def piece_kernel(parts_ref, out_ref):
    out_ref[...] = jnp.sum(parts_ref[...].astype(F32), axis=0).astype(BF16)


def gathered(piece, names, sizes):
    for name, size in zip(names, sizes):
        pairs = [[(i, i ^ k) for i in range(size)] for k in range(1, size)]
        parts = [piece] + [lax.ppermute(piece, name, pair) for pair in pairs]
        piece = jnp.concatenate(parts, axis=0)
    return piece


def weights_out(rows, small_ref, in_chan, sub_ref, down_ref):
    chan = down_ref.shape[0]
    scale = small_ref[2:3, 0:1]
    for n in range(4):
        turned = rows(n).T * scale
        sub_ref[:, n * LANES : (n + 1) * LANES] = turned[:chan]
        left = sub_ref.shape[1] - 16 * in_chan - n * LANES
        if left > 0:
            width = min(left, LANES)
            first = 16 * in_chan + n * LANES
            sub_ref[:, first : first + width] = turned[chan:, :width]
    for n in range(2):
        both = rows(4 + n) * scale
        down_ref[:, 2 * n * LANES : (2 * n + 1) * LANES] = both[:chan]
        down_ref[:, (2 * n + 1) * LANES : (2 * n + 2) * LANES] = both[chan:]


def points_kernel(halves, chan, got_ref, points_ref):
    for d in range(got_ref.shape[0]):
        block = got_ref[d]
        for h in range(halves):
            first = (d * halves + h) * LANES
            points_ref[:, first : first + LANES] = block[h * chan : (h + 1) * chan, :]


def weights_kernel(chan, sizes, at_ref, got_ref, small_ref, sub_ref, down_ref, flat):
    nz, nx, ny = sizes
    piece = got_ref.shape[0] // (nx * ny * nz)
    for y in range(ny):
        for x in range(nx):
            for z in range(nz):
                n = (y * nx + x) * nz + z
                device = ((at_ref[1] ^ x) * ny + (at_ref[2] ^ y)) * nz + (at_ref[0] ^ z)
                own = pl.ds(pl.multiple_of(device * piece, 8), piece)
                flat[own, :] = got_ref[n * piece : (n + 1) * piece, :].astype(F32)
    weights_out(lambda n: flat[n * LANES : (n + 1) * LANES, :], small_ref, chan, sub_ref, down_ref)


def on_device(
    point_feats, voxel_ids, send_counts, active, w_sub, w_down, bn_gain, bn_shift, cotangent
):
    in_chan, slot_total = point_feats.shape
    devices = send_counts.shape[1]
    slot_cap = slot_total // devices
    size_x, size_y, size_z = active.shape
    groups = size_x * size_y
    out_chan = w_sub.shape[0]
    only_two = lax.axis_size("gz") == 2
    sides = jnp.stack(
        [lax.axis_index("gx") % 2, lax.axis_index("gy") % 2, lax.axis_index("gz")]
    ).astype(jnp.int32)
    aligned = slot_cap % LANES == 0
    halves = slot_cap // LANES if aligned else 1
    rows_x, rows_6, rows_64 = groups // 2 * in_chan, 36 * out_chan, 64 * in_chan
    wide, back_wide = 6 * out_chan, 4 * in_chan

    if aligned:
        payload = local_call(
            functools.partial(pack_kernel, halves, groups, size_z),
            [((devices, halves * in_chan + 8, LANES), BF16)],
            send_counts, point_feats, voxel_ids.reshape(-1, LANES),
            scratch=[((in_chan, slot_total), BF16), ((devices * halves, LANES), jnp.int32)],
            smem=(0,), hbm=(1, 2), copies=5, moved=2e6,
        )[0]
        recv = everyone(payload)
    else:
        payload = pack_plain(point_feats, voxel_ids, send_counts, groups, size_z)
        together = LANES // slot_cap
        recv = everyone(payload)
        recv = recv.reshape(devices // together, together, in_chan + 8, slot_cap)
        recv = recv.transpose(0, 2, 1, 3).reshape(devices // together, in_chan + 8, LANES)
    chunks = recv.shape[0]

    acts = active.reshape(groups, size_z).astype(F32)
    params = jnp.pad(jnp.stack([bn_gain, bn_shift]), ((0, 6), (0, LANES - out_chan)))
    front, back = band_inputs(w_sub, in_chan)
    cot = cotangent.transpose(1, 2, 0, 3)
    *ends, grad_c, coarse_mask = local_call(
        coarse_kernel,
        [((2 * out_chan + 16, LANES), BF16)] * 2
        + [((4 * out_chan, LANES), BF16), ((8, LANES), F32)],
        sides, acts, cot, smem=(0,), moved=2e5,
    )
    cot_x = swaps(*ends, "gx")
    ends = local_call(
        coarse_rows_kernel,
        [((4 * out_chan + 16, LANES), BF16)] * 2,
        sides, acts, grad_c, *cot_x, smem=(0,), moved=2e5,
    )
    cot_y = swaps(*ends, "gy")
    by_child = (
        w_down.reshape(out_chan, 4, 2, out_chan)
        .transpose(1, 3, 2, 0)
        .reshape(4 * out_chan, 2 * out_chan)
    )
    recv, acts, grad_c, cot_x, cot_y, by_child, front, back, params = lax.optimization_barrier(
        (recv, acts, grad_c, cot_x, cot_y, by_child, front, back, params)
    )

    per_step = min(chunks, 16 // halves)
    *mine, tags = local_call(
        functools.partial(scatter_kernel, halves, in_chan, size_y),
        [((rows_x, size_z), BF16)] * 2 + [((chunks, 8, LANES), F32)],
        sides, recv, acts,
        scratch=[
            ((groups * in_chan, size_z), F32),
            ((groups * in_chan, per_step * halves * LANES), BF16),
            ((size_z, per_step * halves * LANES), BF16),
            ((chunks, 8, LANES), F32),
        ],
        smem=(0,), hbm_outs=(2,), copies=1, moved=2e7,
    )
    got_x = swaps(*mine, "gx")
    grad_wide, acts_wide = local_call(
        wide_kernel,
        [((16 * out_chan, LANES), BF16), ((40, size_z), F32)],
        sides, acts, grad_c, *cot_x, *cot_y,
        smem=(0,), hbm_outs=(), moved=5e5,
    )
    got_x, grad_wide, acts_wide = lax.optimization_barrier((got_x, grad_wide, acts_wide))
    ends = local_call(
        rows_kernel,
        [((2 * rows_x, size_z), BF16)] * 2,
        sides, *mine, *got_x, smem=(0,), moved=1e6,
    )
    got_y = swaps(*ends, "gy")
    bands_shape, back_shape = (wide, 9 * 8 * in_chan), (back_wide, 9 * 6 * out_chan)
    bands, back_bands = local_call(
        bands_kernel,
        [(bands_shape, BF16), (back_shape, BF16)],
        front, back, hbm_outs=(), moved=4e6,
    )
    got_y, bands, back_bands = lax.optimization_barrier((got_y, bands, back_bands))
    tile_low, tile_high, swap = local_call(
        functools.partial(columns_kernel, in_chan),
        [((rows_64, LANES), BF16)] * 3,
        sides, *mine, *got_x, *got_y, smem=(0,), moved=3e6,
    )
    before, after = z_exchange(tile_low, tile_high, swap)

    stats_shape = (devices, 8, LANES)
    stack_shape = (rows_64 // 8 * 6 * 3, size_z)
    hidden, stack, stats = local_call(
        functools.partial(conv_kernel, only_two),
        [((rows_6, size_z), F32), (stack_shape, BF16), (stats_shape, F32)],
        sides, tile_low, tile_high, before, after, bands, acts_wide,
        scratch=[((rows_6, size_z), F32), ((3 * rows_64, size_z), BF16)],
        smem=(0,), hbm_outs=(0, 1), copies=12, moved=2e7,
    )
    stats = everyone(stats)
    grad_pre, fine_out, sums = local_call(
        norm_kernel,
        [((rows_6, size_z), F32), ((groups * out_chan, size_z), BF16), (stats_shape, F32)],
        stats, params, hidden, grad_wide, acts_wide, by_child,
        scratch=[
            ((rows_6, size_z), F32),
            ((16 * out_chan, LANES), BF16),
            ((40, size_z), F32),
            ((16 * out_chan, 2 * size_z), BF16),
            ((rows_6, size_z), F32),
            ((rows_6, size_z), F32),
            ((groups * out_chan, size_z), BF16),
        ],
        hbm=(2, 3, 4), hbm_outs=(0, 1), copies=15, moved=1e7,
    )
    sums = everyone(sums)
    coarse, raw_down = local_call(
        down_kernel,
        [((4, out_chan, LANES), BF16), ((4 * out_chan, LANES), F32)],
        fine_out, grad_c, coarse_mask, w_down,
        scratch=[((8 * out_chan, 4 * LANES), BF16)], moved=5e6,
    )
    half_x, half_y, half_z = size_x // 2, size_y // 2, size_z // 2
    coarse_out = coarse.reshape(half_x, half_y, out_chan, half_z).transpose(2, 0, 1, 3)

    piece = -(-(16 * in_chan + 4 * out_chan) // devices)
    piece = -(-piece // 8) * 8
    grad_low, grad_high, grad_swap, small, parts = local_call(
        functools.partial(hidden_grad_kernel, in_chan),
        [((rows_6, LANES), BF16)] * 3 + [((8, LANES), F32), ((devices * piece, LANES), BF16)],
        sides, stats, sums, params, hidden, grad_pre, acts_wide, stack, raw_down,
        scratch=[
            (stats_shape, F32),
            ((rows_6, size_z), F32),
            ((rows_6, size_z), F32),
            ((40, size_z), F32),
            (stack_shape, BF16),
            ((4 * out_chan, LANES), F32),
            ((rows_6, LANES), BF16),
            ((rows_6, LANES), BF16),
            ((3, 24 * in_chan, 4 * out_chan), F32),
        ],
        smem=(0,), hbm=(1, 4, 5, 6, 7, 8), hbm_outs=(0, 1), copies=28, moved=2e7,
    )
    grad_before, grad_after = z_exchange(grad_low, grad_high, grad_swap)
    parts = everyone(parts.reshape(devices, piece, LANES))

    points = local_call(
        functools.partial(point_grad_kernel, only_two, halves, in_chan),
        [((chunks, halves * in_chan, LANES), BF16)],
        sides, grad_low, grad_high, grad_before, grad_after, back_bands, acts, tags,
        scratch=[
            ((rows_6, LANES), BF16),
            ((rows_6, LANES), BF16),
            (back_shape, BF16),
            ((groups, size_z), F32),
            ((chunks, 8, LANES), F32),
            ((3 * rows_6, size_z), BF16),
            ((groups * in_chan, size_z), BF16),
        ],
        smem=(0,), hbm=(1, 2, 5, 6, 7), copies=15, moved=2e7,
    )[0]
    parts, points = lax.optimization_barrier((parts, points))
    if aligned:
        returned = local_call(
            functools.partial(points_kernel, halves, in_chan),
            [((in_chan, slot_total), BF16)],
            everyone(points), moved=1e6,
        )[0]
    else:
        points = points.reshape(chunks, in_chan, together, slot_cap).transpose(0, 2, 1, 3)
        returned = everyone(points.reshape(devices, in_chan, slot_cap))
        returned = returned.transpose(1, 0, 2).reshape(in_chan, slot_total)

    names = ("gz", "gx", "gy")
    sizes = tuple(lax.axis_size(name) for name in names)
    at = jnp.stack([lax.axis_index(name) for name in names]).astype(jnp.int32)
    summed = local_call(piece_kernel, [((piece, LANES), BF16)], parts, moved=2e5)[0]
    raw_sub, raw_down = local_call(
        functools.partial(weights_kernel, in_chan, sizes),
        [((out_chan, 27 * in_chan), F32), ((out_chan, 8 * out_chan), F32)],
        at, gathered(summed, names, sizes), small,
        scratch=[((devices * piece, LANES), F32)], smem=(0,), moved=5e5,
    )
    return (
        coarse_out,
        returned,
        raw_sub,
        raw_down,
        small[1, :out_chan],
        small[0, :out_chan],
    )


def solution(mesh):
    in_specs = (
        P(None, AXES),
        P(AXES),
        P(AXES, None),
        P("gx", "gy", "gz"),
        P(),
        P(),
        P(),
        P(),
        P(None, "gx", "gy", "gz"),
    )
    out_specs = (P(None, "gx", "gy", "gz"), P(None, AXES), P(), P(), P(), P())
    return jax.shard_map(
        on_device, mesh=mesh, in_specs=in_specs, out_specs=out_specs, check_vma=False
    )
```

```python
import functools
import math

import jax
import jax.numpy as jnp
from jax import lax
from jax.experimental import pallas as pl
from jax.experimental.pallas import tpu as pltpu
from jax.sharding import PartitionSpec as P

EPS = 1e-05
AXES = ("gx", "gy", "gz")
LANES = 128
GELU_SCALE = 0.7978845608028654
GELU_CUBE = 0.044715
F32 = jnp.float32
BF16 = jnp.bfloat16
NT = (((1,), (1,)), ((), ()))


def local_call(
    kernel, outs, *args, scratch=(), scalars=(), smem=(), hbm=(), hbm_outs=(), copies=0, moved=0
):
    held = sum(math.prod(shape) * jnp.dtype(kind).itemsize for shape, kind in scratch)
    limit = held // 2**20 + 6
    vmem = pl.BlockSpec(memory_space=pltpu.VMEM)
    scalar = pl.BlockSpec(memory_space=pltpu.SMEM)
    far = pl.BlockSpec(memory_space=pltpu.HBM)
    args = [
        pltpu.with_memory_space_constraint(arg, pltpu.HBM) if i in hbm else arg
        for i, arg in enumerate(args)
    ]
    held = [pltpu.VMEM(shape, kind) for shape, kind in scratch]
    held += [pltpu.SMEM(shape, kind) for shape, kind in scalars]
    if copies:
        held.append(pltpu.SemaphoreType.DMA((copies,)))
    return pl.pallas_call(
        kernel,
        out_shape=[
            pltpu.HBM(shape, kind) if i in hbm_outs else jax.ShapeDtypeStruct(shape, kind)
            for i, (shape, kind) in enumerate(outs)
        ],
        in_specs=[
            scalar if i in smem else far if i in hbm else vmem for i in range(len(args))
        ],
        out_specs=[far if i in hbm_outs else vmem for i in range(len(outs))],
        scratch_shapes=held,
        compiler_params=pltpu.CompilerParams(vmem_limit_bytes=limit * 1024 * 1024),
        cost_estimate=pl.CostEstimate(flops=0, bytes_accessed=int(moved), transcendentals=0),
    )(*args)


def started(source, target, semaphore):
    copy = pltpu.make_async_copy(source, target, semaphore)
    copy.start()
    return copy


def rows_of(n, count):
    return pl.ds(n * count, count)


def started_rows(source, target, cuts, semaphores):
    copies = []
    for n, (begin, end) in enumerate(zip(cuts, cuts[1:])):
        own = pl.ds(begin, end - begin)
        copies.append(started(source.at[own, :], target.at[own, :], semaphores.at[n]))
    return copies


OWN = [(p, q) for p in range(1, 5) for q in range(1, 5)]
RING = [(p, q) for p in range(6) for q in range(6) if (p, q) not in OWN]


def neighbours(axis, step):
    count = lax.axis_size(axis)
    return [(i, i + step) for i in range(count) if 0 <= i + step < count]


def swaps(first, second, axis):
    count = lax.axis_size(axis)
    got = []
    for block, begin in ((first, 0), (second, 1)):
        pairs = [(i, i + 1) for i in range(begin, count - 1, 2)]
        got.append(lax.ppermute(block, axis, pairs + [(j, i) for i, j in pairs]))
    return got


def sided(odd, first, second):
    return jnp.where(odd, first, second), jnp.where(odd, second, first)


def z_exchange(low, high, swap):
    if lax.axis_size("gz") != 2:
        return (
            lax.ppermute(high, "gz", neighbours("gz", 1)),
            lax.ppermute(low, "gz", neighbours("gz", -1)),
        )
    got = lax.ppermute(swap, "gz", [(0, 1), (1, 0)])
    return got, got


def everyone(block):
    return lax.all_to_all(block, AXES, split_axis=0, concat_axis=0, tiled=True)


def pack_kernel(
    halves, groups, depth, counts_ref, feats_ref, ids_ref, out_ref, feats, ids, counts, sems
):
    devices = out_ref.shape[0]
    chan = feats_ref.shape[0]
    parts = 4
    width = feats.shape[1] // parts
    got_ids = started(ids_ref, ids, sems.at[parts])
    got_counts = started(counts_ref, counts, sems.at[parts + 1])
    got = []
    for n in range(parts):
        lanes = pl.ds(n * width, width)
        got.append(started(feats_ref.at[:, lanes], feats.at[:, lanes], sems.at[n]))
    got_ids.wait()
    got_counts.wait()
    rank = lax.broadcasted_iota(jnp.int32, (halves, LANES), 0) * LANES + lax.broadcasted_iota(
        jnp.int32, (halves, LANES), 1
    )
    blank = jnp.zeros((8 - 2 * halves, LANES), F32)
    for d in range(devices):
        those = ids[d * halves : (d + 1) * halves, :]
        usable = rank < counts[0, d]
        group = jnp.where(usable, those // depth, groups).astype(F32)
        place = (those % depth).astype(F32)
        tags = jnp.concatenate([group, place, blank], axis=0)
        out_ref[d, halves * chan :, :] = tags.astype(BF16)
    for d in range(devices):
        if d * parts % devices == 0:
            got[d * parts // devices].wait()
        for h in range(halves):
            first = (d * halves + h) * LANES
            out_ref[d, h * chan : (h + 1) * chan, :] = feats[:, first : first + LANES]


def pack_plain(feats, ids, counts, groups, depth):
    chan, total = feats.shape
    devices = counts.shape[1]
    cap = total // devices
    ids = ids.reshape(devices, 1, cap)
    rank = jnp.arange(cap, dtype=jnp.int32)[None, None, :]
    group = jnp.where(rank < counts.reshape(devices, 1, 1), ids // depth, groups)
    tags = jnp.concatenate([group, ids % depth], axis=1).astype(BF16)
    rows = feats.reshape(chan, devices, cap).transpose(1, 0, 2)
    return jnp.concatenate([rows, jnp.pad(tags, ((0, 0), (0, 6), (0, 0)))], axis=1)


def hot_rows(row, first, count):
    index = lax.broadcasted_iota(jnp.int32, (count, LANES), 0).astype(F32).astype(BF16)
    row = jnp.broadcast_to(row, (count, LANES)).astype(BF16)
    return jnp.where(index + jnp.asarray(first, BF16) == row, jnp.ones_like(row), jnp.zeros_like(row))


def scatter_kernel(
    halves, chan, size_y, sides_ref, recv_ref, act_ref, first_ref, second_ref, tags_ref,
    masked, hot, tags_held, sems,
):
    chunks = recv_ref.shape[0]
    groups, depth = act_ref.shape
    for d in range(chunks):
        tags_held[d] = recv_ref[d, halves * chan :, :]
    kept = started(tags_held, tags_ref, sems.at[0])
    for d in range(chunks):
        block = recv_ref[d]
        tags = block[halves * chan :, :].astype(F32)
        for h in range(halves):
            feats = block[h * chan : (h + 1) * chan, :]
            lanes = slice((d * halves + h) * LANES, (d * halves + h + 1) * LANES)
            group = jnp.broadcast_to(tags[h : h + 1, :], (chan, LANES)).astype(BF16)
            for k in range(groups):
                masked[k * chan : (k + 1) * chan, lanes] = jnp.where(
                    group == k, feats, jnp.zeros_like(feats)
                )
            for row in range(0, depth, 32):
                hot[row : row + 32, lanes] = hot_rows(
                    tags[halves + h : halves + h + 1, :], row, 32
                )
    acc = lax.dot_general(masked[...], hot[...], NT, preferred_element_type=F32)
    odd = sides_ref[0] != 0
    half = size_y // 2
    for k in range(groups // 2):
        p, q = k // size_y, k % size_y
        row = ((q // half) * 4 + p * 2 + q % half) * chan
        blocks = []
        for n in (k, k + groups // 2):
            block = acc[n * chan : (n + 1) * chan, :] * act_ref[n : n + 1, :]
            blocks.append(block.astype(BF16))
        first_ref[row : row + chan, :], second_ref[row : row + chan, :] = sided(odd, *blocks)
    kept.wait()


def coarse_kernel(sides_ref, act_ref, cot_ref, first_ref, second_ref, grad_ref, mask_ref):
    depth = act_ref.shape[1]
    chan = cot_ref.shape[2]
    odd = sides_ref[0] != 0
    fine = lax.broadcasted_iota(jnp.int32, (depth, LANES), 0) // 2
    pair = (fine == lax.broadcasted_iota(jnp.int32, (depth, LANES), 1)).astype(BF16)
    acts = act_ref[...]
    sums = jnp.dot(acts.astype(BF16), pair, preferred_element_type=F32)
    masks, grads = [], []
    for x in range(2):
        for y in range(2):
            rows = [sums[(2 * x + a) * 4 + 2 * y + b] for a in range(2) for b in range(2)]
            any_row = (rows[0] + rows[1] + rows[2] + rows[3])[None, :]
            mask = jnp.where(any_row > 0.5, 1.0, 0.0)
            masks.append(mask)
            grads.append((cot_ref[x, y].astype(F32) * mask).astype(BF16))
    for n, grad in enumerate(grads):
        grad_ref[n * chan : (n + 1) * chan, :] = grad
    for y in range(2):
        own = slice(y * chan, (y + 1) * chan)
        first_ref[own, :], second_ref[own, :] = sided(odd, grads[y], grads[2 + y])
    mask_ref[...] = jnp.concatenate(masks + [jnp.zeros((4, LANES), F32)], axis=0)
    blank = jnp.zeros((8, LANES), F32)
    tails = []
    for p in (0, 3):
        rows = acts[4 * p : 4 * p + 4]
        tails.append(jnp.concatenate([rows[:, :LANES], rows[:, LANES:], blank], axis=0))
    tails = sided(odd, *tails)
    for out_ref, tail in zip((first_ref, second_ref), tails):
        out_ref[2 * chan :, :] = tail.astype(BF16)


def coarse_rows_kernel(sides_ref, act_ref, grad_ref, xf_ref, xs_ref, first_ref, second_ref):
    chan = grad_ref.shape[0] // 4
    odd_x, odd_y = sides_ref[0] != 0, sides_ref[1] != 0
    before, after = sided(odd_x, xf_ref[...], xs_ref[...])
    acts = act_ref[...]
    before_acts = before[2 * chan :, :].astype(F32)
    after_acts = after[2 * chan :, :].astype(F32)
    ends = []
    for y, q in ((0, 0), (1, 3)):
        own = slice(y * chan, (y + 1) * chan)
        columns = [before[own], grad_ref[own, :]]
        columns += [grad_ref[(2 + y) * chan : (3 + y) * chan, :], after[own]]
        rows = [before_acts[q : q + 1], before_acts[4 + q : 5 + q]]
        for p in range(4):
            row = acts[4 * p + q : 4 * p + q + 1]
            rows += [row[:, :LANES], row[:, LANES:]]
        rows += [after_acts[q : q + 1], after_acts[4 + q : 5 + q], jnp.zeros((4, LANES), F32)]
        ends.append(columns + [jnp.concatenate(rows, axis=0).astype(BF16)])
    row = 0
    for low, high in zip(*ends):
        own = slice(row, row + low.shape[0])
        first_ref[own, :], second_ref[own, :] = sided(odd_y, low, high)
        row += low.shape[0]


def fine_grad_kernel(
    sides_ref, act_ref, grad_ref, xf_ref, xs_ref, yf_ref, ys_ref, down_ref, acts_ref, own_ref, ring_ref,
    acts_held, wide, up, own, ring, sems,
):
    chan = grad_ref.shape[0] // 4
    depth = act_ref.shape[1]
    acts = act_ref[...]
    x_ends = sided(sides_ref[0] != 0, xf_ref[...], xs_ref[...])
    y_ends = sided(sides_ref[1] != 0, yf_ref[...], ys_ref[...])
    xb, xa = [end[2 * chan :, :].astype(F32) for end in x_ends]
    yb, ya = [end[4 * chan :, :].astype(F32) for end in y_ends]
    rows = []
    for p in range(6):
        rows.append(jnp.concatenate([yb[2 * p : 2 * p + 1], yb[2 * p + 1 : 2 * p + 2]], axis=1))
        for q in range(4):
            if p in (0, 5):
                got = xb if p == 0 else xa
                rows.append(jnp.concatenate([got[q : q + 1], got[4 + q : 5 + q]], axis=1))
            else:
                rows.append(acts[4 * (p - 1) + q : 4 * (p - 1) + q + 1])
        rows.append(jnp.concatenate([ya[2 * p : 2 * p + 1], ya[2 * p + 1 : 2 * p + 2]], axis=1))
    rows.append(jnp.zeros((4, depth), F32))
    acts_held[...] = jnp.concatenate(rows, axis=0)
    kept = [started(acts_held, acts_ref, sems.at[0])]
    for x in range(4):
        for y in range(4):
            if y in (0, 3):
                block = y_ends[y // 3][x * chan : (x + 1) * chan, :]
            elif x in (0, 3):
                block = x_ends[x // 3][(y - 1) * chan : y * chan, :]
            else:
                first = ((x - 1) * 2 + y - 1) * chan
                block = grad_ref[first : first + chan, :]
            wide[(x * 4 + y) * chan : (x * 4 + y + 1) * chan, :] = block
    coarse_z = lax.broadcasted_iota(jnp.int32, (LANES, 2 * depth), 0)
    fine_z = lax.broadcasted_iota(jnp.int32, (LANES, 2 * depth), 1)
    child = jnp.where(fine_z < depth, 0, 1)
    spread = (2 * coarse_z + child == fine_z - child * depth).astype(BF16)
    up[...] = jnp.dot(wide[...], spread, preferred_element_type=F32).astype(BF16)
    for x in range(4):
        for y in range(4):
            those = slice((x * 4 + y) * chan, (x * 4 + y + 1) * chan)
            both = jnp.concatenate([up[those, :depth], up[those, depth:]], axis=0)
            grads = jnp.dot(down_ref[...], both, preferred_element_type=F32)
            for a in range(2):
                for b in range(2):
                    column = (2 * x + a - 1, 2 * y + b - 1)
                    block = grads[(a * 2 + b) * chan : (a * 2 + b + 1) * chan]
                    if column in OWN:
                        n = OWN.index(column)
                        own[n * chan : (n + 1) * chan, :] = block
                    elif column in RING:
                        n = RING.index(column)
                        ring[n * chan : (n + 1) * chan, :] = block
    kept.append(started(own, own_ref, sems.at[1]))
    kept.append(started(ring, ring_ref, sems.at[2]))
    for copy in kept:
        copy.wait()


def bands_kernel(
    front_ref, back_ref, bands_ref, back_bands_ref, own_ref, bands, back_bands, sems
):
    rows, width = front_ref.shape[0], front_ref.shape[1] // 9
    back_rows, back_width = back_ref.shape[0], back_ref.shape[1] // 9
    for t in range(9):
        block = front_ref[:, t * width : (t + 1) * width].astype(F32)
        for q in range(6):
            moved = pltpu.roll(block, q * back_rows, 1) if q else block
            bands[q * rows : (q + 1) * rows, t * width : (t + 1) * width] = moved.astype(BF16)
    kept = [started(bands, bands_ref, sems.at[0])]
    own_ref[...] = bands[rows : 5 * rows, :]
    for t in range(9):
        block = back_ref[:, t * back_width : (t + 1) * back_width].astype(F32)
        for q in range(4):
            moved = pltpu.roll(block, q * rows, 1) if q else block
            back_bands[
                q * back_rows : (q + 1) * back_rows, t * back_width : (t + 1) * back_width
            ] = moved.astype(BF16)
    kept.append(started(back_bands, back_bands_ref, sems.at[1]))
    for copy in kept:
        copy.wait()


def band_inputs(w_sub, in_chan):
    out_chan = w_sub.shape[0]
    taps = w_sub.reshape(out_chan, 3, 3, 3, in_chan)
    front = taps.transpose(0, 1, 3, 2, 4).reshape(out_chan, 9, 3 * in_chan)
    front = jnp.pad(front, ((0, 0), (0, 0), (0, 5 * in_chan)))
    back = taps[:, ::-1, ::-1].transpose(4, 1, 3, 2, 0).reshape(in_chan, 9, 3 * out_chan)
    back = jnp.pad(back, ((0, 0), (0, 0), (0, 3 * out_chan)))
    return front.reshape(out_chan, -1), back.reshape(in_chan, -1)


def rows_kernel(sides_ref, first_ref, second_ref, gf_ref, gs_ref, out_first_ref, out_second_ref):
    odd_x, odd_y = sides_ref[0] != 0, sides_ref[1] != 0
    half = first_ref.shape[0] // 2
    low, high = sided(odd_x, first_ref[...], second_ref[...])
    below, above = sided(odd_x, gf_ref[...], gs_ref[...])
    for n, block in enumerate((below, low, high, above)):
        own = slice(n * half, (n + 1) * half)
        out_first_ref[own, :], out_second_ref[own, :] = sided(odd_y, block[:half], block[half:])


def columns_kernel(
    chan, sides_ref, first_ref, second_ref, gf_ref, gs_ref, yf_ref, ys_ref, front_ref, rear_ref, swap_ref
):
    odd_x, odd_y, place = sides_ref[0] != 0, sides_ref[1] != 0, sides_ref[2]
    low, high = sided(odd_x, first_ref[...], second_ref[...])
    below, above = sided(odd_x, gf_ref[...], gs_ref[...])
    left, right = sided(odd_y, yf_ref[...], ys_ref[...])
    for n, own in enumerate((below, low, high, above)):
        for p in range(2):
            for y in range(8):
                if y in (0, 1, 6, 7):
                    got = left if y < 2 else right
                    row = (n * 4 + p * 2 + y % 2) * chan
                else:
                    got = own
                    row = (((y - 2) // 2) * 4 + p * 2 + y % 2) * chan
                block = got[row : row + chan]
                to = ((n * 2 + p) * 8 + y) * chan
                front_ref[to : to + chan, :] = block[:, :LANES]
                rear_ref[to : to + chan, :] = block[:, LANES:]
                swap_ref[to : to + chan, :] = jnp.where(
                    place == 0, block[:, LANES:], block[:, :LANES]
                )


def shifted(low, high, before, after, step):
    lane = lax.broadcasted_iota(jnp.int32, low.shape, 1)
    if step > 0:
        turned = [pltpu.roll(tile.astype(F32), LANES - 1, 1) for tile in (low, high, after)]
        edge = lane == LANES - 1
        tiles = [jnp.where(edge, turned[1], turned[0]), jnp.where(edge, turned[2], turned[1])]
    else:
        turned = [pltpu.roll(tile.astype(F32), 1, 1) for tile in (before, low, high)]
        edge = lane == 0
        tiles = [jnp.where(edge, turned[0], turned[1]), jnp.where(edge, turned[1], turned[2])]
    return tiles[0].astype(BF16), tiles[1].astype(BF16)


def keep(tile, wanted):
    return jnp.where(wanted, tile, jnp.zeros_like(tile))


def to_rows(columns):
    lane = lax.broadcasted_iota(jnp.int32, (LANES, LANES), 1)
    wide = jnp.zeros((LANES, LANES), F32)
    for n, column in enumerate(columns):
        tall = jnp.concatenate([column, jnp.zeros((LANES - column.shape[0], 1), F32)], axis=0)
        wide = jnp.where(lane == n, tall, wide)
    return wide.T[:8, :]


def to_columns(rows, chan):
    wide = jnp.concatenate(rows + [jnp.zeros((LANES - len(rows), LANES), F32)], axis=0).T
    return [wide[:chan, n : n + 1] for n in range(len(rows))]


def conv_kernel(
    only_two, sides_ref, low_ref, high_ref, before_ref, after_ref, bands_ref, acts_ref,
    hidden_ref, stack_ref, stats_ref, hidden, stack, sems,
):
    rows = low_ref.shape[0] // 8
    depth = acts_ref.shape[1]
    chan = bands_ref.shape[0] // 4
    place = sides_ref[2]
    kept = []
    total = jnp.zeros((chan, depth), F32)
    count = jnp.zeros((1, depth), F32)
    for x in range(8):
        own = slice(x * rows, (x + 1) * rows)
        low, high = low_ref[own, :], high_ref[own, :]
        before, after = before_ref[own, :], after_ref[own, :]
        if only_two:
            before, after = keep(before, place != 0), keep(after, place == 0)
        for n, step in enumerate((-1, 0, 1)):
            tiles = (low, high) if step == 0 else shifted(low, high, before, after, step)
            to = slice((x * 3 + n) * rows, (x * 3 + n + 1) * rows)
            stack[to, :LANES] = tiles[0]
            stack[to, LANES:] = tiles[1]
        own = rows_of(x, 3 * rows)
        kept.append(started(stack.at[own, :], stack_ref.at[own, :], sems.at[x]))
        p = x - 2
        if not 1 <= p <= 4:
            continue
        first = p * 3 * rows
        out = jnp.dot(
            bands_ref[...], stack[first : first + 9 * rows, :], preferred_element_type=F32
        )
        for q in range(1, 5):
            act = acts_ref[p * 6 + q : p * 6 + q + 1, :]
            block = out[(q - 1) * chan : q * chan] * act
            n = OWN.index((p, q))
            hidden[n * chan : (n + 1) * chan, :] = block
            total = total + block
            count = count + act
        own = rows_of(p - 1, 4 * chan)
        kept.append(started(hidden.at[own, :], hidden_ref.at[own, :], sems.at[7 + p]))
    count = jnp.sum(count, axis=1, keepdims=True)
    total = jnp.sum(total, axis=1, keepdims=True)
    mean = total / jnp.maximum(count, 1.0)
    squares = jnp.zeros((chan, depth), F32)
    for n, (p, q) in enumerate(OWN):
        act = acts_ref[p * 6 + q : p * 6 + q + 1, :]
        centred = (hidden[n * chan : (n + 1) * chan, :] - mean) * act
        squares = squares + centred * centred
    squares = jnp.sum(squares, axis=1, keepdims=True)
    packed = to_rows([total, squares, jnp.broadcast_to(count, (chan, 1))])
    for d in range(stats_ref.shape[0]):
        stats_ref[d] = packed
    for copy in kept:
        copy.wait()


def conv_ring_kernel(bands_ref, acts_ref, stack_ref, hidden_ref, bands, acts, stack, hidden, sems):
    rows = stack.shape[0] // 24
    wide = bands.shape[0]
    chan = wide // 6
    got = [
        started(acts_ref, acts, sems.at[0]),
        started(bands_ref, bands, sems.at[1]),
        started(stack_ref, stack, sems.at[2]),
    ]
    for copy in got:
        copy.wait()
    for p in range(6):
        taps = stack[p * 3 * rows : (p * 3 + 9) * rows, :]
        if p in (0, 5):
            out = jnp.dot(bands[...], taps, preferred_element_type=F32)
            columns = range(6)
        else:
            ends = jnp.concatenate([bands[:chan, :], bands[5 * chan :, :]], axis=0)
            out = jnp.dot(ends, taps, preferred_element_type=F32)
            columns = (0, 5)
        for i, q in enumerate(columns):
            n = RING.index((p, q))
            hidden[n * chan : (n + 1) * chan, :] = (
                out[i * chan : (i + 1) * chan] * acts[p * 6 + q : p * 6 + q + 1, :]
            )
    kept = started(hidden, hidden_ref, sems.at[3])
    kept.wait()


def merged_stats(stats_ref):
    totals, squares, counts = stats_ref[:, 0, :], stats_ref[:, 1, :], stats_ref[:, 2, :]
    count = jnp.sum(counts, axis=0, keepdims=True)
    average = jnp.sum(totals, axis=0, keepdims=True) / count
    off = totals / jnp.maximum(counts, 1.0) - average
    spread = jnp.sum(squares + counts * off * off, axis=0, keepdims=True)
    return count, average, lax.rsqrt(spread / count + EPS)


def norm_kernel(
    columns, stats_ref, params_ref, hidden_ref, fine_ref, acts_ref, *rest
):
    own = columns is OWN
    if own:
        pre_ref, out_ref, sums_ref, stats, hidden, fine, acts, pre, outs, sems = rest
    else:
        (out_ref, grad_ref, mask_ref, down_ref, pre_ref, coarse_ref, raw_ref) = rest[:7]
        stats, hidden, fine, acts, pre, outs, grads, taps, sems = rest[7:]
    chan = hidden.shape[0] // len(columns)
    depth = acts.shape[1]
    got_stats = started(stats_ref, stats, sems.at[0])
    got_acts = started(acts_ref, acts, sems.at[1])
    cuts = [n * chan for n in range(0, len(columns) + 1, 4)]
    parts = len(cuts) - 1
    got = started_rows(hidden_ref, hidden, cuts, sems.at[pl.ds(2, parts)])
    got_fine = started_rows(fine_ref, fine, cuts, sems.at[pl.ds(2 + parts, parts)])
    if not own:
        last = 2 + 2 * parts
        got_down = [
            started(out_ref, outs, sems.at[last + 1]),
            started(grad_ref, grads, sems.at[last + 2]),
        ]
    got_stats.wait()
    count, average, inverse = merged_stats(stats)
    full = (chan, LANES)
    average, inverse, gain, shift = [
        jnp.broadcast_to(column, full)
        for column in to_columns([average, inverse, params_ref[0:1, :], params_ref[1:2, :]], chan)
    ]
    sum_shift = jnp.zeros((chan, LANES), F32)
    sum_gain = jnp.zeros((chan, LANES), F32)
    got_acts.wait()
    for n, (p, q) in enumerate(columns):
        if n % 4 == 0:
            got[n // 4].wait()
            got_fine[n // 4].wait()
        own_rows = slice(n * chan, (n + 1) * chan)
        for half in range(depth // LANES):
            lanes = slice(half * LANES, (half + 1) * LANES)
            act = acts[p * 6 + q : p * 6 + q + 1, lanes]
            normed = (hidden[own_rows, lanes] - average) * inverse
            x = gain * normed + shift
            square = x * x
            bent = jnp.tanh(GELU_SCALE * (x + GELU_CUBE * (square * x)))
            cdf = 0.5 + 0.5 * bent
            slope = cdf + (0.5 * x) * (1.0 - bent * bent) * (
                GELU_SCALE + (3.0 * GELU_CUBE * GELU_SCALE) * square
            )
            grad = (act * slope) * fine[own_rows, lanes]
            pre[own_rows, lanes] = grad
            if own:
                sum_shift = sum_shift + grad
                sum_gain = sum_gain + grad * normed
                outs[own_rows, lanes] = (x * cdf * act).astype(BF16)
    kept = [started(pre, pre_ref, sems.at[2 + 2 * parts])]
    if own:
        kept.append(started(outs, out_ref, sems.at[3 + 2 * parts]))
        sums = to_rows(
            [jnp.sum(sum_shift, axis=1, keepdims=True), jnp.sum(sum_gain, axis=1, keepdims=True)]
        )
        for d in range(sums_ref.shape[0]):
            sums_ref[d] = sums
    else:
        for copy in got_down:
            copy.wait()
        down_conv(outs, grads, mask_ref, down_ref, coarse_ref, raw_ref, taps)
    for copy in kept:
        copy.wait()


def down_conv(outs, grads, mask_ref, down_ref, coarse_ref, raw_ref, stack):
    depth = outs.shape[1]
    chan = grads.shape[0] // 4
    source = lax.broadcasted_iota(jnp.int32, (depth, depth), 0)
    target = lax.broadcasted_iota(jnp.int32, (depth, depth), 1)
    wanted = jnp.where(target < LANES, 2 * target, 2 * (target - LANES) + 1)
    sort = (source == wanted).astype(BF16)
    parted = jnp.dot(outs[...], sort, preferred_element_type=F32).astype(BF16)
    for x in range(2):
        for y in range(2):
            for a in range(2):
                for b in range(2):
                    row = ((2 * x + a) * 4 + 2 * y + b) * chan
                    lanes = slice((x * 2 + y) * LANES, (x * 2 + y + 1) * LANES)
                    to = (a * 4 + b * 2) * chan
                    stack[to : to + chan, lanes] = parted[row : row + chan, :LANES]
                    stack[to + chan : to + 2 * chan, lanes] = parted[row : row + chan, LANES:]
    sums = jnp.dot(down_ref[...], stack[...], preferred_element_type=F32)
    for n in range(4):
        coarse_ref[n] = (sums[:, n * LANES : (n + 1) * LANES] * mask_ref[n : n + 1, :]).astype(
            BF16
        )
    wide = jnp.concatenate([grads[n * chan : (n + 1) * chan, :] for n in range(4)], axis=1)
    raw = lax.dot_general(wide, stack[...], NT, preferred_element_type=F32)
    for n in range(4):
        raw_ref[n * chan : (n + 1) * chan, :] = raw[:, n * LANES : (n + 1) * LANES]


def hidden_grad_kernel(
    in_chan, sides_ref, stats_ref, sums_ref, params_ref, hidden_ref, hidden_ring_ref, pre_ref,
    pre_ring_ref, acts_ref, stack_ref, raw_ref, front_ref, rear_ref, swap_ref, small_ref, out_ref,
    stats, hidden, hidden_ring, pre, pre_ring, acts, stack, raw, front, rear, acc, sems,
):
    chan = hidden.shape[0] // 16
    place = sides_ref[2]
    got_stats = started(stats_ref, stats, sems.at[0])
    got_acts = started(acts_ref, acts, sems.at[1])
    got = []
    for n, (source, target) in enumerate(
        ((hidden_ref, hidden), (pre_ref, pre), (hidden_ring_ref, hidden_ring), (pre_ring_ref, pre_ring))
    ):
        cuts = [n * chan for n in range(0, target.shape[0] // chan + 1, 4)]
        got.append(started_rows(source, target, cuts, sems.at[pl.ds(4 + 5 * n, len(cuts) - 1)]))
    got = list(zip(*got[:2])) + list(zip(*got[2:]))
    got_stack = started(
        stack_ref.at[pl.ds(stack.shape[0] // 6, stack.shape[0]), :], stack, sems.at[2]
    )
    got_raw = started(raw_ref, raw, sems.at[3])
    raw_shift = jnp.sum(sums_ref[:, 0, :], axis=0, keepdims=True)
    raw_gain = jnp.sum(sums_ref[:, 1, :], axis=0, keepdims=True)
    got_stats.wait()
    count, average, inverse = merged_stats(stats)
    scale = lax.rsqrt(count)
    small_ref[...] = jnp.concatenate(
        [raw_shift * scale, raw_gain * scale, scale, jnp.zeros((5, LANES), F32)], axis=0
    )
    columns = [average, inverse, raw_shift / count, raw_gain / count, params_ref[0:1, :]]
    average, inverse, mean_shift, mean_gain, gain = [
        jnp.broadcast_to(column, (chan, LANES)) for column in to_columns(columns, chan)
    ]
    weight = gain * inverse
    got_acts.wait()
    kept = []
    for n, (p, q) in enumerate(OWN + RING):
        if n % 4 == 0:
            for copy in got[n // 4]:
                copy.wait()
        held_hidden, held_pre = (hidden, pre) if n < 16 else (hidden_ring, pre_ring)
        own = slice(n * chan, (n + 1) * chan) if n < 16 else slice((n - 16) * chan, (n - 15) * chan)
        to = slice((p * 6 + q) * chan, (p * 6 + q + 1) * chan)
        tiles = []
        for half, held in enumerate((front, rear)):
            lanes = slice(half * LANES, (half + 1) * LANES)
            act = acts[p * 6 + q : p * 6 + q + 1, lanes]
            normed = (held_hidden[own, lanes] - average) * inverse
            grad = held_pre[own, lanes] - (mean_shift + normed * mean_gain)
            tiles.append(((act * weight) * grad).astype(BF16))
            held[to, :] = tiles[-1]
        swap_ref[to, :] = jnp.where(place == 0, tiles[1], tiles[0])
    kept.append(started(front, front_ref, sems.at[24]))
    kept.append(started(rear, rear_ref, sems.at[25]))
    got_stack.wait()
    got_raw.wait()
    rows = stack.shape[0] // 6
    band = rows // 3
    for p in range(4):
        own = slice(((p + 1) * 6 + 1) * chan, ((p + 1) * 6 + 5) * chan)
        grads = jnp.concatenate([front[own, :], rear[own, :]], axis=1)
        for dx in range(3):
            first = (p + dx) * rows
            part = lax.dot_general(
                stack[first : first + rows, :], grads, NT, preferred_element_type=F32
            )
            if p == 0:
                acc[dx] = part
            else:
                acc[dx] += part
    low = lax.broadcasted_iota(jnp.int32, (in_chan, LANES), 1) < chan
    for dx in range(3):
        for dy in range(3):
            for dz in range(3):
                blocks = []
                for q in range(4):
                    row = dz * band + (q + 1 + dy) * in_chan
                    lanes = slice((q // 2) * LANES, (q // 2 + 1) * LANES)
                    blocks.append(acc[dx, row : row + in_chan, lanes])
                both = jnp.where(low, blocks[0] + blocks[2], blocks[1] + blocks[3])
                folded = (both + pltpu.roll(both, chan, 1)).astype(out_ref.dtype)
                tap = (dx * 3 + dy) * 3 + dz
                if tap < 16:
                    out_ref[tap * in_chan : (tap + 1) * in_chan, :chan] = folded[:, :chan]
                else:
                    to = (tap - 16) * in_chan
                    out_ref[to : to + in_chan, chan:] = folded[:, chan:]
    out_ref[11 * in_chan : 16 * in_chan, chan:] = jnp.zeros(
        (5 * in_chan, LANES - chan), out_ref.dtype
    )
    tail = 16 * in_chan
    out_ref[tail : tail + 4 * chan, :] = raw[...].astype(out_ref.dtype)
    left = out_ref.shape[0] - tail - 4 * chan
    if left:
        out_ref[tail + 4 * chan :, :] = jnp.zeros((left, LANES), out_ref.dtype)
    for copy in kept:
        copy.wait()


def point_grad_kernel(
    only_two, halves, chan, sides_ref, front_ref, rear_ref, before_ref, after_ref, bands_ref, act_ref,
    tags_ref, out_ref, front, rear, bands, acts, tags_held, stack, cells, sems,
):
    rows = front.shape[0] // 6
    groups, depth = acts.shape
    place_z = sides_ref[2]
    got = []
    for x in range(6):
        own = rows_of(x, rows)
        got.append(
            (
                started(front_ref.at[own, :], front.at[own, :], sems.at[3 + x]),
                started(rear_ref.at[own, :], rear.at[own, :], sems.at[9 + x]),
            )
        )
    late = [
        started(bands_ref, bands, sems.at[0]),
        started(act_ref, acts, sems.at[1]),
        started(tags_ref, tags_held, sems.at[2]),
    ]
    for x in range(6):
        for copy in got[x]:
            copy.wait()
        own = slice(x * rows, (x + 1) * rows)
        low, high = front[own, :], rear[own, :]
        before, after = before_ref[own, :], after_ref[own, :]
        if only_two:
            before, after = keep(before, place_z != 0), keep(after, place_z == 0)
        for n, step in enumerate((1, 0, -1)):
            tiles = (low, high) if step == 0 else shifted(low, high, before, after, step)
            to = slice((x * 3 + n) * rows, (x * 3 + n + 1) * rows)
            stack[to, :LANES] = tiles[0]
            stack[to, LANES:] = tiles[1]
    for copy in late:
        copy.wait()
    for p in range(4):
        first = p * 3 * rows
        grid = jnp.dot(
            bands[...], stack[first : first + 9 * rows, :], preferred_element_type=F32
        )
        for q in range(4):
            k = p * 4 + q
            cells[k * chan : (k + 1) * chan, :] = (
                grid[q * chan : (q + 1) * chan] * acts[k : k + 1, :]
            ).astype(BF16)

    def from_cells(d):
        tags = tags_held[d].astype(F32)
        hot = jnp.concatenate(
            [hot_rows(tags[halves + h : halves + h + 1, :], 0, depth) for h in range(halves)], axis=1
        )
        found = jnp.dot(cells[...], hot, preferred_element_type=F32)
        for h in range(halves):
            group = jnp.broadcast_to(tags[h : h + 1, :], (chan, LANES))
            lanes = slice(h * LANES, (h + 1) * LANES)
            out = jnp.zeros((chan, LANES), F32)
            for k in range(groups):
                out = jnp.where(group == k, found[k * chan : (k + 1) * chan, lanes], out)
            out_ref[d, h * chan : (h + 1) * chan, :] = out.astype(BF16)

    together = 16

    def step(s, carry):
        for j in range(together):
            from_cells(together * s + j)
        return carry

    lax.fori_loop(0, tags_held.shape[0] // together, step, 0)


def piece_kernel(parts_ref, points_ref, out_ref):
    rows = points_ref.shape[1]
    piece = jnp.sum(parts_ref[...].astype(F32), axis=0).astype(BF16)
    for d in range(out_ref.shape[0]):
        out_ref[d, :rows, :] = points_ref[d]
        out_ref[d, rows:, :] = piece


def sum_kernel(parts_ref, out_ref):
    piece = jnp.sum(parts_ref[...].astype(F32), axis=0).astype(BF16)
    for d in range(out_ref.shape[0]):
        out_ref[d] = piece


def weights_out(rows, small_ref, in_chan, sub_ref, down_ref):
    chan = down_ref.shape[0]
    scale = small_ref[2:3, 0:1]
    for n in range(4):
        turned = rows(n).T * scale
        sub_ref[:, n * LANES : (n + 1) * LANES] = turned[:chan]
        left = sub_ref.shape[1] - 16 * in_chan - n * LANES
        if left > 0:
            width = min(left, LANES)
            first = 16 * in_chan + n * LANES
            sub_ref[:, first : first + width] = turned[chan:, :width]
    for n in range(2):
        both = rows(4 + n) * scale
        down_ref[:, 2 * n * LANES : (2 * n + 1) * LANES] = both[:chan]
        down_ref[:, (2 * n + 1) * LANES : (2 * n + 2) * LANES] = both[chan:]


def last_kernel(halves, chan, got_ref, small_ref, points_ref, sub_ref, down_ref, flat):
    devices = got_ref.shape[0]
    piece = got_ref.shape[1] - halves * chan
    for d in range(devices):
        block = got_ref[d]
        for h in range(halves):
            first = (d * halves + h) * LANES
            points_ref[:, first : first + LANES] = block[h * chan : (h + 1) * chan, :]
        flat[d * piece : (d + 1) * piece, :] = block[halves * chan :, :].astype(F32)
    weights_out(lambda n: flat[n * LANES : (n + 1) * LANES, :], small_ref, chan, sub_ref, down_ref)


def weights_kernel(chan, got_ref, small_ref, sub_ref, down_ref, flat):
    piece = got_ref.shape[1]
    for d in range(got_ref.shape[0]):
        flat[d * piece : (d + 1) * piece, :] = got_ref[d].astype(F32)
    weights_out(lambda n: flat[n * LANES : (n + 1) * LANES, :], small_ref, chan, sub_ref, down_ref)


def on_device(
    point_feats, voxel_ids, send_counts, active, w_sub, w_down, bn_gain, bn_shift, cotangent
):
    in_chan, slot_total = point_feats.shape
    devices = send_counts.shape[1]
    slot_cap = slot_total // devices
    size_x, size_y, size_z = active.shape
    groups = size_x * size_y
    out_chan = w_sub.shape[0]
    only_two = lax.axis_size("gz") == 2
    sides = jnp.stack(
        [lax.axis_index("gx") % 2, lax.axis_index("gy") % 2, lax.axis_index("gz")]
    ).astype(jnp.int32)
    aligned = slot_cap % LANES == 0
    halves = slot_cap // LANES if aligned else 1
    rows_x, rows_6, rows_64 = groups // 2 * in_chan, 36 * out_chan, 64 * in_chan
    wide, back_wide = 6 * out_chan, 4 * in_chan

    if aligned:
        payload = local_call(
            functools.partial(pack_kernel, halves, groups, size_z),
            [((devices, halves * in_chan + 8, LANES), BF16)],
            send_counts, point_feats, voxel_ids.reshape(-1, LANES),
            scratch=[((in_chan, slot_total), BF16), ((devices * halves, LANES), jnp.int32)],
            scalars=[((1, devices), jnp.int32)],
            hbm=(0, 1, 2), copies=6, moved=2e6,
        )[0]
        recv = everyone(payload)
    else:
        payload = pack_plain(point_feats, voxel_ids, send_counts, groups, size_z)
        together = LANES // slot_cap
        recv = everyone(payload)
        recv = recv.reshape(devices // together, together, in_chan + 8, slot_cap)
        recv = recv.transpose(0, 2, 1, 3).reshape(devices // together, in_chan + 8, LANES)
    chunks = recv.shape[0]

    acts = active.reshape(groups, size_z).astype(F32)
    params = jnp.pad(jnp.stack([bn_gain, bn_shift]), ((0, 6), (0, LANES - out_chan)))
    front, back = band_inputs(w_sub, in_chan)
    cot = cotangent.transpose(1, 2, 0, 3)
    *ends, grad_c, coarse_mask = local_call(
        coarse_kernel,
        [((2 * out_chan + 16, LANES), BF16)] * 2
        + [((4 * out_chan, LANES), BF16), ((8, LANES), F32)],
        sides, acts, cot, smem=(0,), moved=2e5,
    )
    cot_x = swaps(*ends, "gx")
    ends = local_call(
        coarse_rows_kernel,
        [((4 * out_chan + 16, LANES), BF16)] * 2,
        sides, acts, grad_c, *cot_x, smem=(0,), moved=2e5,
    )
    cot_y = swaps(*ends, "gy")
    by_child = (
        w_down.reshape(out_chan, 4, 2, out_chan)
        .transpose(1, 3, 2, 0)
        .reshape(4 * out_chan, 2 * out_chan)
    )
    recv, acts, grad_c, cot_x, cot_y, by_child, front, back, params = lax.optimization_barrier(
        (recv, acts, grad_c, cot_x, cot_y, by_child, front, back, params)
    )

    *mine, tags = local_call(
        functools.partial(scatter_kernel, halves, in_chan, size_y),
        [((rows_x, size_z), BF16)] * 2 + [((chunks, 8, LANES), BF16)],
        sides, recv, acts,
        scratch=[
            ((groups * in_chan, chunks * halves * LANES), BF16),
            ((size_z, chunks * halves * LANES), BF16),
            ((chunks, 8, LANES), BF16),
        ],
        smem=(0,), hbm_outs=(2,), copies=1, moved=2e7,
    )
    got_x = swaps(*mine, "gx")
    own, ring = ((16 * out_chan, size_z), F32), ((20 * out_chan, size_z), F32)
    acts_wide, *fine_grad = local_call(
        fine_grad_kernel,
        [((40, size_z), F32), own, ring],
        sides, acts, grad_c, *cot_x, *cot_y, by_child,
        scratch=[
            ((40, size_z), F32),
            ((16 * out_chan, LANES), BF16),
            ((16 * out_chan, 2 * size_z), BF16),
            own,
            ring,
        ],
        smem=(0,), hbm_outs=(0, 1, 2), copies=3, moved=4e6,
    )
    got_x, acts_wide, fine_grad = lax.optimization_barrier((got_x, acts_wide, fine_grad))
    ends = local_call(
        rows_kernel,
        [((2 * rows_x, size_z), BF16)] * 2,
        sides, *mine, *got_x, smem=(0,), moved=1e6,
    )
    got_y = swaps(*ends, "gy")
    bands_shape, back_shape = (wide, 9 * 8 * in_chan), (back_wide, 9 * 6 * out_chan)
    own_bands_shape = (4 * out_chan, bands_shape[1])
    bands, back_bands, own_bands = local_call(
        bands_kernel,
        [(bands_shape, BF16), (back_shape, BF16), (own_bands_shape, BF16)],
        front, back,
        scratch=[(bands_shape, BF16), (back_shape, BF16)],
        hbm_outs=(0, 1), copies=2, moved=4e6,
    )
    got_y, bands, back_bands, own_bands = lax.optimization_barrier(
        (got_y, bands, back_bands, own_bands)
    )
    tile_low, tile_high, swap = local_call(
        functools.partial(columns_kernel, in_chan),
        [((rows_64, LANES), BF16)] * 3,
        sides, *mine, *got_x, *got_y, smem=(0,), moved=3e6,
    )
    before, after = z_exchange(tile_low, tile_high, swap)

    stats_shape = (devices, 8, LANES)
    stack_shape = (3 * rows_64, size_z)
    own_hidden, stack, stats = local_call(
        functools.partial(conv_kernel, only_two),
        [own, (stack_shape, BF16), (stats_shape, F32)],
        sides, tile_low, tile_high, before, after, own_bands, acts_wide,
        scratch=[own, (stack_shape, BF16)],
        smem=(0,), hbm_outs=(0, 1), copies=12, moved=1e7,
    )
    stats_in = everyone(stats)
    ring_hidden = local_call(
        conv_ring_kernel,
        [ring],
        bands, acts_wide, stack,
        scratch=[(bands_shape, BF16), ((40, size_z), F32), (stack_shape, BF16), ring],
        hbm=(0, 1, 2), hbm_outs=(0,), copies=4, moved=1e7,
    )[0]
    stats_in, ring_hidden = lax.optimization_barrier((stats_in, ring_hidden))
    held = [(stats_shape, F32)]
    own_pre, fine_out, sums = local_call(
        functools.partial(norm_kernel, OWN),
        [own, ((groups * out_chan, size_z), BF16), (stats_shape, F32)],
        stats_in, params, own_hidden, fine_grad[0], acts_wide,
        scratch=held + [own, own, ((40, size_z), F32), own, ((groups * out_chan, size_z), BF16)],
        hbm=(2, 3, 4), hbm_outs=(0, 1), copies=12, moved=5e6,
    )
    sums_in = everyone(sums)
    ring_pre, coarse, raw_down = local_call(
        functools.partial(norm_kernel, RING),
        [ring, ((4, out_chan, LANES), BF16), ((4 * out_chan, LANES), F32)],
        stats_in, params, ring_hidden, fine_grad[1], acts_wide, fine_out, grad_c, coarse_mask, w_down,
        scratch=held
        + [
            ring,
            ring,
            ((40, size_z), F32),
            ring,
            ((groups * out_chan, size_z), BF16),
            ((4 * out_chan, LANES), BF16),
            ((8 * out_chan, 4 * LANES), BF16),
        ],
        hbm=(0, 2, 3, 4, 5, 6), hbm_outs=(0,), copies=15, moved=5e6,
    )
    sums_in, ring_pre, raw_down = lax.optimization_barrier((sums_in, ring_pre, raw_down))
    half_x, half_y, half_z = size_x // 2, size_y // 2, size_z // 2
    coarse_out = coarse.reshape(half_x, half_y, out_chan, half_z).transpose(2, 0, 1, 3)

    piece = -(-(16 * in_chan + 4 * out_chan) // devices)
    piece = -(-piece // 8) * 8
    grad_low, grad_high, grad_swap, small, parts = local_call(
        functools.partial(hidden_grad_kernel, in_chan),
        [((rows_6, LANES), BF16)] * 3 + [((8, LANES), F32), ((devices * piece, LANES), BF16)],
        sides, stats_in, sums_in, params, own_hidden, ring_hidden, own_pre, ring_pre, acts_wide,
        stack, raw_down,
        scratch=[
            (stats_shape, F32),
            own,
            ring,
            own,
            ring,
            ((40, size_z), F32),
            ((rows_64 // 8 * 6 * 3, size_z), BF16),
            ((4 * out_chan, LANES), F32),
            ((rows_6, LANES), BF16),
            ((rows_6, LANES), BF16),
            ((3, 24 * in_chan, 4 * out_chan), F32),
        ],
        smem=(0,), hbm=(1, 4, 5, 6, 7, 8, 9, 10), hbm_outs=(0, 1), copies=26, moved=2e7,
    )
    grad_before, grad_after = z_exchange(grad_low, grad_high, grad_swap)
    parts = everyone(parts.reshape(devices, piece, LANES))

    points = local_call(
        functools.partial(point_grad_kernel, only_two, halves, in_chan),
        [((chunks, halves * in_chan, LANES), BF16)],
        sides, grad_low, grad_high, grad_before, grad_after, back_bands, acts, tags,
        scratch=[
            ((rows_6, LANES), BF16),
            ((rows_6, LANES), BF16),
            (back_shape, BF16),
            ((groups, size_z), F32),
            ((chunks, 8, LANES), BF16),
            ((3 * rows_6, size_z), BF16),
            ((groups * in_chan, size_z), BF16),
        ],
        smem=(0,), hbm=(1, 2, 5, 6, 7), copies=15, moved=2e7,
    )[0]
    parts, points = lax.optimization_barrier((parts, points))
    shapes = [((out_chan, 27 * in_chan), F32), ((out_chan, 8 * out_chan), F32)]
    flat = [((devices * piece, LANES), F32)]
    if aligned:
        both = local_call(
            piece_kernel,
            [((devices, halves * in_chan + piece, LANES), BF16)],
            parts, points, moved=2e6,
        )[0]
        returned, raw_sub, raw_down = local_call(
            functools.partial(last_kernel, halves, in_chan),
            [((in_chan, slot_total), BF16)] + shapes,
            everyone(both), small, scratch=flat, moved=2e6,
        )
    else:
        points = points.reshape(chunks, in_chan, together, slot_cap).transpose(0, 2, 1, 3)
        returned = everyone(points.reshape(devices, in_chan, slot_cap))
        returned = returned.transpose(1, 0, 2).reshape(in_chan, slot_total)
        whole = local_call(sum_kernel, [((devices, piece, LANES), BF16)], parts)[0]
        raw_sub, raw_down = local_call(
            functools.partial(weights_kernel, in_chan), shapes, everyone(whole), small, scratch=flat
        )
    return (
        coarse_out,
        returned,
        raw_sub,
        raw_down,
        small[1, :out_chan],
        small[0, :out_chan],
    )


def solution(mesh):
    in_specs = (
        P(None, AXES),
        P(AXES),
        P(AXES, None),
        P("gx", "gy", "gz"),
        P(),
        P(),
        P(),
        P(),
        P(None, "gx", "gy", "gz"),
    )
    out_specs = (P(None, "gx", "gy", "gz"), P(None, AXES), P(), P(), P(), P())
    return jax.shard_map(
        on_device, mesh=mesh, in_specs=in_specs, out_specs=out_specs, check_vma=False
    )
```

```python
import functools
import math

import jax
import jax.numpy as jnp
from jax import lax
from jax.experimental import pallas as pl
from jax.experimental.pallas import tpu as pltpu
from jax.sharding import PartitionSpec as P

EPS = 1e-05
AXES = ("gx", "gy", "gz")
LANES = 128
GELU_SCALE = 0.7978845608028654
GELU_CUBE = 0.044715
F32 = jnp.float32
BF16 = jnp.bfloat16
NT = (((1,), (1,)), ((), ()))


def local_call(
    kernel, outs, *args, scratch=(), scalars=(), smem=(), hbm=(), hbm_outs=(), copies=0, moved=0, aliases=None
):
    held = sum(math.prod(shape) * jnp.dtype(kind).itemsize for shape, kind in scratch)
    limit = held // 2**20 + 6
    vmem = pl.BlockSpec(memory_space=pltpu.VMEM)
    scalar = pl.BlockSpec(memory_space=pltpu.SMEM)
    far = pl.BlockSpec(memory_space=pltpu.HBM)
    args = [
        pltpu.with_memory_space_constraint(arg, pltpu.HBM) if i in hbm else arg
        for i, arg in enumerate(args)
    ]
    held = [pltpu.VMEM(shape, kind) for shape, kind in scratch]
    held += [pltpu.SMEM(shape, kind) for shape, kind in scalars]
    if copies:
        held.append(pltpu.SemaphoreType.DMA((copies,)))
    return pl.pallas_call(
        kernel,
        out_shape=[
            pltpu.HBM(shape, kind) if i in hbm_outs else jax.ShapeDtypeStruct(shape, kind)
            for i, (shape, kind) in enumerate(outs)
        ],
        in_specs=[
            scalar if i in smem else far if i in hbm else vmem for i in range(len(args))
        ],
        out_specs=[far if i in hbm_outs else vmem for i in range(len(outs))],
        scratch_shapes=held,
        input_output_aliases=aliases or {},
        compiler_params=pltpu.CompilerParams(vmem_limit_bytes=limit * 1024 * 1024),
        cost_estimate=pl.CostEstimate(flops=0, bytes_accessed=int(moved), transcendentals=0),
    )(*args)


def started(source, target, semaphore):
    copy = pltpu.make_async_copy(source, target, semaphore)
    copy.start()
    return copy


def rows_of(n, count):
    return pl.ds(n * count, count)


def started_rows(source, target, cuts, semaphores):
    copies = []
    for n, (begin, end) in enumerate(zip(cuts, cuts[1:])):
        own = pl.ds(begin, end - begin)
        copies.append(started(source.at[own, :], target.at[own, :], semaphores.at[n]))
    return copies


OWN = [(p, q) for p in range(1, 5) for q in range(1, 5)]
RING = [(p, q) for p in range(6) for q in range(6) if (p, q) not in OWN]


def neighbours(axis, step):
    count = lax.axis_size(axis)
    return [(i, i + step) for i in range(count) if 0 <= i + step < count]


def swaps(first, second, axis):
    count = lax.axis_size(axis)
    got = []
    for block, begin in ((first, 0), (second, 1)):
        pairs = [(i, i + 1) for i in range(begin, count - 1, 2)]
        got.append(lax.ppermute(block, axis, pairs + [(j, i) for i, j in pairs]))
    return got


def sided(odd, first, second):
    return jnp.where(odd, first, second), jnp.where(odd, second, first)


def z_exchange(low, high, swap):
    if lax.axis_size("gz") != 2:
        return (
            lax.ppermute(high, "gz", neighbours("gz", 1)),
            lax.ppermute(low, "gz", neighbours("gz", -1)),
        )
    got = lax.ppermute(swap, "gz", [(0, 1), (1, 0)])
    return got, got


def everyone(block):
    return lax.all_to_all(block, AXES, split_axis=0, concat_axis=0, tiled=True)


def pack_kernel(
    halves, groups, depth, counts_ref, feats_ref, ids_ref, out_ref, feats, ids, counts, sems
):
    devices = out_ref.shape[0]
    chan = feats_ref.shape[0]
    parts = 4
    width = feats.shape[1] // parts
    got_ids = started(ids_ref, ids, sems.at[parts])
    got_counts = started(counts_ref, counts, sems.at[parts + 1])
    got = []
    for n in range(parts):
        lanes = pl.ds(n * width, width)
        got.append(started(feats_ref.at[:, lanes], feats.at[:, lanes], sems.at[n]))
    got_ids.wait()
    got_counts.wait()
    rank = lax.broadcasted_iota(jnp.int32, (halves, LANES), 0) * LANES + lax.broadcasted_iota(
        jnp.int32, (halves, LANES), 1
    )
    blank = jnp.zeros((8 - 2 * halves, LANES), F32)
    for d in range(devices):
        those = ids[d * halves : (d + 1) * halves, :]
        usable = rank < counts[0, d]
        group = jnp.where(usable, those // depth, groups).astype(F32)
        place = (those % depth).astype(F32)
        tags = jnp.concatenate([group, place, blank], axis=0)
        out_ref[d, halves * chan :, :] = tags.astype(BF16)
    for d in range(devices):
        if d * parts % devices == 0:
            got[d * parts // devices].wait()
        for h in range(halves):
            first = (d * halves + h) * LANES
            out_ref[d, h * chan : (h + 1) * chan, :] = feats[:, first : first + LANES]


def pack_plain(feats, ids, counts, groups, depth):
    chan, total = feats.shape
    devices = counts.shape[1]
    cap = total // devices
    ids = ids.reshape(devices, 1, cap)
    rank = jnp.arange(cap, dtype=jnp.int32)[None, None, :]
    group = jnp.where(rank < counts.reshape(devices, 1, 1), ids // depth, groups)
    tags = jnp.concatenate([group, ids % depth], axis=1).astype(BF16)
    rows = feats.reshape(chan, devices, cap).transpose(1, 0, 2)
    return jnp.concatenate([rows, jnp.pad(tags, ((0, 0), (0, 6), (0, 0)))], axis=1)


def hot_rows(row, first, count):
    index = lax.broadcasted_iota(jnp.int32, (count, LANES), 0).astype(F32).astype(BF16)
    row = jnp.broadcast_to(row, (count, LANES)).astype(BF16)
    return jnp.where(index + jnp.asarray(first, BF16) == row, jnp.ones_like(row), jnp.zeros_like(row))


def scatter_kernel(
    halves, chan, size_y, sides_ref, recv_ref, act_ref, first_ref, second_ref, tags_ref,
    masked, hot, tags_held, sems,
):
    chunks = recv_ref.shape[0]
    groups, depth = act_ref.shape
    for d in range(chunks):
        tags_held[d] = recv_ref[d, halves * chan :, :]
    kept = started(tags_held, tags_ref, sems.at[0])
    for d in range(chunks):
        block = recv_ref[d]
        tags = block[halves * chan :, :].astype(F32)
        for h in range(halves):
            feats = block[h * chan : (h + 1) * chan, :]
            lanes = slice((d * halves + h) * LANES, (d * halves + h + 1) * LANES)
            group = jnp.broadcast_to(tags[h : h + 1, :], (chan, LANES)).astype(BF16)
            for k in range(groups):
                masked[k * chan : (k + 1) * chan, lanes] = jnp.where(
                    group == k, feats, jnp.zeros_like(feats)
                )
            for row in range(0, depth, 32):
                hot[row : row + 32, lanes] = hot_rows(
                    tags[halves + h : halves + h + 1, :], row, 32
                )
    acc = lax.dot_general(masked[...], hot[...], NT, preferred_element_type=F32)
    odd = sides_ref[0] != 0
    half = size_y // 2
    for k in range(groups // 2):
        p, q = k // size_y, k % size_y
        row = ((q // half) * 4 + p * 2 + q % half) * chan
        blocks = []
        for n in (k, k + groups // 2):
            block = acc[n * chan : (n + 1) * chan, :] * act_ref[n : n + 1, :]
            blocks.append(block.astype(BF16))
        first_ref[row : row + chan, :], second_ref[row : row + chan, :] = sided(odd, *blocks)
    kept.wait()


def coarse_kernel(sides_ref, act_ref, cot_ref, first_ref, second_ref, grad_ref, mask_ref):
    depth = act_ref.shape[1]
    chan = cot_ref.shape[2]
    odd = sides_ref[0] != 0
    fine = lax.broadcasted_iota(jnp.int32, (depth, LANES), 0) // 2
    pair = (fine == lax.broadcasted_iota(jnp.int32, (depth, LANES), 1)).astype(BF16)
    acts = act_ref[...]
    sums = jnp.dot(acts.astype(BF16), pair, preferred_element_type=F32)
    masks, grads = [], []
    for x in range(2):
        for y in range(2):
            rows = [sums[(2 * x + a) * 4 + 2 * y + b] for a in range(2) for b in range(2)]
            any_row = (rows[0] + rows[1] + rows[2] + rows[3])[None, :]
            mask = jnp.where(any_row > 0.5, 1.0, 0.0)
            masks.append(mask)
            grads.append((cot_ref[x, y].astype(F32) * mask).astype(BF16))
    for n, grad in enumerate(grads):
        grad_ref[n * chan : (n + 1) * chan, :] = grad
    for y in range(2):
        own = slice(y * chan, (y + 1) * chan)
        first_ref[own, :], second_ref[own, :] = sided(odd, grads[y], grads[2 + y])
    mask_ref[...] = jnp.concatenate(masks + [jnp.zeros((4, LANES), F32)], axis=0)
    blank = jnp.zeros((8, LANES), F32)
    tails = []
    for p in (0, 3):
        rows = acts[4 * p : 4 * p + 4]
        tails.append(jnp.concatenate([rows[:, :LANES], rows[:, LANES:], blank], axis=0))
    tails = sided(odd, *tails)
    for out_ref, tail in zip((first_ref, second_ref), tails):
        out_ref[2 * chan :, :] = tail.astype(BF16)


def coarse_rows_kernel(sides_ref, act_ref, grad_ref, xf_ref, xs_ref, first_ref, second_ref):
    chan = grad_ref.shape[0] // 4
    odd_x, odd_y = sides_ref[0] != 0, sides_ref[1] != 0
    before, after = sided(odd_x, xf_ref[...], xs_ref[...])
    acts = act_ref[...]
    before_acts = before[2 * chan :, :].astype(F32)
    after_acts = after[2 * chan :, :].astype(F32)
    ends = []
    for y, q in ((0, 0), (1, 3)):
        own = slice(y * chan, (y + 1) * chan)
        columns = [before[own], grad_ref[own, :]]
        columns += [grad_ref[(2 + y) * chan : (3 + y) * chan, :], after[own]]
        rows = [before_acts[q : q + 1], before_acts[4 + q : 5 + q]]
        for p in range(4):
            row = acts[4 * p + q : 4 * p + q + 1]
            rows += [row[:, :LANES], row[:, LANES:]]
        rows += [after_acts[q : q + 1], after_acts[4 + q : 5 + q], jnp.zeros((4, LANES), F32)]
        ends.append(columns + [jnp.concatenate(rows, axis=0).astype(BF16)])
    row = 0
    for low, high in zip(*ends):
        own = slice(row, row + low.shape[0])
        first_ref[own, :], second_ref[own, :] = sided(odd_y, low, high)
        row += low.shape[0]


def fine_grad_kernel(
    sides_ref, act_ref, grad_ref, xf_ref, xs_ref, yf_ref, ys_ref, down_ref, acts_ref, own, ring_ref,
    acts_held, wide, up, ring, sems,
):
    chan = grad_ref.shape[0] // 4
    depth = act_ref.shape[1]
    acts = act_ref[...]
    x_ends = sided(sides_ref[0] != 0, xf_ref[...], xs_ref[...])
    y_ends = sided(sides_ref[1] != 0, yf_ref[...], ys_ref[...])
    xb, xa = [end[2 * chan :, :].astype(F32) for end in x_ends]
    yb, ya = [end[4 * chan :, :].astype(F32) for end in y_ends]
    rows = []
    for p in range(6):
        rows.append(jnp.concatenate([yb[2 * p : 2 * p + 1], yb[2 * p + 1 : 2 * p + 2]], axis=1))
        for q in range(4):
            if p in (0, 5):
                got = xb if p == 0 else xa
                rows.append(jnp.concatenate([got[q : q + 1], got[4 + q : 5 + q]], axis=1))
            else:
                rows.append(acts[4 * (p - 1) + q : 4 * (p - 1) + q + 1])
        rows.append(jnp.concatenate([ya[2 * p : 2 * p + 1], ya[2 * p + 1 : 2 * p + 2]], axis=1))
    rows.append(jnp.zeros((4, depth), F32))
    acts_held[...] = jnp.concatenate(rows, axis=0)
    kept = [started(acts_held, acts_ref, sems.at[0])]
    for x in range(4):
        for y in range(4):
            if y in (0, 3):
                block = y_ends[y // 3][x * chan : (x + 1) * chan, :]
            elif x in (0, 3):
                block = x_ends[x // 3][(y - 1) * chan : y * chan, :]
            else:
                first = ((x - 1) * 2 + y - 1) * chan
                block = grad_ref[first : first + chan, :]
            wide[(x * 4 + y) * chan : (x * 4 + y + 1) * chan, :] = block
    coarse_z = lax.broadcasted_iota(jnp.int32, (LANES, 2 * depth), 0)
    fine_z = lax.broadcasted_iota(jnp.int32, (LANES, 2 * depth), 1)
    child = jnp.where(fine_z < depth, 0, 1)
    spread = (2 * coarse_z + child == fine_z - child * depth).astype(BF16)
    up[...] = jnp.dot(wide[...], spread, preferred_element_type=F32).astype(BF16)
    for x in range(4):
        for y in range(4):
            those = slice((x * 4 + y) * chan, (x * 4 + y + 1) * chan)
            both = jnp.concatenate([up[those, :depth], up[those, depth:]], axis=0)
            grads = jnp.dot(down_ref[...], both, preferred_element_type=F32)
            for a in range(2):
                for b in range(2):
                    column = (2 * x + a - 1, 2 * y + b - 1)
                    block = grads[(a * 2 + b) * chan : (a * 2 + b + 1) * chan]
                    if column in OWN:
                        n = OWN.index(column)
                        own[n * chan : (n + 1) * chan, :] = block
                    elif column in RING:
                        n = RING.index(column)
                        ring[n * chan : (n + 1) * chan, :] = block
    kept.append(started(ring, ring_ref, sems.at[1]))
    for copy in kept:
        copy.wait()


def bands_kernel(
    front_ref, back_ref, bands_ref, back_bands_ref, own_ref, bands, back_bands, sems
):
    rows, width = front_ref.shape[0], front_ref.shape[1] // 9
    back_rows, back_width = back_ref.shape[0], back_ref.shape[1] // 9
    for t in range(9):
        block = front_ref[:, t * width : (t + 1) * width].astype(F32)
        for q in range(6):
            moved = pltpu.roll(block, q * back_rows, 1) if q else block
            bands[q * rows : (q + 1) * rows, t * width : (t + 1) * width] = moved.astype(BF16)
    kept = [started(bands, bands_ref, sems.at[0])]
    own_ref[...] = bands[rows : 5 * rows, :]
    for t in range(9):
        block = back_ref[:, t * back_width : (t + 1) * back_width].astype(F32)
        for q in range(4):
            moved = pltpu.roll(block, q * rows, 1) if q else block
            back_bands[
                q * back_rows : (q + 1) * back_rows, t * back_width : (t + 1) * back_width
            ] = moved.astype(BF16)
    kept.append(started(back_bands, back_bands_ref, sems.at[1]))
    for copy in kept:
        copy.wait()


def band_inputs(w_sub, in_chan):
    out_chan = w_sub.shape[0]
    taps = w_sub.reshape(out_chan, 3, 3, 3, in_chan)
    front = taps.transpose(0, 1, 3, 2, 4).reshape(out_chan, 9, 3 * in_chan)
    front = jnp.pad(front, ((0, 0), (0, 0), (0, 5 * in_chan)))
    back = taps[:, ::-1, ::-1].transpose(4, 1, 3, 2, 0).reshape(in_chan, 9, 3 * out_chan)
    back = jnp.pad(back, ((0, 0), (0, 0), (0, 3 * out_chan)))
    return front.reshape(out_chan, -1), back.reshape(in_chan, -1)


def rows_kernel(sides_ref, first_ref, second_ref, gf_ref, gs_ref, out_first_ref, out_second_ref):
    odd_x, odd_y = sides_ref[0] != 0, sides_ref[1] != 0
    half = first_ref.shape[0] // 2
    low, high = sided(odd_x, first_ref[...], second_ref[...])
    below, above = sided(odd_x, gf_ref[...], gs_ref[...])
    for n, block in enumerate((below, low, high, above)):
        own = slice(n * half, (n + 1) * half)
        out_first_ref[own, :], out_second_ref[own, :] = sided(odd_y, block[:half], block[half:])


def columns_kernel(
    chan, sides_ref, first_ref, second_ref, gf_ref, gs_ref, yf_ref, ys_ref, front_ref, rear_ref, swap_ref
):
    odd_x, odd_y, place = sides_ref[0] != 0, sides_ref[1] != 0, sides_ref[2]
    low, high = sided(odd_x, first_ref[...], second_ref[...])
    below, above = sided(odd_x, gf_ref[...], gs_ref[...])
    left, right = sided(odd_y, yf_ref[...], ys_ref[...])
    for n, own in enumerate((below, low, high, above)):
        for p in range(2):
            for y in range(8):
                if y in (0, 1, 6, 7):
                    got = left if y < 2 else right
                    row = (n * 4 + p * 2 + y % 2) * chan
                else:
                    got = own
                    row = (((y - 2) // 2) * 4 + p * 2 + y % 2) * chan
                block = got[row : row + chan]
                to = ((n * 2 + p) * 8 + y) * chan
                front_ref[to : to + chan, :] = block[:, :LANES]
                rear_ref[to : to + chan, :] = block[:, LANES:]
                swap_ref[to : to + chan, :] = jnp.where(
                    place == 0, block[:, LANES:], block[:, :LANES]
                )


def shifted(low, high, before, after, step):
    lane = lax.broadcasted_iota(jnp.int32, low.shape, 1)
    if step > 0:
        turned = [pltpu.roll(tile.astype(F32), LANES - 1, 1) for tile in (low, high, after)]
        edge = lane == LANES - 1
        tiles = [jnp.where(edge, turned[1], turned[0]), jnp.where(edge, turned[2], turned[1])]
    else:
        turned = [pltpu.roll(tile.astype(F32), 1, 1) for tile in (before, low, high)]
        edge = lane == 0
        tiles = [jnp.where(edge, turned[0], turned[1]), jnp.where(edge, turned[1], turned[2])]
    return tiles[0].astype(BF16), tiles[1].astype(BF16)


def keep(tile, wanted):
    return jnp.where(wanted, tile, jnp.zeros_like(tile))


def to_rows(columns):
    lane = lax.broadcasted_iota(jnp.int32, (LANES, LANES), 1)
    wide = jnp.zeros((LANES, LANES), F32)
    for n, column in enumerate(columns):
        tall = jnp.concatenate([column, jnp.zeros((LANES - column.shape[0], 1), F32)], axis=0)
        wide = jnp.where(lane == n, tall, wide)
    return wide.T[:8, :]


def to_columns(rows, chan):
    wide = jnp.concatenate(rows + [jnp.zeros((LANES - len(rows), LANES), F32)], axis=0).T
    return [wide[:chan, n : n + 1] for n in range(len(rows))]


def stack_kernel(low_ref, high_ref, stack_ref):
    rows = low_ref.shape[0] // 8
    for x in range(8):
        own = slice(x * rows, (x + 1) * rows)
        low, high = low_ref[own, :], high_ref[own, :]
        for n, step in enumerate((-1, 0, 1)):
            tiles = (low, high) if step == 0 else shifted(low, high, high, low, step)
            to = slice((x * 3 + n) * rows, (x * 3 + n + 1) * rows)
            stack_ref[to, :LANES] = tiles[0]
            stack_ref[to, LANES:] = tiles[1]


def patch(stack, x, rows, before, after):
    lane = lax.broadcasted_iota(jnp.int32, before.shape, 1)
    to = slice(x * 3 * rows, (x * 3 + 1) * rows)
    edge = pltpu.roll(before.astype(F32), 1, 1)
    own = stack[to, :LANES].astype(F32)
    stack[to, :LANES] = jnp.where(lane == 0, edge, own).astype(BF16)
    to = slice((x * 3 + 2) * rows, (x * 3 + 3) * rows)
    edge = pltpu.roll(after.astype(F32), LANES - 1, 1)
    own = stack[to, LANES:].astype(F32)
    stack[to, LANES:] = jnp.where(lane == LANES - 1, edge, own).astype(BF16)


def conv_kernel(
    only_two, sides_ref, stack_in_ref, before_ref, after_ref, bands_ref, acts_ref,
    hidden, stack_ref, stats_ref, stack, sems,
):
    rows = before_ref.shape[0] // 8
    depth = acts_ref.shape[1]
    chan = bands_ref.shape[0] // 4
    place = sides_ref[2]
    kept = []
    total = jnp.zeros((chan, depth), F32)
    count = jnp.zeros((1, depth), F32)
    for x in range(8):
        own = slice(x * rows, (x + 1) * rows)
        before, after = before_ref[own, :], after_ref[own, :]
        if only_two:
            before, after = keep(before, place != 0), keep(after, place == 0)
        patch(stack, x, rows, before, after)
        own = rows_of(x, 3 * rows)
        kept.append(started(stack.at[own, :], stack_ref.at[own, :], sems.at[x]))
        p = x - 2
        if not 1 <= p <= 4:
            continue
        first = p * 3 * rows
        out = jnp.dot(
            bands_ref[...], stack[first : first + 9 * rows, :], preferred_element_type=F32
        )
        for q in range(1, 5):
            act = acts_ref[p * 6 + q : p * 6 + q + 1, :]
            block = out[(q - 1) * chan : q * chan] * act
            n = OWN.index((p, q))
            hidden[n * chan : (n + 1) * chan, :] = block
            total = total + block
            count = count + act
    count = jnp.sum(count, axis=1, keepdims=True)
    total = jnp.sum(total, axis=1, keepdims=True)
    mean = total / jnp.maximum(count, 1.0)
    squares = jnp.zeros((chan, depth), F32)
    for n, (p, q) in enumerate(OWN):
        act = acts_ref[p * 6 + q : p * 6 + q + 1, :]
        centred = (hidden[n * chan : (n + 1) * chan, :] - mean) * act
        squares = squares + centred * centred
    squares = jnp.sum(squares, axis=1, keepdims=True)
    packed = to_rows([total, squares, jnp.broadcast_to(count, (chan, 1))])
    for d in range(stats_ref.shape[0]):
        stats_ref[d] = packed
    for copy in kept:
        copy.wait()


def conv_ring_kernel(bands_ref, acts_ref, stack_ref, hidden_ref, bands, acts, stack, hidden, sems):
    rows = stack.shape[0] // 24
    wide = bands.shape[0]
    chan = wide // 6
    got = [
        started(acts_ref, acts, sems.at[0]),
        started(bands_ref, bands, sems.at[1]),
        started(stack_ref, stack, sems.at[2]),
    ]
    for copy in got:
        copy.wait()
    for p in range(6):
        taps = stack[p * 3 * rows : (p * 3 + 9) * rows, :]
        if p in (0, 5):
            out = jnp.dot(bands[...], taps, preferred_element_type=F32)
            columns = range(6)
        else:
            ends = jnp.concatenate([bands[:chan, :], bands[5 * chan :, :]], axis=0)
            out = jnp.dot(ends, taps, preferred_element_type=F32)
            columns = (0, 5)
        for i, q in enumerate(columns):
            n = RING.index((p, q))
            hidden[n * chan : (n + 1) * chan, :] = (
                out[i * chan : (i + 1) * chan] * acts[p * 6 + q : p * 6 + q + 1, :]
            )
    kept = started(hidden, hidden_ref, sems.at[3])
    kept.wait()


def merged_stats(stats_ref):
    totals, squares, counts = stats_ref[:, 0, :], stats_ref[:, 1, :], stats_ref[:, 2, :]
    count = jnp.sum(counts, axis=0, keepdims=True)
    average = jnp.sum(totals, axis=0, keepdims=True) / count
    off = totals / jnp.maximum(counts, 1.0) - average
    spread = jnp.sum(squares + counts * off * off, axis=0, keepdims=True)
    return count, average, lax.rsqrt(spread / count + EPS)


def norm_kernel(
    columns, stats_ref, params_ref, hidden, fine, acts_ref, *rest
):
    own = columns is OWN
    if own:
        pre, out_ref, sums_ref, stats, acts, outs, sums_held, sems = rest
    else:
        hidden_ref, fine_ref = hidden, fine
        (out_ref, grad_ref, mask_ref, down_ref, pre_ref, coarse_ref, raw_ref) = rest[:7]
        stats, hidden, fine, acts, pre, outs, grads, taps, raw, sems = rest[7:]
    chan = hidden.shape[0] // len(columns)
    depth = acts.shape[1]
    got_stats = started(stats_ref, stats, sems.at[0])
    got_acts = started(acts_ref, acts, sems.at[1])
    cuts = [n * chan for n in range(0, len(columns) + 1, 4)]
    parts = len(cuts) - 1
    if not own:
        got = started_rows(hidden_ref, hidden, cuts, sems.at[pl.ds(2, parts)])
        got_fine = started_rows(fine_ref, fine, cuts, sems.at[pl.ds(2 + parts, parts)])
        last = 2 + 2 * parts
        got_down = [
            started(out_ref, outs, sems.at[last + 1]),
            started(grad_ref, grads, sems.at[last + 2]),
        ]
    got_stats.wait()
    count, average, inverse = merged_stats(stats)
    full = (chan, LANES)
    average, inverse, gain, shift = [
        jnp.broadcast_to(column, full)
        for column in to_columns([average, inverse, params_ref[0:1, :], params_ref[1:2, :]], chan)
    ]
    sum_shift = jnp.zeros((chan, LANES), F32)
    sum_gain = jnp.zeros((chan, LANES), F32)
    got_acts.wait()
    for n, (p, q) in enumerate(columns):
        if n % 4 == 0 and not own:
            got[n // 4].wait()
            got_fine[n // 4].wait()
        own_rows = slice(n * chan, (n + 1) * chan)
        for half in range(depth // LANES):
            lanes = slice(half * LANES, (half + 1) * LANES)
            act = acts[p * 6 + q : p * 6 + q + 1, lanes]
            normed = (hidden[own_rows, lanes] - average) * inverse
            x = gain * normed + shift
            square = x * x
            bent = jnp.tanh(GELU_SCALE * (x + GELU_CUBE * (square * x)))
            cdf = 0.5 + 0.5 * bent
            slope = cdf + (0.5 * x) * (1.0 - bent * bent) * (
                GELU_SCALE + (3.0 * GELU_CUBE * GELU_SCALE) * square
            )
            grad = (act * slope) * fine[own_rows, lanes]
            pre[own_rows, lanes] = grad
            if own:
                sum_shift = sum_shift + grad
                sum_gain = sum_gain + grad * normed
                outs[own_rows, lanes] = (x * cdf * act).astype(BF16)
    if own:
        kept = [started(outs, out_ref, sems.at[2])]
        sums = to_rows(
            [jnp.sum(sum_shift, axis=1, keepdims=True), jnp.sum(sum_gain, axis=1, keepdims=True)]
        )
        for d in range(sums_ref.shape[0]):
            sums_held[d] = sums
        kept.append(started(sums_held, sums_ref, sems.at[3]))
    else:
        kept = [started(pre, pre_ref, sems.at[2 + 2 * parts])]
        for copy in got_down:
            copy.wait()
        down_conv(outs, grads, mask_ref, down_ref, coarse_ref, raw, taps)
        kept.append(started(raw, raw_ref, sems.at[last + 3]))
    for copy in kept:
        copy.wait()


def down_conv(outs, grads, mask_ref, down_ref, coarse_ref, raw_ref, stack):
    depth = outs.shape[1]
    chan = grads.shape[0] // 4
    source = lax.broadcasted_iota(jnp.int32, (depth, depth), 0)
    target = lax.broadcasted_iota(jnp.int32, (depth, depth), 1)
    wanted = jnp.where(target < LANES, 2 * target, 2 * (target - LANES) + 1)
    sort = (source == wanted).astype(BF16)
    parted = jnp.dot(outs[...], sort, preferred_element_type=F32).astype(BF16)
    for x in range(2):
        for y in range(2):
            for a in range(2):
                for b in range(2):
                    row = ((2 * x + a) * 4 + 2 * y + b) * chan
                    lanes = slice((x * 2 + y) * LANES, (x * 2 + y + 1) * LANES)
                    to = (a * 4 + b * 2) * chan
                    stack[to : to + chan, lanes] = parted[row : row + chan, :LANES]
                    stack[to + chan : to + 2 * chan, lanes] = parted[row : row + chan, LANES:]
    sums = jnp.dot(down_ref[...], stack[...], preferred_element_type=F32)
    for n in range(4):
        coarse_ref[n] = (sums[:, n * LANES : (n + 1) * LANES] * mask_ref[n : n + 1, :]).astype(
            BF16
        )
    wide = jnp.concatenate([grads[n * chan : (n + 1) * chan, :] for n in range(4)], axis=1)
    raw = lax.dot_general(wide, stack[...], NT, preferred_element_type=F32)
    for n in range(4):
        raw_ref[n * chan : (n + 1) * chan, :] = raw[:, n * LANES : (n + 1) * LANES]


def hidden_grad_kernel(
    in_chan, sides_ref, stats_ref, sums_ref, params_ref, hidden, hidden_ring_ref, pre,
    pre_ring_ref, acts_ref, stack_ref, raw_ref, front, rear, swap_ref, small_ref, out_ref,
    stats, hidden_ring, pre_ring, acts, stack, raw, acc, sems,
):
    chan = hidden.shape[0] // 16
    place = sides_ref[2]
    got_stats = started(stats_ref, stats, sems.at[0])
    got_acts = started(acts_ref, acts, sems.at[1])
    got = []
    for n, (source, target) in enumerate(
        ((hidden_ring_ref, hidden_ring), (pre_ring_ref, pre_ring))
    ):
        cuts = [n * chan for n in range(0, target.shape[0] // chan + 1, 4)]
        got.append(started_rows(source, target, cuts, sems.at[pl.ds(4 + 5 * n, len(cuts) - 1)]))
    got = list(zip(*got))
    got_stack = started(
        stack_ref.at[pl.ds(stack.shape[0] // 6, stack.shape[0]), :], stack, sems.at[2]
    )
    got_raw = started(raw_ref, raw, sems.at[3])
    raw_shift = jnp.sum(sums_ref[:, 0, :], axis=0, keepdims=True)
    raw_gain = jnp.sum(sums_ref[:, 1, :], axis=0, keepdims=True)
    got_stats.wait()
    count, average, inverse = merged_stats(stats)
    scale = lax.rsqrt(count)
    small_ref[...] = jnp.concatenate(
        [raw_shift * scale, raw_gain * scale, scale, jnp.zeros((5, LANES), F32)], axis=0
    )
    columns = [average, inverse, raw_shift / count, raw_gain / count, params_ref[0:1, :]]
    average, inverse, mean_shift, mean_gain, gain = [
        jnp.broadcast_to(column, (chan, LANES)) for column in to_columns(columns, chan)
    ]
    weight = gain * inverse
    got_acts.wait()
    for n, (p, q) in enumerate(OWN + RING):
        if n % 4 == 0 and n >= 16:
            for copy in got[n // 4 - 4]:
                copy.wait()
        held_hidden, held_pre = (hidden, pre) if n < 16 else (hidden_ring, pre_ring)
        own = slice(n * chan, (n + 1) * chan) if n < 16 else slice((n - 16) * chan, (n - 15) * chan)
        to = slice((p * 6 + q) * chan, (p * 6 + q + 1) * chan)
        tiles = []
        for half, held in enumerate((front, rear)):
            lanes = slice(half * LANES, (half + 1) * LANES)
            act = acts[p * 6 + q : p * 6 + q + 1, lanes]
            normed = (held_hidden[own, lanes] - average) * inverse
            grad = held_pre[own, lanes] - (mean_shift + normed * mean_gain)
            tiles.append(((act * weight) * grad).astype(BF16))
            held[to, :] = tiles[-1]
        swap_ref[to, :] = jnp.where(place == 0, tiles[1], tiles[0])
    got_stack.wait()
    got_raw.wait()
    rows = stack.shape[0] // 6
    band = rows // 3
    for p in range(4):
        own = slice(((p + 1) * 6 + 1) * chan, ((p + 1) * 6 + 5) * chan)
        grads = jnp.concatenate([front[own, :], rear[own, :]], axis=1)
        for dx in range(3):
            first = (p + dx) * rows
            part = lax.dot_general(
                stack[first : first + rows, :], grads, NT, preferred_element_type=F32
            )
            if p == 0:
                acc[dx] = part
            else:
                acc[dx] += part
    low = lax.broadcasted_iota(jnp.int32, (in_chan, LANES), 1) < chan
    for dx in range(3):
        for dy in range(3):
            for dz in range(3):
                blocks = []
                for q in range(4):
                    row = dz * band + (q + 1 + dy) * in_chan
                    lanes = slice((q // 2) * LANES, (q // 2 + 1) * LANES)
                    blocks.append(acc[dx, row : row + in_chan, lanes])
                both = jnp.where(low, blocks[0] + blocks[2], blocks[1] + blocks[3])
                folded = (both + pltpu.roll(both, chan, 1)).astype(out_ref.dtype)
                tap = (dx * 3 + dy) * 3 + dz
                if tap < 16:
                    out_ref[tap * in_chan : (tap + 1) * in_chan, :chan] = folded[:, :chan]
                else:
                    to = (tap - 16) * in_chan
                    out_ref[to : to + in_chan, chan:] = folded[:, chan:]
    out_ref[11 * in_chan : 16 * in_chan, chan:] = jnp.zeros(
        (5 * in_chan, LANES - chan), out_ref.dtype
    )
    tail = 16 * in_chan
    out_ref[tail : tail + 4 * chan, :] = raw[...].astype(out_ref.dtype)
    left = out_ref.shape[0] - tail - 4 * chan
    if left:
        out_ref[tail + 4 * chan :, :] = jnp.zeros((left, LANES), out_ref.dtype)


def point_grad_kernel(
    only_two, halves, chan, sides_ref, front, rear, before_ref, after_ref, bands_ref, act_ref,
    tags_ref, out_ref, bands, acts, tags_held, stack, cells, sems,
):
    rows = front.shape[0] // 6
    groups, depth = acts.shape
    place_z = sides_ref[2]
    late = [
        started(bands_ref, bands, sems.at[0]),
        started(act_ref, acts, sems.at[1]),
        started(tags_ref, tags_held, sems.at[2]),
    ]
    for x in range(6):
        own = slice(x * rows, (x + 1) * rows)
        low, high = front[own, :], rear[own, :]
        before, after = before_ref[own, :], after_ref[own, :]
        if only_two:
            before, after = keep(before, place_z != 0), keep(after, place_z == 0)
        for n, step in enumerate((1, 0, -1)):
            tiles = (low, high) if step == 0 else shifted(low, high, before, after, step)
            to = slice((x * 3 + n) * rows, (x * 3 + n + 1) * rows)
            stack[to, :LANES] = tiles[0]
            stack[to, LANES:] = tiles[1]
    for copy in late:
        copy.wait()
    for p in range(4):
        first = p * 3 * rows
        grid = jnp.dot(
            bands[...], stack[first : first + 9 * rows, :], preferred_element_type=F32
        )
        for q in range(4):
            k = p * 4 + q
            cells[k * chan : (k + 1) * chan, :] = (
                grid[q * chan : (q + 1) * chan] * acts[k : k + 1, :]
            ).astype(BF16)

    def from_cells(d):
        tags = tags_held[d].astype(F32)
        hot = jnp.concatenate(
            [hot_rows(tags[halves + h : halves + h + 1, :], 0, depth) for h in range(halves)], axis=1
        )
        found = jnp.dot(cells[...], hot, preferred_element_type=F32)
        for h in range(halves):
            group = jnp.broadcast_to(tags[h : h + 1, :], (chan, LANES))
            lanes = slice(h * LANES, (h + 1) * LANES)
            out = jnp.zeros((chan, LANES), F32)
            for k in range(groups):
                out = jnp.where(group == k, found[k * chan : (k + 1) * chan, lanes], out)
            out_ref[d, h * chan : (h + 1) * chan, :] = out.astype(BF16)

    together = 16

    def step(s, carry):
        for j in range(together):
            from_cells(together * s + j)
        return carry

    lax.fori_loop(0, tags_held.shape[0] // together, step, 0)


def piece_kernel(parts_ref, points_ref, out_ref):
    rows = points_ref.shape[1]
    piece = jnp.sum(parts_ref[...].astype(F32), axis=0).astype(BF16)
    for d in range(out_ref.shape[0]):
        out_ref[d, :rows, :] = points_ref[d]
        out_ref[d, rows:, :] = piece


def sum_kernel(parts_ref, out_ref):
    piece = jnp.sum(parts_ref[...].astype(F32), axis=0).astype(BF16)
    for d in range(out_ref.shape[0]):
        out_ref[d] = piece


def weights_out(rows, small_ref, in_chan, sub_ref, down_ref):
    chan = down_ref.shape[0]
    scale = small_ref[2:3, 0:1]
    for n in range(4):
        turned = rows(n).T * scale
        sub_ref[:, n * LANES : (n + 1) * LANES] = turned[:chan]
        left = sub_ref.shape[1] - 16 * in_chan - n * LANES
        if left > 0:
            width = min(left, LANES)
            first = 16 * in_chan + n * LANES
            sub_ref[:, first : first + width] = turned[chan:, :width]
    for n in range(2):
        both = rows(4 + n) * scale
        down_ref[:, 2 * n * LANES : (2 * n + 1) * LANES] = both[:chan]
        down_ref[:, (2 * n + 1) * LANES : (2 * n + 2) * LANES] = both[chan:]


def last_kernel(halves, chan, got_ref, small_ref, points_ref, sub_ref, down_ref, flat):
    devices = got_ref.shape[0]
    piece = got_ref.shape[1] - halves * chan
    for d in range(devices):
        block = got_ref[d]
        for h in range(halves):
            first = (d * halves + h) * LANES
            points_ref[:, first : first + LANES] = block[h * chan : (h + 1) * chan, :]
        flat[d * piece : (d + 1) * piece, :] = block[halves * chan :, :].astype(F32)
    weights_out(lambda n: flat[n * LANES : (n + 1) * LANES, :], small_ref, chan, sub_ref, down_ref)


def weights_kernel(chan, got_ref, small_ref, sub_ref, down_ref, flat):
    piece = got_ref.shape[1]
    for d in range(got_ref.shape[0]):
        flat[d * piece : (d + 1) * piece, :] = got_ref[d].astype(F32)
    weights_out(lambda n: flat[n * LANES : (n + 1) * LANES, :], small_ref, chan, sub_ref, down_ref)


def on_device(
    point_feats, voxel_ids, send_counts, active, w_sub, w_down, bn_gain, bn_shift, cotangent
):
    in_chan, slot_total = point_feats.shape
    devices = send_counts.shape[1]
    slot_cap = slot_total // devices
    size_x, size_y, size_z = active.shape
    groups = size_x * size_y
    out_chan = w_sub.shape[0]
    only_two = lax.axis_size("gz") == 2
    sides = jnp.stack(
        [lax.axis_index("gx") % 2, lax.axis_index("gy") % 2, lax.axis_index("gz")]
    ).astype(jnp.int32)
    aligned = slot_cap % LANES == 0
    halves = slot_cap // LANES if aligned else 1
    rows_x, rows_6, rows_64 = groups // 2 * in_chan, 36 * out_chan, 64 * in_chan
    wide, back_wide = 6 * out_chan, 4 * in_chan

    if aligned:
        payload = local_call(
            functools.partial(pack_kernel, halves, groups, size_z),
            [((devices, halves * in_chan + 8, LANES), BF16)],
            send_counts, point_feats, voxel_ids.reshape(-1, LANES),
            scratch=[((in_chan, slot_total), BF16), ((devices * halves, LANES), jnp.int32)],
            scalars=[((1, devices), jnp.int32)],
            hbm=(0, 1, 2), copies=6, moved=2e6,
        )[0]
        recv = everyone(payload)
    else:
        payload = pack_plain(point_feats, voxel_ids, send_counts, groups, size_z)
        together = LANES // slot_cap
        recv = everyone(payload)
        recv = recv.reshape(devices // together, together, in_chan + 8, slot_cap)
        recv = recv.transpose(0, 2, 1, 3).reshape(devices // together, in_chan + 8, LANES)
    chunks = recv.shape[0]

    acts = active.reshape(groups, size_z).astype(F32)
    params = jnp.pad(jnp.stack([bn_gain, bn_shift]), ((0, 6), (0, LANES - out_chan)))
    front, back = band_inputs(w_sub, in_chan)
    cot = cotangent.transpose(1, 2, 0, 3)
    *ends, grad_c, coarse_mask = local_call(
        coarse_kernel,
        [((2 * out_chan + 16, LANES), BF16)] * 2
        + [((4 * out_chan, LANES), BF16), ((8, LANES), F32)],
        sides, acts, cot, smem=(0,), moved=2e5,
    )
    cot_x = swaps(*ends, "gx")
    ends = local_call(
        coarse_rows_kernel,
        [((4 * out_chan + 16, LANES), BF16)] * 2,
        sides, acts, grad_c, *cot_x, smem=(0,), moved=2e5,
    )
    cot_y = swaps(*ends, "gy")
    by_child = (
        w_down.reshape(out_chan, 4, 2, out_chan)
        .transpose(1, 3, 2, 0)
        .reshape(4 * out_chan, 2 * out_chan)
    )
    recv, acts, grad_c, cot_x, cot_y, by_child, front, back, params = lax.optimization_barrier(
        (recv, acts, grad_c, cot_x, cot_y, by_child, front, back, params)
    )

    *mine, tags = local_call(
        functools.partial(scatter_kernel, halves, in_chan, size_y),
        [((rows_x, size_z), BF16)] * 2 + [((chunks, 8, LANES), BF16)],
        sides, recv, acts,
        scratch=[
            ((groups * in_chan, chunks * halves * LANES), BF16),
            ((size_z, chunks * halves * LANES), BF16),
            ((chunks, 8, LANES), BF16),
        ],
        smem=(0,), hbm_outs=(2,), copies=1, moved=2e7,
    )
    got_x = swaps(*mine, "gx")
    own, ring = ((16 * out_chan, size_z), F32), ((20 * out_chan, size_z), F32)
    acts_wide, *fine_grad = local_call(
        fine_grad_kernel,
        [((40, size_z), F32), own, ring],
        sides, acts, grad_c, *cot_x, *cot_y, by_child,
        scratch=[
            ((40, size_z), F32),
            ((16 * out_chan, LANES), BF16),
            ((16 * out_chan, 2 * size_z), BF16),
            ring,
        ],
        smem=(0,), hbm_outs=(0, 2), copies=2, moved=4e6,
    )
    got_x, acts_wide, fine_grad = lax.optimization_barrier((got_x, acts_wide, fine_grad))
    ends = local_call(
        rows_kernel,
        [((2 * rows_x, size_z), BF16)] * 2,
        sides, *mine, *got_x, smem=(0,), moved=1e6,
    )
    got_y = swaps(*ends, "gy")
    bands_shape, back_shape = (wide, 9 * 8 * in_chan), (back_wide, 9 * 6 * out_chan)
    own_bands_shape = (4 * out_chan, bands_shape[1])
    bands, back_bands, own_bands = local_call(
        bands_kernel,
        [(bands_shape, BF16), (back_shape, BF16), (own_bands_shape, BF16)],
        front, back,
        scratch=[(bands_shape, BF16), (back_shape, BF16)],
        hbm_outs=(0, 1), copies=2, moved=4e6,
    )
    got_y, bands, back_bands, own_bands = lax.optimization_barrier(
        (got_y, bands, back_bands, own_bands)
    )
    tile_low, tile_high, swap = local_call(
        functools.partial(columns_kernel, in_chan),
        [((rows_64, LANES), BF16)] * 3,
        sides, *mine, *got_x, *got_y, smem=(0,), moved=3e6,
    )
    before, after = z_exchange(tile_low, tile_high, swap)
    stack_shape = (3 * rows_64, size_z)
    stack = local_call(stack_kernel, [(stack_shape, BF16)], tile_low, tile_high, moved=4e6)[0]
    before, after, stack = lax.optimization_barrier((before, after, stack))

    stats_shape = (devices, 8, LANES)
    own_hidden, stack, stats, _ = local_call(
        functools.partial(conv_kernel, only_two),
        [own, (stack_shape, BF16), (stats_shape, F32), (stack_shape, BF16)],
        sides, stack, before, after, own_bands, acts_wide,
        aliases={1: 3}, smem=(0,), hbm_outs=(1,), copies=8, moved=1e7,
    )
    stats_in = everyone(stats)
    ring_hidden = local_call(
        conv_ring_kernel,
        [ring],
        bands, acts_wide, stack,
        scratch=[(bands_shape, BF16), ((40, size_z), F32), (stack_shape, BF16), ring],
        hbm=(0, 1, 2), hbm_outs=(0,), copies=4, moved=1e7,
    )[0]
    stats_in, ring_hidden = lax.optimization_barrier((stats_in, ring_hidden))
    held = [(stats_shape, F32)]
    own_pre, fine_out, sums = local_call(
        functools.partial(norm_kernel, OWN),
        [own, ((groups * out_chan, size_z), BF16), (stats_shape, F32)],
        stats_in, params, own_hidden, fine_grad[0], acts_wide,
        scratch=held
        + [((40, size_z), F32), ((groups * out_chan, size_z), BF16), (stats_shape, F32)],
        hbm=(4,), hbm_outs=(1, 2), copies=4, moved=5e6,
    )
    sums_in = everyone(sums)
    ring_pre, coarse, raw_down = local_call(
        functools.partial(norm_kernel, RING),
        [ring, ((4, out_chan, LANES), BF16), ((4 * out_chan, LANES), F32)],
        stats_in, params, ring_hidden, fine_grad[1], acts_wide, fine_out, grad_c, coarse_mask, w_down,
        scratch=held
        + [
            ring,
            ring,
            ((40, size_z), F32),
            ring,
            ((groups * out_chan, size_z), BF16),
            ((4 * out_chan, LANES), BF16),
            ((8 * out_chan, 4 * LANES), BF16),
            ((4 * out_chan, LANES), F32),
        ],
        hbm=(0, 2, 3, 4, 5, 6), hbm_outs=(0, 2), copies=16, moved=5e6,
    )
    sums_in, ring_pre, raw_down = lax.optimization_barrier((sums_in, ring_pre, raw_down))
    half_x, half_y, half_z = size_x // 2, size_y // 2, size_z // 2
    coarse_out = coarse.reshape(half_x, half_y, out_chan, half_z).transpose(2, 0, 1, 3)

    piece = -(-(16 * in_chan + 4 * out_chan) // devices)
    piece = -(-piece // 8) * 8
    grad_low, grad_high, grad_swap, small, parts = local_call(
        functools.partial(hidden_grad_kernel, in_chan),
        [((rows_6, LANES), BF16)] * 3 + [((8, LANES), F32), ((devices * piece, LANES), BF16)],
        sides, stats_in, sums_in, params, own_hidden, ring_hidden, own_pre, ring_pre, acts_wide,
        stack, raw_down,
        scratch=[
            (stats_shape, F32),
            ring,
            ring,
            ((40, size_z), F32),
            ((rows_64 // 8 * 6 * 3, size_z), BF16),
            ((4 * out_chan, LANES), F32),
            ((3, 24 * in_chan, 4 * out_chan), F32),
        ],
        smem=(0,), hbm=(1, 5, 7, 8, 9, 10), copies=24, moved=2e7,
    )
    grad_before, grad_after = z_exchange(grad_low, grad_high, grad_swap)
    parts = everyone(parts.reshape(devices, piece, LANES))

    points = local_call(
        functools.partial(point_grad_kernel, only_two, halves, in_chan),
        [((chunks, halves * in_chan, LANES), BF16)],
        sides, grad_low, grad_high, grad_before, grad_after, back_bands, acts, tags,
        scratch=[
            (back_shape, BF16),
            ((groups, size_z), F32),
            ((chunks, 8, LANES), BF16),
            ((3 * rows_6, size_z), BF16),
            ((groups * in_chan, size_z), BF16),
        ],
        smem=(0,), hbm=(5, 6, 7), copies=3, moved=2e7,
    )[0]
    parts, points = lax.optimization_barrier((parts, points))
    shapes = [((out_chan, 27 * in_chan), F32), ((out_chan, 8 * out_chan), F32)]
    flat = [((devices * piece, LANES), F32)]
    if aligned:
        both = local_call(
            piece_kernel,
            [((devices, halves * in_chan + piece, LANES), BF16)],
            parts, points, moved=2e6,
        )[0]
        returned, raw_sub, raw_down = local_call(
            functools.partial(last_kernel, halves, in_chan),
            [((in_chan, slot_total), BF16)] + shapes,
            everyone(both), small, scratch=flat, moved=2e6,
        )
    else:
        points = points.reshape(chunks, in_chan, together, slot_cap).transpose(0, 2, 1, 3)
        returned = everyone(points.reshape(devices, in_chan, slot_cap))
        returned = returned.transpose(1, 0, 2).reshape(in_chan, slot_total)
        whole = local_call(sum_kernel, [((devices, piece, LANES), BF16)], parts)[0]
        raw_sub, raw_down = local_call(
            functools.partial(weights_kernel, in_chan), shapes, everyone(whole), small, scratch=flat
        )
    return (
        coarse_out,
        returned,
        raw_sub,
        raw_down,
        small[1, :out_chan],
        small[0, :out_chan],
    )


def solution(mesh):
    in_specs = (
        P(None, AXES),
        P(AXES),
        P(AXES, None),
        P("gx", "gy", "gz"),
        P(),
        P(),
        P(),
        P(),
        P(None, "gx", "gy", "gz"),
    )
    out_specs = (P(None, "gx", "gy", "gz"), P(None, AXES), P(), P(), P(), P())
    return jax.shard_map(
        on_device, mesh=mesh, in_specs=in_specs, out_specs=out_specs, check_vma=False
    )
```

```python
import functools
import math

import jax
import jax.numpy as jnp
from jax import lax
from jax.experimental import pallas as pl
from jax.experimental.pallas import tpu as pltpu
from jax.sharding import PartitionSpec as P

EPS = 1e-05
AXES = ("gx", "gy", "gz")
LANES = 128
GELU_SCALE = 0.7978845608028654
GELU_CUBE = 0.044715
F32 = jnp.float32
BF16 = jnp.bfloat16
NT = (((1,), (1,)), ((), ()))


def local_call(
    kernel, outs, *args, scratch=(), scalars=(), smem=(), hbm=(), hbm_outs=(), copies=0, moved=0, aliases=None
):
    held = sum(math.prod(shape) * jnp.dtype(kind).itemsize for shape, kind in scratch)
    limit = held // 2**20 + 6
    vmem = pl.BlockSpec(memory_space=pltpu.VMEM)
    scalar = pl.BlockSpec(memory_space=pltpu.SMEM)
    far = pl.BlockSpec(memory_space=pltpu.HBM)
    args = [
        pltpu.with_memory_space_constraint(arg, pltpu.HBM) if i in hbm else arg
        for i, arg in enumerate(args)
    ]
    held = [pltpu.VMEM(shape, kind) for shape, kind in scratch]
    held += [pltpu.SMEM(shape, kind) for shape, kind in scalars]
    if copies:
        held.append(pltpu.SemaphoreType.DMA((copies,)))
    return pl.pallas_call(
        kernel,
        out_shape=[
            pltpu.HBM(shape, kind) if i in hbm_outs else jax.ShapeDtypeStruct(shape, kind)
            for i, (shape, kind) in enumerate(outs)
        ],
        in_specs=[
            scalar if i in smem else far if i in hbm else vmem for i in range(len(args))
        ],
        out_specs=[far if i in hbm_outs else vmem for i in range(len(outs))],
        scratch_shapes=held,
        input_output_aliases=aliases or {},
        compiler_params=pltpu.CompilerParams(vmem_limit_bytes=limit * 1024 * 1024),
        cost_estimate=pl.CostEstimate(flops=0, bytes_accessed=int(moved), transcendentals=0),
    )(*args)


def started(source, target, semaphore):
    copy = pltpu.make_async_copy(source, target, semaphore)
    copy.start()
    return copy


def rows_of(n, count):
    return pl.ds(n * count, count)


def started_rows(source, target, cuts, semaphores):
    copies = []
    for n, (begin, end) in enumerate(zip(cuts, cuts[1:])):
        own = pl.ds(begin, end - begin)
        copies.append(started(source.at[own, :], target.at[own, :], semaphores.at[n]))
    return copies


OWN = [(p, q) for p in range(1, 5) for q in range(1, 5)]
RING = [(p, q) for p in range(6) for q in range(6) if (p, q) not in OWN]


def neighbours(axis, step):
    count = lax.axis_size(axis)
    return [(i, i + step) for i in range(count) if 0 <= i + step < count]


def swaps(first, second, axis):
    count = lax.axis_size(axis)
    got = []
    for block, begin in ((first, 0), (second, 1)):
        pairs = [(i, i + 1) for i in range(begin, count - 1, 2)]
        got.append(lax.ppermute(block, axis, pairs + [(j, i) for i, j in pairs]))
    return got


def sided(odd, first, second):
    return jnp.where(odd, first, second), jnp.where(odd, second, first)


def z_exchange(low, high, swap):
    if lax.axis_size("gz") != 2:
        return (
            lax.ppermute(high, "gz", neighbours("gz", 1)),
            lax.ppermute(low, "gz", neighbours("gz", -1)),
        )
    got = lax.ppermute(swap, "gz", [(0, 1), (1, 0)])
    return got, got


def everyone(block):
    return lax.all_to_all(block, AXES, split_axis=0, concat_axis=0, tiled=True)


def pack_kernel(
    halves, groups, depth, counts_ref, feats_ref, ids_ref, out_ref, feats, ids, counts, sems
):
    devices = out_ref.shape[0]
    chan = feats_ref.shape[0]
    parts = 4
    width = feats.shape[1] // parts
    got_ids = started(ids_ref, ids, sems.at[parts])
    got_counts = started(counts_ref, counts, sems.at[parts + 1])
    got = []
    for n in range(parts):
        lanes = pl.ds(n * width, width)
        got.append(started(feats_ref.at[:, lanes], feats.at[:, lanes], sems.at[n]))
    got_ids.wait()
    got_counts.wait()
    rank = lax.broadcasted_iota(jnp.int32, (halves, LANES), 0) * LANES + lax.broadcasted_iota(
        jnp.int32, (halves, LANES), 1
    )
    blank = jnp.zeros((8 - 2 * halves, LANES), F32)
    for d in range(devices):
        those = ids[d * halves : (d + 1) * halves, :]
        usable = rank < counts[0, d]
        group = jnp.where(usable, those // depth, groups).astype(F32)
        place = (those % depth).astype(F32)
        tags = jnp.concatenate([group, place, blank], axis=0)
        out_ref[d, halves * chan :, :] = tags.astype(BF16)
    for d in range(devices):
        if d * parts % devices == 0:
            got[d * parts // devices].wait()
        for h in range(halves):
            first = (d * halves + h) * LANES
            out_ref[d, h * chan : (h + 1) * chan, :] = feats[:, first : first + LANES]


def pack_plain(feats, ids, counts, groups, depth):
    chan, total = feats.shape
    devices = counts.shape[1]
    cap = total // devices
    ids = ids.reshape(devices, 1, cap)
    rank = jnp.arange(cap, dtype=jnp.int32)[None, None, :]
    group = jnp.where(rank < counts.reshape(devices, 1, 1), ids // depth, groups)
    tags = jnp.concatenate([group, ids % depth], axis=1).astype(BF16)
    rows = feats.reshape(chan, devices, cap).transpose(1, 0, 2)
    return jnp.concatenate([rows, jnp.pad(tags, ((0, 0), (0, 6), (0, 0)))], axis=1)


def hot_rows(row, first, count):
    index = lax.broadcasted_iota(jnp.int32, (count, LANES), 0).astype(F32).astype(BF16)
    row = jnp.broadcast_to(row, (count, LANES)).astype(BF16)
    return jnp.where(index + jnp.asarray(first, BF16) == row, jnp.ones_like(row), jnp.zeros_like(row))


def scatter_kernel(
    halves, chan, size_y, sides_ref, recv_ref, act_ref, first_ref, second_ref, tags_ref,
    masked, hot, tags_held, sems,
):
    chunks = recv_ref.shape[0]
    groups, depth = act_ref.shape
    for d in range(chunks):
        tags_held[d] = recv_ref[d][halves * chan :, :].astype(F32)
    kept = started(tags_held, tags_ref, sems.at[0])
    for d in range(chunks):
        block = recv_ref[d]
        tags = tags_held[d]
        for h in range(halves):
            feats = block[h * chan : (h + 1) * chan, :]
            lanes = slice((d * halves + h) * LANES, (d * halves + h + 1) * LANES)
            group = jnp.broadcast_to(tags[h : h + 1, :], (chan, LANES)).astype(BF16)
            for k in range(groups):
                masked[k * chan : (k + 1) * chan, lanes] = jnp.where(
                    group == k, feats, jnp.zeros_like(feats)
                )
            for row in range(0, depth, 32):
                hot[row : row + 32, lanes] = hot_rows(
                    tags[halves + h : halves + h + 1, :], row, 32
                )
    acc = lax.dot_general(masked[...], hot[...], NT, preferred_element_type=F32)
    odd = sides_ref[0] != 0
    half = size_y // 2
    for k in range(groups // 2):
        p, q = k // size_y, k % size_y
        row = ((q // half) * 4 + p * 2 + q % half) * chan
        blocks = []
        for n in (k, k + groups // 2):
            block = acc[n * chan : (n + 1) * chan, :] * act_ref[n : n + 1, :]
            blocks.append(block.astype(BF16))
        first_ref[row : row + chan, :], second_ref[row : row + chan, :] = sided(odd, *blocks)
    kept.wait()


def coarse_kernel(sides_ref, act_ref, cot_ref, first_ref, second_ref, grad_ref, mask_ref):
    depth = act_ref.shape[1]
    chan = cot_ref.shape[2]
    odd = sides_ref[0] != 0
    fine = lax.broadcasted_iota(jnp.int32, (depth, LANES), 0) // 2
    pair = (fine == lax.broadcasted_iota(jnp.int32, (depth, LANES), 1)).astype(BF16)
    acts = act_ref[...]
    sums = jnp.dot(acts.astype(BF16), pair, preferred_element_type=F32)
    masks, grads = [], []
    for x in range(2):
        for y in range(2):
            rows = [sums[(2 * x + a) * 4 + 2 * y + b] for a in range(2) for b in range(2)]
            any_row = (rows[0] + rows[1] + rows[2] + rows[3])[None, :]
            mask = jnp.where(any_row > 0.5, 1.0, 0.0)
            masks.append(mask)
            grads.append((cot_ref[x, y].astype(F32) * mask).astype(BF16))
    for n, grad in enumerate(grads):
        grad_ref[n * chan : (n + 1) * chan, :] = grad
    for y in range(2):
        own = slice(y * chan, (y + 1) * chan)
        first_ref[own, :], second_ref[own, :] = sided(odd, grads[y], grads[2 + y])
    mask_ref[...] = jnp.concatenate(masks + [jnp.zeros((4, LANES), F32)], axis=0)
    blank = jnp.zeros((8, LANES), F32)
    tails = []
    for p in (0, 3):
        rows = acts[4 * p : 4 * p + 4]
        tails.append(jnp.concatenate([rows[:, :LANES], rows[:, LANES:], blank], axis=0))
    tails = sided(odd, *tails)
    for out_ref, tail in zip((first_ref, second_ref), tails):
        out_ref[2 * chan :, :] = tail.astype(BF16)


def coarse_rows_kernel(sides_ref, act_ref, grad_ref, xf_ref, xs_ref, first_ref, second_ref):
    chan = grad_ref.shape[0] // 4
    odd_x, odd_y = sides_ref[0] != 0, sides_ref[1] != 0
    before, after = sided(odd_x, xf_ref[...], xs_ref[...])
    acts = act_ref[...]
    before_acts = before[2 * chan :, :].astype(F32)
    after_acts = after[2 * chan :, :].astype(F32)
    ends = []
    for y, q in ((0, 0), (1, 3)):
        own = slice(y * chan, (y + 1) * chan)
        columns = [before[own], grad_ref[own, :]]
        columns += [grad_ref[(2 + y) * chan : (3 + y) * chan, :], after[own]]
        rows = [before_acts[q : q + 1], before_acts[4 + q : 5 + q]]
        for p in range(4):
            row = acts[4 * p + q : 4 * p + q + 1]
            rows += [row[:, :LANES], row[:, LANES:]]
        rows += [after_acts[q : q + 1], after_acts[4 + q : 5 + q], jnp.zeros((4, LANES), F32)]
        ends.append(columns + [jnp.concatenate(rows, axis=0).astype(BF16)])
    row = 0
    for low, high in zip(*ends):
        own = slice(row, row + low.shape[0])
        first_ref[own, :], second_ref[own, :] = sided(odd_y, low, high)
        row += low.shape[0]


def fine_grad_kernel(
    sides_ref, act_ref, grad_ref, xf_ref, xs_ref, yf_ref, ys_ref, down_ref, acts_ref, own, ring_ref,
    acts_held, wide, up, ring, sems,
):
    chan = grad_ref.shape[0] // 4
    depth = act_ref.shape[1]
    acts = act_ref[...]
    x_ends = sided(sides_ref[0] != 0, xf_ref[...], xs_ref[...])
    y_ends = sided(sides_ref[1] != 0, yf_ref[...], ys_ref[...])
    xb, xa = [end[2 * chan :, :].astype(F32) for end in x_ends]
    yb, ya = [end[4 * chan :, :].astype(F32) for end in y_ends]
    rows = []
    for p in range(6):
        rows.append(jnp.concatenate([yb[2 * p : 2 * p + 1], yb[2 * p + 1 : 2 * p + 2]], axis=1))
        for q in range(4):
            if p in (0, 5):
                got = xb if p == 0 else xa
                rows.append(jnp.concatenate([got[q : q + 1], got[4 + q : 5 + q]], axis=1))
            else:
                rows.append(acts[4 * (p - 1) + q : 4 * (p - 1) + q + 1])
        rows.append(jnp.concatenate([ya[2 * p : 2 * p + 1], ya[2 * p + 1 : 2 * p + 2]], axis=1))
    rows.append(jnp.zeros((4, depth), F32))
    acts_held[...] = jnp.concatenate(rows, axis=0)
    kept = [started(acts_held, acts_ref, sems.at[0])]
    for x in range(4):
        for y in range(4):
            if y in (0, 3):
                block = y_ends[y // 3][x * chan : (x + 1) * chan, :]
            elif x in (0, 3):
                block = x_ends[x // 3][(y - 1) * chan : y * chan, :]
            else:
                first = ((x - 1) * 2 + y - 1) * chan
                block = grad_ref[first : first + chan, :]
            wide[(x * 4 + y) * chan : (x * 4 + y + 1) * chan, :] = block
    coarse_z = lax.broadcasted_iota(jnp.int32, (LANES, 2 * depth), 0)
    fine_z = lax.broadcasted_iota(jnp.int32, (LANES, 2 * depth), 1)
    child = jnp.where(fine_z < depth, 0, 1)
    spread = (2 * coarse_z + child == fine_z - child * depth).astype(BF16)
    up[...] = jnp.dot(wide[...], spread, preferred_element_type=F32).astype(BF16)
    for x in range(4):
        for y in range(4):
            those = slice((x * 4 + y) * chan, (x * 4 + y + 1) * chan)
            both = jnp.concatenate([up[those, :depth], up[those, depth:]], axis=0)
            grads = jnp.dot(down_ref[...], both, preferred_element_type=F32)
            for a in range(2):
                for b in range(2):
                    column = (2 * x + a - 1, 2 * y + b - 1)
                    block = grads[(a * 2 + b) * chan : (a * 2 + b + 1) * chan]
                    if column in OWN:
                        n = OWN.index(column)
                        own[n * chan : (n + 1) * chan, :] = block
                    elif column in RING:
                        n = RING.index(column)
                        ring[n * chan : (n + 1) * chan, :] = block
    kept.append(started(ring, ring_ref, sems.at[1]))
    for copy in kept:
        copy.wait()


def bands_kernel(
    front_ref, back_ref, bands_ref, back_bands_ref, own_ref, bands, back_bands, sems
):
    rows, width = front_ref.shape[0], front_ref.shape[1] // 9
    back_rows, back_width = back_ref.shape[0], back_ref.shape[1] // 9
    for t in range(9):
        block = front_ref[:, t * width : (t + 1) * width].astype(F32)
        for q in range(6):
            moved = pltpu.roll(block, q * back_rows, 1) if q else block
            bands[q * rows : (q + 1) * rows, t * width : (t + 1) * width] = moved.astype(BF16)
    kept = [started(bands, bands_ref, sems.at[0])]
    own_ref[...] = bands[rows : 5 * rows, :]
    for t in range(9):
        block = back_ref[:, t * back_width : (t + 1) * back_width].astype(F32)
        for q in range(4):
            moved = pltpu.roll(block, q * rows, 1) if q else block
            back_bands[
                q * back_rows : (q + 1) * back_rows, t * back_width : (t + 1) * back_width
            ] = moved.astype(BF16)
    kept.append(started(back_bands, back_bands_ref, sems.at[1]))
    for copy in kept:
        copy.wait()


def band_inputs(w_sub, in_chan):
    out_chan = w_sub.shape[0]
    taps = w_sub.reshape(out_chan, 3, 3, 3, in_chan)
    front = taps.transpose(0, 1, 3, 2, 4).reshape(out_chan, 9, 3 * in_chan)
    front = jnp.pad(front, ((0, 0), (0, 0), (0, 5 * in_chan)))
    back = taps[:, ::-1, ::-1].transpose(4, 1, 3, 2, 0).reshape(in_chan, 9, 3 * out_chan)
    back = jnp.pad(back, ((0, 0), (0, 0), (0, 3 * out_chan)))
    return front.reshape(out_chan, -1), back.reshape(in_chan, -1)


def rows_kernel(sides_ref, first_ref, second_ref, gf_ref, gs_ref, out_first_ref, out_second_ref):
    odd_x, odd_y = sides_ref[0] != 0, sides_ref[1] != 0
    half = first_ref.shape[0] // 2
    low, high = sided(odd_x, first_ref[...], second_ref[...])
    below, above = sided(odd_x, gf_ref[...], gs_ref[...])
    for n, block in enumerate((below, low, high, above)):
        own = slice(n * half, (n + 1) * half)
        out_first_ref[own, :], out_second_ref[own, :] = sided(odd_y, block[:half], block[half:])


def columns_kernel(
    chan, sides_ref, first_ref, second_ref, gf_ref, gs_ref, yf_ref, ys_ref, front_ref, rear_ref, swap_ref
):
    odd_x, odd_y, place = sides_ref[0] != 0, sides_ref[1] != 0, sides_ref[2]
    low, high = sided(odd_x, first_ref[...], second_ref[...])
    below, above = sided(odd_x, gf_ref[...], gs_ref[...])
    left, right = sided(odd_y, yf_ref[...], ys_ref[...])
    for n, own in enumerate((below, low, high, above)):
        for p in range(2):
            for y in range(8):
                if y in (0, 1, 6, 7):
                    got = left if y < 2 else right
                    row = (n * 4 + p * 2 + y % 2) * chan
                else:
                    got = own
                    row = (((y - 2) // 2) * 4 + p * 2 + y % 2) * chan
                block = got[row : row + chan]
                to = ((n * 2 + p) * 8 + y) * chan
                front_ref[to : to + chan, :] = block[:, :LANES]
                rear_ref[to : to + chan, :] = block[:, LANES:]
                swap_ref[to : to + chan, :] = jnp.where(
                    place == 0, block[:, LANES:], block[:, :LANES]
                )


def shifted(low, high, before, after, step):
    lane = lax.broadcasted_iota(jnp.int32, low.shape, 1)
    if step > 0:
        turned = [pltpu.roll(tile.astype(F32), LANES - 1, 1) for tile in (low, high, after)]
        edge = lane == LANES - 1
        tiles = [jnp.where(edge, turned[1], turned[0]), jnp.where(edge, turned[2], turned[1])]
    else:
        turned = [pltpu.roll(tile.astype(F32), 1, 1) for tile in (before, low, high)]
        edge = lane == 0
        tiles = [jnp.where(edge, turned[0], turned[1]), jnp.where(edge, turned[1], turned[2])]
    return tiles[0].astype(BF16), tiles[1].astype(BF16)


def keep(tile, wanted):
    return jnp.where(wanted, tile, jnp.zeros_like(tile))


def to_rows(columns):
    lane = lax.broadcasted_iota(jnp.int32, (LANES, LANES), 1)
    wide = jnp.zeros((LANES, LANES), F32)
    for n, column in enumerate(columns):
        tall = jnp.concatenate([column, jnp.zeros((LANES - column.shape[0], 1), F32)], axis=0)
        wide = jnp.where(lane == n, tall, wide)
    return wide.T[:8, :]


def to_columns(rows, chan):
    wide = jnp.concatenate(rows + [jnp.zeros((LANES - len(rows), LANES), F32)], axis=0).T
    return [wide[:chan, n : n + 1] for n in range(len(rows))]


def stack_kernel(low_ref, high_ref, stack_ref):
    rows = low_ref.shape[0] // 8
    for x in range(8):
        own = slice(x * rows, (x + 1) * rows)
        low, high = low_ref[own, :], high_ref[own, :]
        for n, step in enumerate((-1, 0, 1)):
            tiles = (low, high) if step == 0 else shifted(low, high, high, low, step)
            to = slice((x * 3 + n) * rows, (x * 3 + n + 1) * rows)
            stack_ref[to, :LANES] = tiles[0]
            stack_ref[to, LANES:] = tiles[1]


def patch(stack, x, rows, before, after):
    lane = lax.broadcasted_iota(jnp.int32, before.shape, 1)
    to = slice(x * 3 * rows, (x * 3 + 1) * rows)
    edge = pltpu.roll(before.astype(F32), 1, 1)
    own = stack[to, :LANES].astype(F32)
    stack[to, :LANES] = jnp.where(lane == 0, edge, own).astype(BF16)
    to = slice((x * 3 + 2) * rows, (x * 3 + 3) * rows)
    edge = pltpu.roll(after.astype(F32), LANES - 1, 1)
    own = stack[to, LANES:].astype(F32)
    stack[to, LANES:] = jnp.where(lane == LANES - 1, edge, own).astype(BF16)


def conv_kernel(
    only_two, sides_ref, stack_in_ref, before_ref, after_ref, bands_ref, acts_ref,
    hidden, stack_ref, stats_ref, stack, sems,
):
    rows = before_ref.shape[0] // 8
    depth = acts_ref.shape[1]
    chan = bands_ref.shape[0] // 4
    place = sides_ref[2]
    kept = []
    total = jnp.zeros((chan, depth), F32)
    count = jnp.zeros((1, depth), F32)
    for x in range(8):
        own = slice(x * rows, (x + 1) * rows)
        before, after = before_ref[own, :], after_ref[own, :]
        if only_two:
            before, after = keep(before, place != 0), keep(after, place == 0)
        patch(stack, x, rows, before, after)
        own = rows_of(x, 3 * rows)
        kept.append(started(stack.at[own, :], stack_ref.at[own, :], sems.at[x]))
        p = x - 2
        if not 1 <= p <= 4:
            continue
        first = p * 3 * rows
        out = jnp.dot(
            bands_ref[...], stack[first : first + 9 * rows, :], preferred_element_type=F32
        )
        for q in range(1, 5):
            act = acts_ref[p * 6 + q : p * 6 + q + 1, :]
            block = out[(q - 1) * chan : q * chan] * act
            n = OWN.index((p, q))
            hidden[n * chan : (n + 1) * chan, :] = block
            total = total + block
            count = count + act
    count = jnp.sum(count, axis=1, keepdims=True)
    total = jnp.sum(total, axis=1, keepdims=True)
    mean = total / jnp.maximum(count, 1.0)
    squares = jnp.zeros((chan, depth), F32)
    for n, (p, q) in enumerate(OWN):
        act = acts_ref[p * 6 + q : p * 6 + q + 1, :]
        centred = (hidden[n * chan : (n + 1) * chan, :] - mean) * act
        squares = squares + centred * centred
    squares = jnp.sum(squares, axis=1, keepdims=True)
    packed = to_rows([total, squares, jnp.broadcast_to(count, (chan, 1))])
    for d in range(stats_ref.shape[0]):
        stats_ref[d] = packed
    for copy in kept:
        copy.wait()


def conv_ring_kernel(bands_ref, acts_ref, stack_ref, hidden_ref, bands, acts, stack, hidden, sems):
    rows = stack.shape[0] // 24
    wide = bands.shape[0]
    chan = wide // 6
    got = [
        started(acts_ref, acts, sems.at[0]),
        started(bands_ref, bands, sems.at[1]),
        started(stack_ref, stack, sems.at[2]),
    ]
    for copy in got:
        copy.wait()
    for p in range(6):
        taps = stack[p * 3 * rows : (p * 3 + 9) * rows, :]
        if p in (0, 5):
            out = jnp.dot(bands[...], taps, preferred_element_type=F32)
            columns = range(6)
        else:
            ends = jnp.concatenate([bands[:chan, :], bands[5 * chan :, :]], axis=0)
            out = jnp.dot(ends, taps, preferred_element_type=F32)
            columns = (0, 5)
        for i, q in enumerate(columns):
            n = RING.index((p, q))
            hidden[n * chan : (n + 1) * chan, :] = (
                out[i * chan : (i + 1) * chan] * acts[p * 6 + q : p * 6 + q + 1, :]
            )
    kept = started(hidden, hidden_ref, sems.at[3])
    kept.wait()


def merged_stats(stats_ref):
    totals, squares, counts = stats_ref[:, 0, :], stats_ref[:, 1, :], stats_ref[:, 2, :]
    count = jnp.sum(counts, axis=0, keepdims=True)
    average = jnp.sum(totals, axis=0, keepdims=True) / count
    off = totals / jnp.maximum(counts, 1.0) - average
    spread = jnp.sum(squares + counts * off * off, axis=0, keepdims=True)
    return count, average, lax.rsqrt(spread / count + EPS)


def norm_kernel(
    columns, stats_ref, params_ref, hidden, fine, acts_ref, *rest
):
    own = columns is OWN
    if own:
        pre, out_ref, sums_ref, stats, acts, outs, sums_held, sems = rest
    else:
        hidden_ref, fine_ref = hidden, fine
        (out_ref, grad_ref, mask_ref, down_ref, pre_ref, coarse_ref, raw_ref) = rest[:7]
        stats, hidden, fine, acts, pre, outs, grads, taps, raw, sems = rest[7:]
    chan = hidden.shape[0] // len(columns)
    depth = acts.shape[1]
    got_stats = started(stats_ref, stats, sems.at[0])
    got_acts = started(acts_ref, acts, sems.at[1])
    cuts = [n * chan for n in range(0, len(columns) + 1, 4)]
    parts = len(cuts) - 1
    if not own:
        got = started_rows(hidden_ref, hidden, cuts, sems.at[pl.ds(2, parts)])
        got_fine = started_rows(fine_ref, fine, cuts, sems.at[pl.ds(2 + parts, parts)])
        last = 2 + 2 * parts
        got_down = [
            started(out_ref, outs, sems.at[last + 1]),
            started(grad_ref, grads, sems.at[last + 2]),
        ]
    got_stats.wait()
    count, average, inverse = merged_stats(stats)
    full = (chan, LANES)
    average, inverse, gain, shift = [
        jnp.broadcast_to(column, full)
        for column in to_columns([average, inverse, params_ref[0:1, :], params_ref[1:2, :]], chan)
    ]
    sum_shift = jnp.zeros((chan, LANES), F32)
    sum_gain = jnp.zeros((chan, LANES), F32)
    got_acts.wait()
    for n, (p, q) in enumerate(columns):
        if n % 4 == 0 and not own:
            got[n // 4].wait()
            got_fine[n // 4].wait()
        own_rows = slice(n * chan, (n + 1) * chan)
        for half in range(depth // LANES):
            lanes = slice(half * LANES, (half + 1) * LANES)
            act = acts[p * 6 + q : p * 6 + q + 1, lanes]
            normed = (hidden[own_rows, lanes] - average) * inverse
            x = gain * normed + shift
            square = x * x
            bent = jnp.tanh(GELU_SCALE * (x + GELU_CUBE * (square * x)))
            cdf = 0.5 + 0.5 * bent
            slope = cdf + (0.5 * x) * (1.0 - bent * bent) * (
                GELU_SCALE + (3.0 * GELU_CUBE * GELU_SCALE) * square
            )
            grad = (act * slope) * fine[own_rows, lanes]
            pre[own_rows, lanes] = grad
            if own:
                sum_shift = sum_shift + grad
                sum_gain = sum_gain + grad * normed
                outs[own_rows, lanes] = (x * cdf * act).astype(BF16)
    if own:
        kept = [started(outs, out_ref, sems.at[2])]
        sums = to_rows(
            [jnp.sum(sum_shift, axis=1, keepdims=True), jnp.sum(sum_gain, axis=1, keepdims=True)]
        )
        for d in range(sums_ref.shape[0]):
            sums_held[d] = sums
        kept.append(started(sums_held, sums_ref, sems.at[3]))
    else:
        kept = [started(pre, pre_ref, sems.at[2 + 2 * parts])]
        for copy in got_down:
            copy.wait()
        down_conv(outs, grads, mask_ref, down_ref, coarse_ref, raw, taps)
        kept.append(started(raw, raw_ref, sems.at[last + 3]))
    for copy in kept:
        copy.wait()


def down_conv(outs, grads, mask_ref, down_ref, coarse_ref, raw_ref, stack):
    depth = outs.shape[1]
    chan = grads.shape[0] // 4
    source = lax.broadcasted_iota(jnp.int32, (depth, depth), 0)
    target = lax.broadcasted_iota(jnp.int32, (depth, depth), 1)
    wanted = jnp.where(target < LANES, 2 * target, 2 * (target - LANES) + 1)
    sort = (source == wanted).astype(BF16)
    parted = jnp.dot(outs[...], sort, preferred_element_type=F32).astype(BF16)
    for x in range(2):
        for y in range(2):
            for a in range(2):
                for b in range(2):
                    row = ((2 * x + a) * 4 + 2 * y + b) * chan
                    lanes = slice((x * 2 + y) * LANES, (x * 2 + y + 1) * LANES)
                    to = (a * 4 + b * 2) * chan
                    stack[to : to + chan, lanes] = parted[row : row + chan, :LANES]
                    stack[to + chan : to + 2 * chan, lanes] = parted[row : row + chan, LANES:]
    sums = jnp.dot(down_ref[...], stack[...], preferred_element_type=F32)
    for n in range(4):
        coarse_ref[n] = (sums[:, n * LANES : (n + 1) * LANES] * mask_ref[n : n + 1, :]).astype(
            BF16
        )
    wide = jnp.concatenate([grads[n * chan : (n + 1) * chan, :] for n in range(4)], axis=1)
    raw = lax.dot_general(wide, stack[...], NT, preferred_element_type=F32)
    for n in range(4):
        raw_ref[n * chan : (n + 1) * chan, :] = raw[:, n * LANES : (n + 1) * LANES]


def hidden_grad_kernel(
    in_chan, sides_ref, stats_ref, sums_ref, params_ref, hidden, hidden_ring_ref, pre,
    pre_ring_ref, acts_ref, stack_ref, raw_ref, front, rear, swap_out_ref, small_ref, out_ref,
    stats, hidden_ring, pre_ring, acts, stack, raw, acc, swap_ref, sems,
):
    chan = hidden.shape[0] // 16
    place = sides_ref[2]
    got_stats = started(stats_ref, stats, sems.at[0])
    got_acts = started(acts_ref, acts, sems.at[1])
    got = []
    for n, (source, target) in enumerate(
        ((hidden_ring_ref, hidden_ring), (pre_ring_ref, pre_ring))
    ):
        cuts = [n * chan for n in range(0, target.shape[0] // chan + 1, 4)]
        got.append(started_rows(source, target, cuts, sems.at[pl.ds(4 + 5 * n, len(cuts) - 1)]))
    got = list(zip(*got))
    got_stack = started(
        stack_ref.at[pl.ds(stack.shape[0] // 6, stack.shape[0]), :], stack, sems.at[2]
    )
    got_raw = started(raw_ref, raw, sems.at[3])
    raw_shift = jnp.sum(sums_ref[:, 0, :], axis=0, keepdims=True)
    raw_gain = jnp.sum(sums_ref[:, 1, :], axis=0, keepdims=True)
    got_stats.wait()
    count, average, inverse = merged_stats(stats)
    scale = lax.rsqrt(count)
    small_ref[...] = jnp.concatenate(
        [raw_shift * scale, raw_gain * scale, scale, jnp.zeros((5, LANES), F32)], axis=0
    )
    columns = [average, inverse, raw_shift / count, raw_gain / count, params_ref[0:1, :]]
    average, inverse, mean_shift, mean_gain, gain = [
        jnp.broadcast_to(column, (chan, LANES)) for column in to_columns(columns, chan)
    ]
    weight = gain * inverse
    got_acts.wait()
    for n, (p, q) in enumerate(OWN + RING):
        if n % 4 == 0 and n >= 16:
            for copy in got[n // 4 - 4]:
                copy.wait()
        held_hidden, held_pre = (hidden, pre) if n < 16 else (hidden_ring, pre_ring)
        own = slice(n * chan, (n + 1) * chan) if n < 16 else slice((n - 16) * chan, (n - 15) * chan)
        to = slice((p * 6 + q) * chan, (p * 6 + q + 1) * chan)
        tiles = []
        for half, held in enumerate((front, rear)):
            lanes = slice(half * LANES, (half + 1) * LANES)
            act = acts[p * 6 + q : p * 6 + q + 1, lanes]
            normed = (held_hidden[own, lanes] - average) * inverse
            grad = held_pre[own, lanes] - (mean_shift + normed * mean_gain)
            tiles.append(((act * weight) * grad).astype(BF16))
            held[to, :] = tiles[-1]
        swap_ref[to, :] = jnp.where(place == 0, tiles[1], tiles[0])
    kept = started(swap_ref, swap_out_ref, sems.at[24])
    got_stack.wait()
    got_raw.wait()
    rows = stack.shape[0] // 6
    band = rows // 3
    for p in range(4):
        own = slice(((p + 1) * 6 + 1) * chan, ((p + 1) * 6 + 5) * chan)
        grads = jnp.concatenate([front[own, :], rear[own, :]], axis=1)
        for dx in range(3):
            first = (p + dx) * rows
            part = lax.dot_general(
                stack[first : first + rows, :], grads, NT, preferred_element_type=F32
            )
            if p == 0:
                acc[dx] = part
            else:
                acc[dx] += part
    low = lax.broadcasted_iota(jnp.int32, (in_chan, LANES), 1) < chan
    for dx in range(3):
        for dy in range(3):
            for dz in range(3):
                blocks = []
                for q in range(4):
                    row = dz * band + (q + 1 + dy) * in_chan
                    lanes = slice((q // 2) * LANES, (q // 2 + 1) * LANES)
                    blocks.append(acc[dx, row : row + in_chan, lanes])
                both = jnp.where(low, blocks[0] + blocks[2], blocks[1] + blocks[3])
                folded = (both + pltpu.roll(both, chan, 1)).astype(out_ref.dtype)
                tap = (dx * 3 + dy) * 3 + dz
                if tap < 16:
                    out_ref[tap * in_chan : (tap + 1) * in_chan, :chan] = folded[:, :chan]
                else:
                    to = (tap - 16) * in_chan
                    out_ref[to : to + in_chan, chan:] = folded[:, chan:]
    out_ref[11 * in_chan : 16 * in_chan, chan:] = jnp.zeros(
        (5 * in_chan, LANES - chan), out_ref.dtype
    )
    tail = 16 * in_chan
    out_ref[tail : tail + 4 * chan, :] = raw[...].astype(out_ref.dtype)
    left = out_ref.shape[0] - tail - 4 * chan
    if left:
        out_ref[tail + 4 * chan :, :] = jnp.zeros((left, LANES), out_ref.dtype)
    kept.wait()


def point_grad_kernel(
    only_two, halves, chan, sides_ref, front, rear, before_ref, after_ref, bands_ref, act_ref,
    tags_ref, out_ref, bands, acts, tags_held, stack, cells, sems,
):
    rows = front.shape[0] // 6
    groups, depth = acts.shape
    place_z = sides_ref[2]
    late = [
        started(bands_ref, bands, sems.at[0]),
        started(act_ref, acts, sems.at[1]),
        started(tags_ref, tags_held, sems.at[2]),
    ]
    for x in range(6):
        own = slice(x * rows, (x + 1) * rows)
        low, high = front[own, :], rear[own, :]
        before, after = before_ref[own, :], after_ref[own, :]
        if only_two:
            before, after = keep(before, place_z != 0), keep(after, place_z == 0)
        for n, step in enumerate((1, 0, -1)):
            tiles = (low, high) if step == 0 else shifted(low, high, before, after, step)
            to = slice((x * 3 + n) * rows, (x * 3 + n + 1) * rows)
            stack[to, :LANES] = tiles[0]
            stack[to, LANES:] = tiles[1]
    for copy in late:
        copy.wait()
    for p in range(4):
        first = p * 3 * rows
        grid = jnp.dot(
            bands[...], stack[first : first + 9 * rows, :], preferred_element_type=F32
        )
        for q in range(4):
            k = p * 4 + q
            cells[k * chan : (k + 1) * chan, :] = (
                grid[q * chan : (q + 1) * chan] * acts[k : k + 1, :]
            ).astype(BF16)

    def from_cells(d):
        tags = tags_held[d]
        hot = jnp.concatenate(
            [hot_rows(tags[halves + h : halves + h + 1, :], 0, depth) for h in range(halves)], axis=1
        )
        found = jnp.dot(cells[...], hot, preferred_element_type=F32)
        for h in range(halves):
            group = jnp.broadcast_to(tags[h : h + 1, :], (chan, LANES))
            lanes = slice(h * LANES, (h + 1) * LANES)
            out = jnp.zeros((chan, LANES), F32)
            for k in range(groups):
                out = jnp.where(group == k, found[k * chan : (k + 1) * chan, lanes], out)
            out_ref[d, h * chan : (h + 1) * chan, :] = out.astype(BF16)

    together = 16

    def step(s, carry):
        for j in range(together):
            from_cells(together * s + j)
        return carry

    lax.fori_loop(0, tags_held.shape[0] // together, step, 0)


def piece_kernel(parts_ref, points_ref, out_ref):
    rows = points_ref.shape[1]
    piece = jnp.sum(parts_ref[...].astype(F32), axis=0).astype(BF16)
    for d in range(out_ref.shape[0]):
        out_ref[d, :rows, :] = points_ref[d]
        out_ref[d, rows:, :] = piece


def sum_kernel(parts_ref, out_ref):
    piece = jnp.sum(parts_ref[...].astype(F32), axis=0).astype(BF16)
    for d in range(out_ref.shape[0]):
        out_ref[d] = piece


def weights_out(rows, small_ref, in_chan, sub_ref, down_ref):
    chan = down_ref.shape[0]
    scale = small_ref[2:3, 0:1]
    for n in range(4):
        turned = rows(n).T * scale
        sub_ref[:, n * LANES : (n + 1) * LANES] = turned[:chan]
        left = sub_ref.shape[1] - 16 * in_chan - n * LANES
        if left > 0:
            width = min(left, LANES)
            first = 16 * in_chan + n * LANES
            sub_ref[:, first : first + width] = turned[chan:, :width]
    for n in range(2):
        both = rows(4 + n) * scale
        down_ref[:, 2 * n * LANES : (2 * n + 1) * LANES] = both[:chan]
        down_ref[:, (2 * n + 1) * LANES : (2 * n + 2) * LANES] = both[chan:]


def last_kernel(halves, chan, got_ref, small_ref, points_ref, sub_ref, down_ref, flat):
    devices = got_ref.shape[0]
    piece = got_ref.shape[1] - halves * chan
    for d in range(devices):
        block = got_ref[d]
        for h in range(halves):
            first = (d * halves + h) * LANES
            points_ref[:, first : first + LANES] = block[h * chan : (h + 1) * chan, :]
        flat[d * piece : (d + 1) * piece, :] = block[halves * chan :, :].astype(F32)
    weights_out(lambda n: flat[n * LANES : (n + 1) * LANES, :], small_ref, chan, sub_ref, down_ref)


def weights_kernel(chan, got_ref, small_ref, sub_ref, down_ref, flat):
    piece = got_ref.shape[1]
    for d in range(got_ref.shape[0]):
        flat[d * piece : (d + 1) * piece, :] = got_ref[d].astype(F32)
    weights_out(lambda n: flat[n * LANES : (n + 1) * LANES, :], small_ref, chan, sub_ref, down_ref)


def on_device(
    point_feats, voxel_ids, send_counts, active, w_sub, w_down, bn_gain, bn_shift, cotangent
):
    in_chan, slot_total = point_feats.shape
    devices = send_counts.shape[1]
    slot_cap = slot_total // devices
    size_x, size_y, size_z = active.shape
    groups = size_x * size_y
    out_chan = w_sub.shape[0]
    only_two = lax.axis_size("gz") == 2
    sides = jnp.stack(
        [lax.axis_index("gx") % 2, lax.axis_index("gy") % 2, lax.axis_index("gz")]
    ).astype(jnp.int32)
    aligned = slot_cap % LANES == 0
    halves = slot_cap // LANES if aligned else 1
    rows_x, rows_6, rows_64 = groups // 2 * in_chan, 36 * out_chan, 64 * in_chan
    wide, back_wide = 6 * out_chan, 4 * in_chan

    if aligned:
        payload = local_call(
            functools.partial(pack_kernel, halves, groups, size_z),
            [((devices, halves * in_chan + 8, LANES), BF16)],
            send_counts, point_feats, voxel_ids.reshape(-1, LANES),
            scratch=[((in_chan, slot_total), BF16), ((devices * halves, LANES), jnp.int32)],
            scalars=[((1, devices), jnp.int32)],
            hbm=(0, 1, 2), copies=6, moved=2e6,
        )[0]
        recv = everyone(payload)
    else:
        payload = pack_plain(point_feats, voxel_ids, send_counts, groups, size_z)
        together = LANES // slot_cap
        recv = everyone(payload)
        recv = recv.reshape(devices // together, together, in_chan + 8, slot_cap)
        recv = recv.transpose(0, 2, 1, 3).reshape(devices // together, in_chan + 8, LANES)
    chunks = recv.shape[0]

    acts = active.reshape(groups, size_z).astype(F32)
    params = jnp.pad(jnp.stack([bn_gain, bn_shift]), ((0, 6), (0, LANES - out_chan)))
    front, back = band_inputs(w_sub, in_chan)
    cot = cotangent.transpose(1, 2, 0, 3)
    *ends, grad_c, coarse_mask = local_call(
        coarse_kernel,
        [((2 * out_chan + 16, LANES), BF16)] * 2
        + [((4 * out_chan, LANES), BF16), ((8, LANES), F32)],
        sides, acts, cot, smem=(0,), moved=2e5,
    )
    cot_x = swaps(*ends, "gx")
    ends = local_call(
        coarse_rows_kernel,
        [((4 * out_chan + 16, LANES), BF16)] * 2,
        sides, acts, grad_c, *cot_x, smem=(0,), moved=2e5,
    )
    cot_y = swaps(*ends, "gy")
    by_child = (
        w_down.reshape(out_chan, 4, 2, out_chan)
        .transpose(1, 3, 2, 0)
        .reshape(4 * out_chan, 2 * out_chan)
    )
    recv, acts, grad_c, cot_x, cot_y, by_child, front, back, params = lax.optimization_barrier(
        (recv, acts, grad_c, cot_x, cot_y, by_child, front, back, params)
    )

    *mine, tags = local_call(
        functools.partial(scatter_kernel, halves, in_chan, size_y),
        [((rows_x, size_z), BF16)] * 2 + [((chunks, 8, LANES), F32)],
        sides, recv, acts,
        scratch=[
            ((groups * in_chan, chunks * halves * LANES), BF16),
            ((size_z, chunks * halves * LANES), BF16),
            ((chunks, 8, LANES), F32),
        ],
        smem=(0,), hbm_outs=(2,), copies=1, moved=2e7,
    )
    got_x = swaps(*mine, "gx")
    own, ring = ((16 * out_chan, size_z), F32), ((20 * out_chan, size_z), F32)
    acts_wide, *fine_grad = local_call(
        fine_grad_kernel,
        [((40, size_z), F32), own, ring],
        sides, acts, grad_c, *cot_x, *cot_y, by_child,
        scratch=[
            ((40, size_z), F32),
            ((16 * out_chan, LANES), BF16),
            ((16 * out_chan, 2 * size_z), BF16),
            ring,
        ],
        smem=(0,), hbm_outs=(0, 2), copies=2, moved=4e6,
    )
    got_x, acts_wide, fine_grad = lax.optimization_barrier((got_x, acts_wide, fine_grad))
    ends = local_call(
        rows_kernel,
        [((2 * rows_x, size_z), BF16)] * 2,
        sides, *mine, *got_x, smem=(0,), moved=1e6,
    )
    got_y = swaps(*ends, "gy")
    bands_shape, back_shape = (wide, 9 * 8 * in_chan), (back_wide, 9 * 6 * out_chan)
    own_bands_shape = (4 * out_chan, bands_shape[1])
    bands, back_bands, own_bands = local_call(
        bands_kernel,
        [(bands_shape, BF16), (back_shape, BF16), (own_bands_shape, BF16)],
        front, back,
        scratch=[(bands_shape, BF16), (back_shape, BF16)],
        hbm_outs=(0, 1), copies=2, moved=4e6,
    )
    got_y, bands, back_bands, own_bands = lax.optimization_barrier(
        (got_y, bands, back_bands, own_bands)
    )
    tile_low, tile_high, swap = local_call(
        functools.partial(columns_kernel, in_chan),
        [((rows_64, LANES), BF16)] * 3,
        sides, *mine, *got_x, *got_y, smem=(0,), moved=3e6,
    )
    before, after = z_exchange(tile_low, tile_high, swap)
    stack_shape = (3 * rows_64, size_z)
    stack = local_call(stack_kernel, [(stack_shape, BF16)], tile_low, tile_high, moved=4e6)[0]
    before, after, stack = lax.optimization_barrier((before, after, stack))

    stats_shape = (devices, 8, LANES)
    own_hidden, stack, stats, _ = local_call(
        functools.partial(conv_kernel, only_two),
        [own, (stack_shape, BF16), (stats_shape, F32), (stack_shape, BF16)],
        sides, stack, before, after, own_bands, acts_wide,
        aliases={1: 3}, smem=(0,), hbm_outs=(1,), copies=8, moved=1e7,
    )
    stats_in = everyone(stats)
    ring_hidden = local_call(
        conv_ring_kernel,
        [ring],
        bands, acts_wide, stack,
        scratch=[(bands_shape, BF16), ((40, size_z), F32), (stack_shape, BF16), ring],
        hbm=(0, 1, 2), hbm_outs=(0,), copies=4, moved=1e7,
    )[0]
    stats_in, ring_hidden = lax.optimization_barrier((stats_in, ring_hidden))
    held = [(stats_shape, F32)]
    own_pre, fine_out, sums = local_call(
        functools.partial(norm_kernel, OWN),
        [own, ((groups * out_chan, size_z), BF16), (stats_shape, F32)],
        stats_in, params, own_hidden, fine_grad[0], acts_wide,
        scratch=held
        + [((40, size_z), F32), ((groups * out_chan, size_z), BF16), (stats_shape, F32)],
        hbm=(4,), hbm_outs=(1, 2), copies=4, moved=5e6,
    )
    sums_in = everyone(sums)
    ring_pre, coarse, raw_down = local_call(
        functools.partial(norm_kernel, RING),
        [ring, ((4, out_chan, LANES), BF16), ((4 * out_chan, LANES), F32)],
        stats_in, params, ring_hidden, fine_grad[1], acts_wide, fine_out, grad_c, coarse_mask, w_down,
        scratch=held
        + [
            ring,
            ring,
            ((40, size_z), F32),
            ring,
            ((groups * out_chan, size_z), BF16),
            ((4 * out_chan, LANES), BF16),
            ((8 * out_chan, 4 * LANES), BF16),
            ((4 * out_chan, LANES), F32),
        ],
        hbm=(0, 2, 3, 4, 5, 6), hbm_outs=(0, 2), copies=16, moved=5e6,
    )
    sums_in, ring_pre, raw_down = lax.optimization_barrier((sums_in, ring_pre, raw_down))
    half_x, half_y, half_z = size_x // 2, size_y // 2, size_z // 2
    coarse_out = coarse.reshape(half_x, half_y, out_chan, half_z).transpose(2, 0, 1, 3)

    piece = -(-(16 * in_chan + 4 * out_chan) // devices)
    piece = -(-piece // 8) * 8
    grad_low, grad_high, grad_swap, small, parts = local_call(
        functools.partial(hidden_grad_kernel, in_chan),
        [((rows_6, LANES), BF16)] * 3 + [((8, LANES), F32), ((devices * piece, LANES), BF16)],
        sides, stats_in, sums_in, params, own_hidden, ring_hidden, own_pre, ring_pre, acts_wide,
        stack, raw_down,
        scratch=[
            (stats_shape, F32),
            ring,
            ring,
            ((40, size_z), F32),
            ((rows_64 // 8 * 6 * 3, size_z), BF16),
            ((4 * out_chan, LANES), F32),
            ((3, 24 * in_chan, 4 * out_chan), F32),
            ((rows_6, LANES), BF16),
        ],
        smem=(0,), hbm=(1, 5, 7, 8, 9, 10), hbm_outs=(2,), copies=25, moved=2e7,
    )
    grad_before, grad_after = z_exchange(grad_low, grad_high, grad_swap)
    parts = everyone(parts.reshape(devices, piece, LANES))

    points = local_call(
        functools.partial(point_grad_kernel, only_two, halves, in_chan),
        [((chunks, halves * in_chan, LANES), BF16)],
        sides, grad_low, grad_high, grad_before, grad_after, back_bands, acts, tags,
        scratch=[
            (back_shape, BF16),
            ((groups, size_z), F32),
            ((chunks, 8, LANES), F32),
            ((3 * rows_6, size_z), BF16),
            ((groups * in_chan, size_z), BF16),
        ],
        smem=(0,), hbm=(5, 6, 7), copies=3, moved=2e7,
    )[0]
    parts, points = lax.optimization_barrier((parts, points))
    shapes = [((out_chan, 27 * in_chan), F32), ((out_chan, 8 * out_chan), F32)]
    flat = [((devices * piece, LANES), F32)]
    if aligned:
        both = local_call(
            piece_kernel,
            [((devices, halves * in_chan + piece, LANES), BF16)],
            parts, points, moved=2e6,
        )[0]
        returned, raw_sub, raw_down = local_call(
            functools.partial(last_kernel, halves, in_chan),
            [((in_chan, slot_total), BF16)] + shapes,
            everyone(both), small, scratch=flat, moved=2e6,
        )
    else:
        points = points.reshape(chunks, in_chan, together, slot_cap).transpose(0, 2, 1, 3)
        returned = everyone(points.reshape(devices, in_chan, slot_cap))
        returned = returned.transpose(1, 0, 2).reshape(in_chan, slot_total)
        whole = local_call(sum_kernel, [((devices, piece, LANES), BF16)], parts)[0]
        raw_sub, raw_down = local_call(
            functools.partial(weights_kernel, in_chan), shapes, everyone(whole), small, scratch=flat
        )
    return (
        coarse_out,
        returned,
        raw_sub,
        raw_down,
        small[1, :out_chan],
        small[0, :out_chan],
    )


def solution(mesh):
    in_specs = (
        P(None, AXES),
        P(AXES),
        P(AXES, None),
        P("gx", "gy", "gz"),
        P(),
        P(),
        P(),
        P(),
        P(None, "gx", "gy", "gz"),
    )
    out_specs = (P(None, "gx", "gy", "gz"), P(None, AXES), P(), P(), P(), P())
    return jax.shard_map(
        on_device, mesh=mesh, in_specs=in_specs, out_specs=out_specs, check_vma=False
    )
```

```python
import functools
import math

import jax
import jax.numpy as jnp
from jax import lax
from jax.experimental import pallas as pl
from jax.experimental.pallas import tpu as pltpu
from jax.sharding import PartitionSpec as P

EPS = 1e-05
AXES = ("gx", "gy", "gz")
LANES = 128
GELU_SCALE = 0.7978845608028654
GELU_CUBE = 0.044715
F32 = jnp.float32
BF16 = jnp.bfloat16
NT = (((1,), (1,)), ((), ()))


def local_call(
    kernel, outs, *args, scratch=(), scalars=(), smem=(), hbm=(), hbm_outs=(), copies=0, moved=0, aliases=None
):
    held = sum(math.prod(shape) * jnp.dtype(kind).itemsize for shape, kind in scratch)
    limit = held // 2**20 + 6
    vmem = pl.BlockSpec(memory_space=pltpu.VMEM)
    scalar = pl.BlockSpec(memory_space=pltpu.SMEM)
    far = pl.BlockSpec(memory_space=pltpu.HBM)
    args = [
        pltpu.with_memory_space_constraint(arg, pltpu.HBM) if i in hbm else arg
        for i, arg in enumerate(args)
    ]
    held = [pltpu.VMEM(shape, kind) for shape, kind in scratch]
    held += [pltpu.SMEM(shape, kind) for shape, kind in scalars]
    if copies:
        held.append(pltpu.SemaphoreType.DMA((copies,)))
    return pl.pallas_call(
        kernel,
        out_shape=[
            pltpu.HBM(shape, kind) if i in hbm_outs else jax.ShapeDtypeStruct(shape, kind)
            for i, (shape, kind) in enumerate(outs)
        ],
        in_specs=[
            scalar if i in smem else far if i in hbm else vmem for i in range(len(args))
        ],
        out_specs=[far if i in hbm_outs else vmem for i in range(len(outs))],
        scratch_shapes=held,
        input_output_aliases=aliases or {},
        compiler_params=pltpu.CompilerParams(vmem_limit_bytes=limit * 1024 * 1024),
        cost_estimate=pl.CostEstimate(flops=0, bytes_accessed=int(moved), transcendentals=0),
    )(*args)


def started(source, target, semaphore):
    copy = pltpu.make_async_copy(source, target, semaphore)
    copy.start()
    return copy


def rows_of(n, count):
    return pl.ds(n * count, count)


def started_rows(source, target, cuts, semaphores):
    copies = []
    for n, (begin, end) in enumerate(zip(cuts, cuts[1:])):
        own = pl.ds(begin, end - begin)
        copies.append(started(source.at[own, :], target.at[own, :], semaphores.at[n]))
    return copies


OWN = [(p, q) for p in range(1, 5) for q in range(1, 5)]
RING = [(p, q) for p in range(6) for q in range(6) if (p, q) not in OWN]


def neighbours(axis, step):
    count = lax.axis_size(axis)
    return [(i, i + step) for i in range(count) if 0 <= i + step < count]


def swaps(first, second, axis):
    count = lax.axis_size(axis)
    got = []
    for block, begin in ((first, 0), (second, 1)):
        pairs = [(i, i + 1) for i in range(begin, count - 1, 2)]
        got.append(lax.ppermute(block, axis, pairs + [(j, i) for i, j in pairs]))
    return got


def sided(odd, first, second):
    return jnp.where(odd, first, second), jnp.where(odd, second, first)


def z_exchange(low, high, swap):
    if lax.axis_size("gz") != 2:
        return (
            lax.ppermute(high, "gz", neighbours("gz", 1)),
            lax.ppermute(low, "gz", neighbours("gz", -1)),
        )
    got = lax.ppermute(swap, "gz", [(0, 1), (1, 0)])
    return got, got


def everyone(block):
    return lax.all_to_all(block, AXES, split_axis=0, concat_axis=0, tiled=True)


def pack_kernel(
    halves, groups, depth, counts_ref, feats_ref, ids_ref, out_ref, feats, ids, counts, sems
):
    devices = out_ref.shape[0]
    chan = feats_ref.shape[0]
    parts = 4
    width = feats.shape[1] // parts
    got_ids = started(ids_ref, ids, sems.at[parts])
    got_counts = started(counts_ref, counts, sems.at[parts + 1])
    got = []
    for n in range(parts):
        lanes = pl.ds(n * width, width)
        got.append(started(feats_ref.at[:, lanes], feats.at[:, lanes], sems.at[n]))
    got_ids.wait()
    got_counts.wait()
    rank = lax.broadcasted_iota(jnp.int32, (halves, LANES), 0) * LANES + lax.broadcasted_iota(
        jnp.int32, (halves, LANES), 1
    )
    blank = jnp.zeros((8 - 2 * halves, LANES), F32)
    for d in range(devices):
        those = ids[d * halves : (d + 1) * halves, :]
        usable = rank < counts[0, d]
        group = jnp.where(usable, those // depth, groups).astype(F32)
        place = (those % depth).astype(F32)
        tags = jnp.concatenate([group, place, blank], axis=0)
        out_ref[d, halves * chan :, :] = tags.astype(BF16)
    for d in range(devices):
        if d * parts % devices == 0:
            got[d * parts // devices].wait()
        for h in range(halves):
            first = (d * halves + h) * LANES
            out_ref[d, h * chan : (h + 1) * chan, :] = feats[:, first : first + LANES]


def pack_plain(feats, ids, counts, groups, depth):
    chan, total = feats.shape
    devices = counts.shape[1]
    cap = total // devices
    ids = ids.reshape(devices, 1, cap)
    rank = jnp.arange(cap, dtype=jnp.int32)[None, None, :]
    group = jnp.where(rank < counts.reshape(devices, 1, 1), ids // depth, groups)
    tags = jnp.concatenate([group, ids % depth], axis=1).astype(BF16)
    rows = feats.reshape(chan, devices, cap).transpose(1, 0, 2)
    return jnp.concatenate([rows, jnp.pad(tags, ((0, 0), (0, 6), (0, 0)))], axis=1)


def hot_rows(row, first, count):
    index = lax.broadcasted_iota(jnp.int32, (count, LANES), 0).astype(F32).astype(BF16)
    row = jnp.broadcast_to(row, (count, LANES)).astype(BF16)
    return jnp.where(index + jnp.asarray(first, BF16) == row, jnp.ones_like(row), jnp.zeros_like(row))


def scatter_kernel(
    halves, chan, size_y, sides_ref, recv_ref, act_ref, first_ref, second_ref, tags_ref,
    masked, hot, tags_held, sems,
):
    chunks = recv_ref.shape[0]
    groups, depth = act_ref.shape
    for d in range(chunks):
        tags_held[d] = recv_ref[d][halves * chan :, :].astype(F32)
    kept = started(tags_held, tags_ref, sems.at[0])
    for d in range(chunks):
        block = recv_ref[d]
        tags = tags_held[d]
        for h in range(halves):
            feats = block[h * chan : (h + 1) * chan, :]
            lanes = slice((d * halves + h) * LANES, (d * halves + h + 1) * LANES)
            group = jnp.broadcast_to(tags[h : h + 1, :], (chan, LANES)).astype(BF16)
            for k in range(groups):
                masked[k * chan : (k + 1) * chan, lanes] = jnp.where(
                    group == k, feats, jnp.zeros_like(feats)
                )
            for row in range(0, depth, 32):
                hot[row : row + 32, lanes] = hot_rows(
                    tags[halves + h : halves + h + 1, :], row, 32
                )
    acc = lax.dot_general(masked[...], hot[...], NT, preferred_element_type=F32)
    odd = sides_ref[0] != 0
    half = size_y // 2
    for k in range(groups // 2):
        p, q = k // size_y, k % size_y
        row = ((q // half) * 4 + p * 2 + q % half) * chan
        blocks = []
        for n in (k, k + groups // 2):
            block = acc[n * chan : (n + 1) * chan, :] * act_ref[n : n + 1, :]
            blocks.append(block.astype(BF16))
        first_ref[row : row + chan, :], second_ref[row : row + chan, :] = sided(odd, *blocks)
    kept.wait()


def coarse_kernel(sides_ref, act_ref, cot_ref, first_ref, second_ref, grad_ref, mask_ref):
    depth = act_ref.shape[1]
    chan = cot_ref.shape[2]
    odd = sides_ref[0] != 0
    fine = lax.broadcasted_iota(jnp.int32, (depth, LANES), 0) // 2
    pair = (fine == lax.broadcasted_iota(jnp.int32, (depth, LANES), 1)).astype(BF16)
    acts = act_ref[...]
    sums = jnp.dot(acts.astype(BF16), pair, preferred_element_type=F32)
    masks, grads = [], []
    for x in range(2):
        for y in range(2):
            rows = [sums[(2 * x + a) * 4 + 2 * y + b] for a in range(2) for b in range(2)]
            any_row = (rows[0] + rows[1] + rows[2] + rows[3])[None, :]
            mask = jnp.where(any_row > 0.5, 1.0, 0.0)
            masks.append(mask)
            grads.append((cot_ref[x, y].astype(F32) * mask).astype(BF16))
    for n, grad in enumerate(grads):
        grad_ref[n * chan : (n + 1) * chan, :] = grad
    for y in range(2):
        own = slice(y * chan, (y + 1) * chan)
        first_ref[own, :], second_ref[own, :] = sided(odd, grads[y], grads[2 + y])
    mask_ref[...] = jnp.concatenate(masks + [jnp.zeros((4, LANES), F32)], axis=0)
    blank = jnp.zeros((8, LANES), F32)
    tails = []
    for p in (0, 3):
        rows = acts[4 * p : 4 * p + 4]
        tails.append(jnp.concatenate([rows[:, :LANES], rows[:, LANES:], blank], axis=0))
    tails = sided(odd, *tails)
    for out_ref, tail in zip((first_ref, second_ref), tails):
        out_ref[2 * chan :, :] = tail.astype(BF16)


def coarse_rows_kernel(sides_ref, act_ref, grad_ref, xf_ref, xs_ref, first_ref, second_ref):
    chan = grad_ref.shape[0] // 4
    odd_x, odd_y = sides_ref[0] != 0, sides_ref[1] != 0
    before, after = sided(odd_x, xf_ref[...], xs_ref[...])
    acts = act_ref[...]
    before_acts = before[2 * chan :, :].astype(F32)
    after_acts = after[2 * chan :, :].astype(F32)
    ends = []
    for y, q in ((0, 0), (1, 3)):
        own = slice(y * chan, (y + 1) * chan)
        columns = [before[own], grad_ref[own, :]]
        columns += [grad_ref[(2 + y) * chan : (3 + y) * chan, :], after[own]]
        rows = [before_acts[q : q + 1], before_acts[4 + q : 5 + q]]
        for p in range(4):
            row = acts[4 * p + q : 4 * p + q + 1]
            rows += [row[:, :LANES], row[:, LANES:]]
        rows += [after_acts[q : q + 1], after_acts[4 + q : 5 + q], jnp.zeros((4, LANES), F32)]
        ends.append(columns + [jnp.concatenate(rows, axis=0).astype(BF16)])
    row = 0
    for low, high in zip(*ends):
        own = slice(row, row + low.shape[0])
        first_ref[own, :], second_ref[own, :] = sided(odd_y, low, high)
        row += low.shape[0]


def fine_grad_kernel(
    sides_ref, act_ref, grad_ref, xf_ref, xs_ref, yf_ref, ys_ref, down_ref, acts_ref, own, ring_ref,
    acts_held, wide, up, ring, sems,
):
    chan = grad_ref.shape[0] // 4
    depth = act_ref.shape[1]
    acts = act_ref[...]
    x_ends = sided(sides_ref[0] != 0, xf_ref[...], xs_ref[...])
    y_ends = sided(sides_ref[1] != 0, yf_ref[...], ys_ref[...])
    xb, xa = [end[2 * chan :, :].astype(F32) for end in x_ends]
    yb, ya = [end[4 * chan :, :].astype(F32) for end in y_ends]
    rows = []
    for p in range(6):
        rows.append(jnp.concatenate([yb[2 * p : 2 * p + 1], yb[2 * p + 1 : 2 * p + 2]], axis=1))
        for q in range(4):
            if p in (0, 5):
                got = xb if p == 0 else xa
                rows.append(jnp.concatenate([got[q : q + 1], got[4 + q : 5 + q]], axis=1))
            else:
                rows.append(acts[4 * (p - 1) + q : 4 * (p - 1) + q + 1])
        rows.append(jnp.concatenate([ya[2 * p : 2 * p + 1], ya[2 * p + 1 : 2 * p + 2]], axis=1))
    rows.append(jnp.zeros((4, depth), F32))
    acts_held[...] = jnp.concatenate(rows, axis=0)
    kept = [started(acts_held, acts_ref, sems.at[0])]
    for x in range(4):
        for y in range(4):
            if y in (0, 3):
                block = y_ends[y // 3][x * chan : (x + 1) * chan, :]
            elif x in (0, 3):
                block = x_ends[x // 3][(y - 1) * chan : y * chan, :]
            else:
                first = ((x - 1) * 2 + y - 1) * chan
                block = grad_ref[first : first + chan, :]
            wide[(x * 4 + y) * chan : (x * 4 + y + 1) * chan, :] = block
    coarse_z = lax.broadcasted_iota(jnp.int32, (LANES, 2 * depth), 0)
    fine_z = lax.broadcasted_iota(jnp.int32, (LANES, 2 * depth), 1)
    child = jnp.where(fine_z < depth, 0, 1)
    spread = (2 * coarse_z + child == fine_z - child * depth).astype(BF16)
    up[...] = jnp.dot(wide[...], spread, preferred_element_type=F32).astype(BF16)
    for x in range(4):
        for y in range(4):
            those = slice((x * 4 + y) * chan, (x * 4 + y + 1) * chan)
            both = jnp.concatenate([up[those, :depth], up[those, depth:]], axis=0)
            grads = jnp.dot(down_ref[...], both, preferred_element_type=F32)
            for a in range(2):
                for b in range(2):
                    column = (2 * x + a - 1, 2 * y + b - 1)
                    block = grads[(a * 2 + b) * chan : (a * 2 + b + 1) * chan]
                    if column in OWN:
                        n = OWN.index(column)
                        own[n * chan : (n + 1) * chan, :] = block
                    elif column in RING:
                        n = RING.index(column)
                        ring[n * chan : (n + 1) * chan, :] = block
    kept.append(started(ring, ring_ref, sems.at[1]))
    for copy in kept:
        copy.wait()


def bands_kernel(
    front_ref, back_ref, bands_ref, back_bands_ref, own_ref, bands, back_bands, sems
):
    rows, width = front_ref.shape[0], front_ref.shape[1] // 9
    back_rows, back_width = back_ref.shape[0], back_ref.shape[1] // 9
    for t in range(9):
        block = front_ref[:, t * width : (t + 1) * width].astype(F32)
        for q in range(6):
            moved = pltpu.roll(block, q * back_rows, 1) if q else block
            bands[q * rows : (q + 1) * rows, t * width : (t + 1) * width] = moved.astype(BF16)
    kept = [started(bands, bands_ref, sems.at[0])]
    own_ref[...] = bands[rows : 5 * rows, :]
    for t in range(9):
        block = back_ref[:, t * back_width : (t + 1) * back_width].astype(F32)
        for q in range(4):
            moved = pltpu.roll(block, q * rows, 1) if q else block
            back_bands[
                q * back_rows : (q + 1) * back_rows, t * back_width : (t + 1) * back_width
            ] = moved.astype(BF16)
    kept.append(started(back_bands, back_bands_ref, sems.at[1]))
    for copy in kept:
        copy.wait()


def band_inputs(w_sub, in_chan):
    out_chan = w_sub.shape[0]
    taps = w_sub.reshape(out_chan, 3, 3, 3, in_chan)
    front = taps.transpose(0, 1, 3, 2, 4).reshape(out_chan, 9, 3 * in_chan)
    front = jnp.pad(front, ((0, 0), (0, 0), (0, 5 * in_chan)))
    back = taps[:, ::-1, ::-1].transpose(4, 1, 3, 2, 0).reshape(in_chan, 9, 3 * out_chan)
    back = jnp.pad(back, ((0, 0), (0, 0), (0, 3 * out_chan)))
    return front.reshape(out_chan, -1), back.reshape(in_chan, -1)


def rows_kernel(sides_ref, first_ref, second_ref, gf_ref, gs_ref, out_first_ref, out_second_ref):
    odd_x, odd_y = sides_ref[0] != 0, sides_ref[1] != 0
    half = first_ref.shape[0] // 2
    low, high = sided(odd_x, first_ref[...], second_ref[...])
    below, above = sided(odd_x, gf_ref[...], gs_ref[...])
    for n, block in enumerate((below, low, high, above)):
        own = slice(n * half, (n + 1) * half)
        out_first_ref[own, :], out_second_ref[own, :] = sided(odd_y, block[:half], block[half:])


def columns_kernel(
    chan, sides_ref, first_ref, second_ref, gf_ref, gs_ref, yf_ref, ys_ref, front_ref, rear_ref, swap_ref
):
    odd_x, odd_y, place = sides_ref[0] != 0, sides_ref[1] != 0, sides_ref[2]
    low, high = sided(odd_x, first_ref[...], second_ref[...])
    below, above = sided(odd_x, gf_ref[...], gs_ref[...])
    left, right = sided(odd_y, yf_ref[...], ys_ref[...])
    for n, own in enumerate((below, low, high, above)):
        for p in range(2):
            for y in range(8):
                if y in (0, 1, 6, 7):
                    got = left if y < 2 else right
                    row = (n * 4 + p * 2 + y % 2) * chan
                else:
                    got = own
                    row = (((y - 2) // 2) * 4 + p * 2 + y % 2) * chan
                block = got[row : row + chan]
                to = ((n * 2 + p) * 8 + y) * chan
                front_ref[to : to + chan, :] = block[:, :LANES]
                rear_ref[to : to + chan, :] = block[:, LANES:]
                swap_ref[to : to + chan, :] = jnp.where(
                    place == 0, block[:, LANES:], block[:, :LANES]
                )


def shifted(low, high, before, after, step):
    lane = lax.broadcasted_iota(jnp.int32, low.shape, 1)
    if step > 0:
        turned = [pltpu.roll(tile.astype(F32), LANES - 1, 1) for tile in (low, high, after)]
        edge = lane == LANES - 1
        tiles = [jnp.where(edge, turned[1], turned[0]), jnp.where(edge, turned[2], turned[1])]
    else:
        turned = [pltpu.roll(tile.astype(F32), 1, 1) for tile in (before, low, high)]
        edge = lane == 0
        tiles = [jnp.where(edge, turned[0], turned[1]), jnp.where(edge, turned[1], turned[2])]
    return tiles[0].astype(BF16), tiles[1].astype(BF16)


def keep(tile, wanted):
    return jnp.where(wanted, tile, jnp.zeros_like(tile))


def to_rows(columns):
    lane = lax.broadcasted_iota(jnp.int32, (LANES, LANES), 1)
    wide = jnp.zeros((LANES, LANES), F32)
    for n, column in enumerate(columns):
        tall = jnp.concatenate([column, jnp.zeros((LANES - column.shape[0], 1), F32)], axis=0)
        wide = jnp.where(lane == n, tall, wide)
    return wide.T[:8, :]


def to_columns(rows, chan):
    wide = jnp.concatenate(rows + [jnp.zeros((LANES - len(rows), LANES), F32)], axis=0).T
    return [wide[:chan, n : n + 1] for n in range(len(rows))]


def stack_kernel(low_ref, high_ref, stack_ref):
    rows = low_ref.shape[0] // 8
    for x in range(8):
        own = slice(x * rows, (x + 1) * rows)
        low, high = low_ref[own, :], high_ref[own, :]
        for n, step in enumerate((-1, 0, 1)):
            tiles = (low, high) if step == 0 else shifted(low, high, high, low, step)
            to = slice((x * 3 + n) * rows, (x * 3 + n + 1) * rows)
            stack_ref[to, :LANES] = tiles[0]
            stack_ref[to, LANES:] = tiles[1]


def patch(stack, x, rows, before, after):
    lane = lax.broadcasted_iota(jnp.int32, before.shape, 1)
    to = slice(x * 3 * rows, (x * 3 + 1) * rows)
    edge = pltpu.roll(before.astype(F32), 1, 1)
    own = stack[to, :LANES].astype(F32)
    stack[to, :LANES] = jnp.where(lane == 0, edge, own).astype(BF16)
    to = slice((x * 3 + 2) * rows, (x * 3 + 3) * rows)
    edge = pltpu.roll(after.astype(F32), LANES - 1, 1)
    own = stack[to, LANES:].astype(F32)
    stack[to, LANES:] = jnp.where(lane == LANES - 1, edge, own).astype(BF16)


def conv_kernel(
    only_two, sides_ref, stack_in_ref, before_ref, after_ref, bands_ref, acts_ref,
    hidden, stack_ref, stats_ref, stack, sems,
):
    rows = before_ref.shape[0] // 8
    depth = acts_ref.shape[1]
    chan = bands_ref.shape[0] // 4
    place = sides_ref[2]
    kept = []
    total = jnp.zeros((chan, depth), F32)
    count = jnp.zeros((1, depth), F32)
    for x in range(8):
        own = slice(x * rows, (x + 1) * rows)
        before, after = before_ref[own, :], after_ref[own, :]
        if only_two:
            before, after = keep(before, place != 0), keep(after, place == 0)
        patch(stack, x, rows, before, after)
        own = rows_of(x, 3 * rows)
        kept.append(started(stack.at[own, :], stack_ref.at[own, :], sems.at[x]))
        p = x - 2
        if not 1 <= p <= 4:
            continue
        first = p * 3 * rows
        out = jnp.dot(
            bands_ref[...], stack[first : first + 9 * rows, :], preferred_element_type=F32
        )
        for q in range(1, 5):
            act = acts_ref[p * 6 + q : p * 6 + q + 1, :]
            block = out[(q - 1) * chan : q * chan] * act
            n = OWN.index((p, q))
            hidden[n * chan : (n + 1) * chan, :] = block
            total = total + block
            count = count + act
    count = jnp.sum(count, axis=1, keepdims=True)
    total = jnp.sum(total, axis=1, keepdims=True)
    mean = total / jnp.maximum(count, 1.0)
    squares = jnp.zeros((chan, depth), F32)
    for n, (p, q) in enumerate(OWN):
        act = acts_ref[p * 6 + q : p * 6 + q + 1, :]
        centred = (hidden[n * chan : (n + 1) * chan, :] - mean) * act
        squares = squares + centred * centred
    squares = jnp.sum(squares, axis=1, keepdims=True)
    packed = to_rows([total, squares, jnp.broadcast_to(count, (chan, 1))])
    for d in range(stats_ref.shape[0]):
        stats_ref[d] = packed
    for copy in kept:
        copy.wait()


def conv_ring_kernel(bands_ref, acts_ref, stack_ref, hidden_ref, bands, acts, stack, hidden, sems):
    rows = stack.shape[0] // 24
    wide = bands.shape[0]
    chan = wide // 6
    got = [
        started(acts_ref, acts, sems.at[0]),
        started(bands_ref, bands, sems.at[1]),
        started(stack_ref, stack, sems.at[2]),
    ]
    for copy in got:
        copy.wait()
    for p in range(6):
        taps = stack[p * 3 * rows : (p * 3 + 9) * rows, :]
        if p in (0, 5):
            out = jnp.dot(bands[...], taps, preferred_element_type=F32)
            columns = range(6)
        else:
            ends = jnp.concatenate([bands[:chan, :], bands[5 * chan :, :]], axis=0)
            out = jnp.dot(ends, taps, preferred_element_type=F32)
            columns = (0, 5)
        for i, q in enumerate(columns):
            n = RING.index((p, q))
            hidden[n * chan : (n + 1) * chan, :] = (
                out[i * chan : (i + 1) * chan] * acts[p * 6 + q : p * 6 + q + 1, :]
            )
    kept = started(hidden, hidden_ref, sems.at[3])
    kept.wait()


def merged_stats(stats_ref):
    totals, squares, counts = stats_ref[:, 0, :], stats_ref[:, 1, :], stats_ref[:, 2, :]
    count = jnp.sum(counts, axis=0, keepdims=True)
    average = jnp.sum(totals, axis=0, keepdims=True) / count
    off = totals / jnp.maximum(counts, 1.0) - average
    spread = jnp.sum(squares + counts * off * off, axis=0, keepdims=True)
    return count, average, lax.rsqrt(spread / count + EPS)


def norm_kernel(
    columns, stats_ref, params_ref, hidden, fine, acts_ref, *rest
):
    own = columns is OWN
    if own:
        pre, out_ref, sums_ref, stats, acts, outs, sums_held, sems = rest
    else:
        hidden_ref, fine_ref = hidden, fine
        (out_ref, grad_ref, mask_ref, down_ref, pre_ref, coarse_ref, raw_ref) = rest[:7]
        stats, hidden, fine, acts, pre, outs, grads, taps, raw, sems = rest[7:]
    chan = hidden.shape[0] // len(columns)
    depth = acts.shape[1]
    got_stats = started(stats_ref, stats, sems.at[0])
    got_acts = started(acts_ref, acts, sems.at[1])
    cuts = [n * chan for n in range(0, len(columns) + 1, 4)]
    parts = len(cuts) - 1
    if not own:
        got = started_rows(hidden_ref, hidden, cuts, sems.at[pl.ds(2, parts)])
        got_fine = started_rows(fine_ref, fine, cuts, sems.at[pl.ds(2 + parts, parts)])
        last = 2 + 2 * parts
        got_down = [
            started(out_ref, outs, sems.at[last + 1]),
            started(grad_ref, grads, sems.at[last + 2]),
        ]
    got_stats.wait()
    count, average, inverse = merged_stats(stats)
    full = (chan, LANES)
    average, inverse, gain, shift = [
        jnp.broadcast_to(column, full)
        for column in to_columns([average, inverse, params_ref[0:1, :], params_ref[1:2, :]], chan)
    ]
    sum_shift = jnp.zeros((chan, LANES), F32)
    sum_gain = jnp.zeros((chan, LANES), F32)
    got_acts.wait()
    for n, (p, q) in enumerate(columns):
        if n % 4 == 0 and not own:
            got[n // 4].wait()
            got_fine[n // 4].wait()
        own_rows = slice(n * chan, (n + 1) * chan)
        for half in range(depth // LANES):
            lanes = slice(half * LANES, (half + 1) * LANES)
            act = acts[p * 6 + q : p * 6 + q + 1, lanes]
            normed = (hidden[own_rows, lanes] - average) * inverse
            x = gain * normed + shift
            square = x * x
            bent = jnp.tanh(GELU_SCALE * (x + GELU_CUBE * (square * x)))
            cdf = 0.5 + 0.5 * bent
            slope = cdf + (0.5 * x) * (1.0 - bent * bent) * (
                GELU_SCALE + (3.0 * GELU_CUBE * GELU_SCALE) * square
            )
            grad = (act * slope) * fine[own_rows, lanes]
            pre[own_rows, lanes] = grad
            if own:
                sum_shift = sum_shift + grad
                sum_gain = sum_gain + grad * normed
                outs[own_rows, lanes] = (x * cdf * act).astype(BF16)
    if own:
        kept = [started(outs, out_ref, sems.at[2])]
        sums = to_rows(
            [jnp.sum(sum_shift, axis=1, keepdims=True), jnp.sum(sum_gain, axis=1, keepdims=True)]
        )
        for d in range(sums_ref.shape[0]):
            sums_held[d] = sums
        kept.append(started(sums_held, sums_ref, sems.at[3]))
    else:
        kept = [started(pre, pre_ref, sems.at[2 + 2 * parts])]
        for copy in got_down:
            copy.wait()
        down_conv(outs, grads, mask_ref, down_ref, coarse_ref, raw, taps)
        kept.append(started(raw, raw_ref, sems.at[last + 3]))
    for copy in kept:
        copy.wait()


def down_conv(outs, grads, mask_ref, down_ref, coarse_ref, raw_ref, stack):
    depth = outs.shape[1]
    chan = grads.shape[0] // 4
    source = lax.broadcasted_iota(jnp.int32, (depth, depth), 0)
    target = lax.broadcasted_iota(jnp.int32, (depth, depth), 1)
    wanted = jnp.where(target < LANES, 2 * target, 2 * (target - LANES) + 1)
    sort = (source == wanted).astype(BF16)
    parted = jnp.dot(outs[...], sort, preferred_element_type=F32).astype(BF16)
    for x in range(2):
        for y in range(2):
            for a in range(2):
                for b in range(2):
                    row = ((2 * x + a) * 4 + 2 * y + b) * chan
                    lanes = slice((x * 2 + y) * LANES, (x * 2 + y + 1) * LANES)
                    to = (a * 4 + b * 2) * chan
                    stack[to : to + chan, lanes] = parted[row : row + chan, :LANES]
                    stack[to + chan : to + 2 * chan, lanes] = parted[row : row + chan, LANES:]
    sums = jnp.dot(down_ref[...], stack[...], preferred_element_type=F32)
    for n in range(4):
        coarse_ref[n] = (sums[:, n * LANES : (n + 1) * LANES] * mask_ref[n : n + 1, :]).astype(
            BF16
        )
    wide = jnp.concatenate([grads[n * chan : (n + 1) * chan, :] for n in range(4)], axis=1)
    raw = lax.dot_general(wide, stack[...], NT, preferred_element_type=F32)
    for n in range(4):
        raw_ref[n * chan : (n + 1) * chan, :] = raw[:, n * LANES : (n + 1) * LANES]


def hidden_grad_kernel(
    in_chan, sides_ref, stats_ref, sums_ref, params_ref, hidden, hidden_ring_ref, pre,
    pre_ring_ref, acts_ref, stack_ref, raw_ref, front, rear, swap_out_ref, small_ref, out_ref,
    stats, hidden_ring, pre_ring, acts, stack, raw, acc, swap_ref, sems,
):
    chan = hidden.shape[0] // 16
    place = sides_ref[2]
    got_stats = started(stats_ref, stats, sems.at[0])
    got_acts = started(acts_ref, acts, sems.at[1])
    got = []
    for n, (source, target) in enumerate(
        ((hidden_ring_ref, hidden_ring), (pre_ring_ref, pre_ring))
    ):
        cuts = [n * chan for n in range(0, target.shape[0] // chan + 1, 4)]
        got.append(started_rows(source, target, cuts, sems.at[pl.ds(4 + 5 * n, len(cuts) - 1)]))
    got = list(zip(*got))
    got_stack = started(
        stack_ref.at[pl.ds(stack.shape[0] // 6, stack.shape[0]), :], stack, sems.at[2]
    )
    got_raw = started(raw_ref, raw, sems.at[3])
    raw_shift = jnp.sum(sums_ref[:, 0, :], axis=0, keepdims=True)
    raw_gain = jnp.sum(sums_ref[:, 1, :], axis=0, keepdims=True)
    got_stats.wait()
    count, average, inverse = merged_stats(stats)
    scale = lax.rsqrt(count)
    small_ref[...] = jnp.concatenate(
        [raw_shift * scale, raw_gain * scale, scale, jnp.zeros((5, LANES), F32)], axis=0
    )
    columns = [average, inverse, raw_shift / count, raw_gain / count, params_ref[0:1, :]]
    average, inverse, mean_shift, mean_gain, gain = [
        jnp.broadcast_to(column, (chan, LANES)) for column in to_columns(columns, chan)
    ]
    weight = gain * inverse
    got_acts.wait()
    for n, (p, q) in enumerate(OWN + RING):
        if n % 4 == 0 and n >= 16:
            for copy in got[n // 4 - 4]:
                copy.wait()
        held_hidden, held_pre = (hidden, pre) if n < 16 else (hidden_ring, pre_ring)
        own = slice(n * chan, (n + 1) * chan) if n < 16 else slice((n - 16) * chan, (n - 15) * chan)
        to = slice((p * 6 + q) * chan, (p * 6 + q + 1) * chan)
        tiles = []
        for half, held in enumerate((front, rear)):
            lanes = slice(half * LANES, (half + 1) * LANES)
            act = acts[p * 6 + q : p * 6 + q + 1, lanes]
            normed = (held_hidden[own, lanes] - average) * inverse
            grad = held_pre[own, lanes] - (mean_shift + normed * mean_gain)
            tiles.append(((act * weight) * grad).astype(BF16))
            held[to, :] = tiles[-1]
        swap_ref[to, :] = jnp.where(place == 0, tiles[1], tiles[0])
    kept = started(swap_ref, swap_out_ref, sems.at[24])
    got_stack.wait()
    got_raw.wait()
    rows = stack.shape[0] // 6
    band = rows // 3
    owned = [slice(((p + 1) * 6 + 1) * chan, ((p + 1) * 6 + 5) * chan) for p in range(4)]
    grads = jnp.concatenate([held[own, :] for own in owned for held in (front, rear)], axis=1)
    for dx in range(3):
        taps = jnp.concatenate(
            [stack[(p + dx) * rows : (p + dx + 1) * rows, :] for p in range(4)], axis=1
        )
        acc[dx] = lax.dot_general(taps, grads, NT, preferred_element_type=F32)
    low = lax.broadcasted_iota(jnp.int32, (in_chan, LANES), 1) < chan
    for dx in range(3):
        for dy in range(3):
            for dz in range(3):
                blocks = []
                for q in range(4):
                    row = dz * band + (q + 1 + dy) * in_chan
                    lanes = slice((q // 2) * LANES, (q // 2 + 1) * LANES)
                    blocks.append(acc[dx, row : row + in_chan, lanes])
                both = jnp.where(low, blocks[0] + blocks[2], blocks[1] + blocks[3])
                folded = (both + pltpu.roll(both, chan, 1)).astype(out_ref.dtype)
                tap = (dx * 3 + dy) * 3 + dz
                if tap < 16:
                    out_ref[tap * in_chan : (tap + 1) * in_chan, :chan] = folded[:, :chan]
                else:
                    to = (tap - 16) * in_chan
                    out_ref[to : to + in_chan, chan:] = folded[:, chan:]
    out_ref[11 * in_chan : 16 * in_chan, chan:] = jnp.zeros(
        (5 * in_chan, LANES - chan), out_ref.dtype
    )
    tail = 16 * in_chan
    out_ref[tail : tail + 4 * chan, :] = raw[...].astype(out_ref.dtype)
    left = out_ref.shape[0] - tail - 4 * chan
    if left:
        out_ref[tail + 4 * chan :, :] = jnp.zeros((left, LANES), out_ref.dtype)
    kept.wait()


def point_grad_kernel(
    only_two, halves, chan, sides_ref, front, rear, before_ref, after_ref, bands_ref, act_ref,
    tags_ref, out_ref, bands, acts, tags_held, stack, cells, sems,
):
    rows = front.shape[0] // 6
    groups, depth = acts.shape
    place_z = sides_ref[2]
    late = [
        started(bands_ref, bands, sems.at[0]),
        started(act_ref, acts, sems.at[1]),
        started(tags_ref, tags_held, sems.at[2]),
    ]
    for x in range(6):
        own = slice(x * rows, (x + 1) * rows)
        low, high = front[own, :], rear[own, :]
        before, after = before_ref[own, :], after_ref[own, :]
        if only_two:
            before, after = keep(before, place_z != 0), keep(after, place_z == 0)
        for n, step in enumerate((1, 0, -1)):
            tiles = (low, high) if step == 0 else shifted(low, high, before, after, step)
            to = slice((x * 3 + n) * rows, (x * 3 + n + 1) * rows)
            stack[to, :LANES] = tiles[0]
            stack[to, LANES:] = tiles[1]
    for copy in late:
        copy.wait()
    for p in range(4):
        first = p * 3 * rows
        grid = jnp.dot(
            bands[...], stack[first : first + 9 * rows, :], preferred_element_type=F32
        )
        for q in range(4):
            k = p * 4 + q
            cells[k * chan : (k + 1) * chan, :] = (
                grid[q * chan : (q + 1) * chan] * acts[k : k + 1, :]
            ).astype(BF16)

    def from_cells(d):
        tags = tags_held[d]
        hot = jnp.concatenate(
            [hot_rows(tags[halves + h : halves + h + 1, :], 0, depth) for h in range(halves)], axis=1
        )
        found = jnp.dot(cells[...], hot, preferred_element_type=F32)
        for h in range(halves):
            group = jnp.broadcast_to(tags[h : h + 1, :], (chan, LANES))
            lanes = slice(h * LANES, (h + 1) * LANES)
            out = jnp.zeros((chan, LANES), F32)
            for k in range(groups):
                out = jnp.where(group == k, found[k * chan : (k + 1) * chan, lanes], out)
            out_ref[d, h * chan : (h + 1) * chan, :] = out.astype(BF16)

    together = 16

    def step(s, carry):
        for j in range(together):
            from_cells(together * s + j)
        return carry

    lax.fori_loop(0, tags_held.shape[0] // together, step, 0)


def piece_kernel(parts_ref, points_ref, out_ref):
    rows = points_ref.shape[1]
    piece = jnp.sum(parts_ref[...].astype(F32), axis=0).astype(BF16)
    for d in range(out_ref.shape[0]):
        out_ref[d, :rows, :] = points_ref[d]
        out_ref[d, rows:, :] = piece


def sum_kernel(parts_ref, out_ref):
    piece = jnp.sum(parts_ref[...].astype(F32), axis=0).astype(BF16)
    for d in range(out_ref.shape[0]):
        out_ref[d] = piece


def weights_out(rows, small_ref, in_chan, sub_ref, down_ref):
    chan = down_ref.shape[0]
    scale = small_ref[2:3, 0:1]
    for n in range(4):
        turned = rows(n).T * scale
        sub_ref[:, n * LANES : (n + 1) * LANES] = turned[:chan]
        left = sub_ref.shape[1] - 16 * in_chan - n * LANES
        if left > 0:
            width = min(left, LANES)
            first = 16 * in_chan + n * LANES
            sub_ref[:, first : first + width] = turned[chan:, :width]
    for n in range(2):
        both = rows(4 + n) * scale
        down_ref[:, 2 * n * LANES : (2 * n + 1) * LANES] = both[:chan]
        down_ref[:, (2 * n + 1) * LANES : (2 * n + 2) * LANES] = both[chan:]


def last_kernel(halves, chan, got_ref, small_ref, points_ref, sub_ref, down_ref, flat):
    devices = got_ref.shape[0]
    piece = got_ref.shape[1] - halves * chan
    for d in range(devices):
        block = got_ref[d]
        for h in range(halves):
            first = (d * halves + h) * LANES
            points_ref[:, first : first + LANES] = block[h * chan : (h + 1) * chan, :]
        flat[d * piece : (d + 1) * piece, :] = block[halves * chan :, :].astype(F32)
    weights_out(lambda n: flat[n * LANES : (n + 1) * LANES, :], small_ref, chan, sub_ref, down_ref)


def weights_kernel(chan, got_ref, small_ref, sub_ref, down_ref, flat):
    piece = got_ref.shape[1]
    for d in range(got_ref.shape[0]):
        flat[d * piece : (d + 1) * piece, :] = got_ref[d].astype(F32)
    weights_out(lambda n: flat[n * LANES : (n + 1) * LANES, :], small_ref, chan, sub_ref, down_ref)


def on_device(
    point_feats, voxel_ids, send_counts, active, w_sub, w_down, bn_gain, bn_shift, cotangent
):
    in_chan, slot_total = point_feats.shape
    devices = send_counts.shape[1]
    slot_cap = slot_total // devices
    size_x, size_y, size_z = active.shape
    groups = size_x * size_y
    out_chan = w_sub.shape[0]
    only_two = lax.axis_size("gz") == 2
    sides = jnp.stack(
        [lax.axis_index("gx") % 2, lax.axis_index("gy") % 2, lax.axis_index("gz")]
    ).astype(jnp.int32)
    aligned = slot_cap % LANES == 0
    halves = slot_cap // LANES if aligned else 1
    rows_x, rows_6, rows_64 = groups // 2 * in_chan, 36 * out_chan, 64 * in_chan
    wide, back_wide = 6 * out_chan, 4 * in_chan

    if aligned:
        payload = local_call(
            functools.partial(pack_kernel, halves, groups, size_z),
            [((devices, halves * in_chan + 8, LANES), BF16)],
            send_counts, point_feats, voxel_ids.reshape(-1, LANES),
            scratch=[((in_chan, slot_total), BF16), ((devices * halves, LANES), jnp.int32)],
            scalars=[((1, devices), jnp.int32)],
            hbm=(0, 1, 2), copies=6, moved=2e6,
        )[0]
        recv = everyone(payload)
    else:
        payload = pack_plain(point_feats, voxel_ids, send_counts, groups, size_z)
        together = LANES // slot_cap
        recv = everyone(payload)
        recv = recv.reshape(devices // together, together, in_chan + 8, slot_cap)
        recv = recv.transpose(0, 2, 1, 3).reshape(devices // together, in_chan + 8, LANES)
    chunks = recv.shape[0]

    acts = active.reshape(groups, size_z).astype(F32)
    params = jnp.pad(jnp.stack([bn_gain, bn_shift]), ((0, 6), (0, LANES - out_chan)))
    front, back = band_inputs(w_sub, in_chan)
    cot = cotangent.transpose(1, 2, 0, 3)
    *ends, grad_c, coarse_mask = local_call(
        coarse_kernel,
        [((2 * out_chan + 16, LANES), BF16)] * 2
        + [((4 * out_chan, LANES), BF16), ((8, LANES), F32)],
        sides, acts, cot, smem=(0,), moved=2e5,
    )
    cot_x = swaps(*ends, "gx")
    ends = local_call(
        coarse_rows_kernel,
        [((4 * out_chan + 16, LANES), BF16)] * 2,
        sides, acts, grad_c, *cot_x, smem=(0,), moved=2e5,
    )
    cot_y = swaps(*ends, "gy")
    by_child = (
        w_down.reshape(out_chan, 4, 2, out_chan)
        .transpose(1, 3, 2, 0)
        .reshape(4 * out_chan, 2 * out_chan)
    )
    recv, acts, grad_c, cot_x, cot_y, by_child, front, back, params = lax.optimization_barrier(
        (recv, acts, grad_c, cot_x, cot_y, by_child, front, back, params)
    )

    *mine, tags = local_call(
        functools.partial(scatter_kernel, halves, in_chan, size_y),
        [((rows_x, size_z), BF16)] * 2 + [((chunks, 8, LANES), F32)],
        sides, recv, acts,
        scratch=[
            ((groups * in_chan, chunks * halves * LANES), BF16),
            ((size_z, chunks * halves * LANES), BF16),
            ((chunks, 8, LANES), F32),
        ],
        smem=(0,), hbm_outs=(2,), copies=1, moved=2e7,
    )
    got_x = swaps(*mine, "gx")
    own, ring = ((16 * out_chan, size_z), F32), ((20 * out_chan, size_z), F32)
    acts_wide, *fine_grad = local_call(
        fine_grad_kernel,
        [((40, size_z), F32), own, ring],
        sides, acts, grad_c, *cot_x, *cot_y, by_child,
        scratch=[
            ((40, size_z), F32),
            ((16 * out_chan, LANES), BF16),
            ((16 * out_chan, 2 * size_z), BF16),
            ring,
        ],
        smem=(0,), hbm_outs=(0, 2), copies=2, moved=4e6,
    )
    got_x, acts_wide, fine_grad = lax.optimization_barrier((got_x, acts_wide, fine_grad))
    ends = local_call(
        rows_kernel,
        [((2 * rows_x, size_z), BF16)] * 2,
        sides, *mine, *got_x, smem=(0,), moved=1e6,
    )
    got_y = swaps(*ends, "gy")
    bands_shape, back_shape = (wide, 9 * 8 * in_chan), (back_wide, 9 * 6 * out_chan)
    own_bands_shape = (4 * out_chan, bands_shape[1])
    bands, back_bands, own_bands = local_call(
        bands_kernel,
        [(bands_shape, BF16), (back_shape, BF16), (own_bands_shape, BF16)],
        front, back,
        scratch=[(bands_shape, BF16), (back_shape, BF16)],
        hbm_outs=(0, 1), copies=2, moved=4e6,
    )
    got_y, bands, back_bands, own_bands = lax.optimization_barrier(
        (got_y, bands, back_bands, own_bands)
    )
    tile_low, tile_high, swap = local_call(
        functools.partial(columns_kernel, in_chan),
        [((rows_64, LANES), BF16)] * 3,
        sides, *mine, *got_x, *got_y, smem=(0,), moved=3e6,
    )
    before, after = z_exchange(tile_low, tile_high, swap)
    stack_shape = (3 * rows_64, size_z)
    stack = local_call(stack_kernel, [(stack_shape, BF16)], tile_low, tile_high, moved=4e6)[0]
    before, after, stack = lax.optimization_barrier((before, after, stack))

    stats_shape = (devices, 8, LANES)
    own_hidden, stack, stats, _ = local_call(
        functools.partial(conv_kernel, only_two),
        [own, (stack_shape, BF16), (stats_shape, F32), (stack_shape, BF16)],
        sides, stack, before, after, own_bands, acts_wide,
        aliases={1: 3}, smem=(0,), hbm_outs=(1,), copies=8, moved=1e7,
    )
    stats_in = everyone(stats)
    ring_hidden = local_call(
        conv_ring_kernel,
        [ring],
        bands, acts_wide, stack,
        scratch=[(bands_shape, BF16), ((40, size_z), F32), (stack_shape, BF16), ring],
        hbm=(0, 1, 2), hbm_outs=(0,), copies=4, moved=1e7,
    )[0]
    stats_in, ring_hidden = lax.optimization_barrier((stats_in, ring_hidden))
    held = [(stats_shape, F32)]
    own_pre, fine_out, sums = local_call(
        functools.partial(norm_kernel, OWN),
        [own, ((groups * out_chan, size_z), BF16), (stats_shape, F32)],
        stats_in, params, own_hidden, fine_grad[0], acts_wide,
        scratch=held
        + [((40, size_z), F32), ((groups * out_chan, size_z), BF16), (stats_shape, F32)],
        hbm=(4,), hbm_outs=(1, 2), copies=4, moved=5e6,
    )
    sums_in = everyone(sums)
    ring_pre, coarse, raw_down = local_call(
        functools.partial(norm_kernel, RING),
        [ring, ((4, out_chan, LANES), BF16), ((4 * out_chan, LANES), F32)],
        stats_in, params, ring_hidden, fine_grad[1], acts_wide, fine_out, grad_c, coarse_mask, w_down,
        scratch=held
        + [
            ring,
            ring,
            ((40, size_z), F32),
            ring,
            ((groups * out_chan, size_z), BF16),
            ((4 * out_chan, LANES), BF16),
            ((8 * out_chan, 4 * LANES), BF16),
            ((4 * out_chan, LANES), F32),
        ],
        hbm=(0, 2, 3, 4, 5, 6), hbm_outs=(0, 2), copies=16, moved=5e6,
    )
    sums_in, ring_pre, raw_down = lax.optimization_barrier((sums_in, ring_pre, raw_down))
    half_x, half_y, half_z = size_x // 2, size_y // 2, size_z // 2
    coarse_out = coarse.reshape(half_x, half_y, out_chan, half_z).transpose(2, 0, 1, 3)

    piece = -(-(16 * in_chan + 4 * out_chan) // devices)
    piece = -(-piece // 8) * 8
    grad_low, grad_high, grad_swap, small, parts = local_call(
        functools.partial(hidden_grad_kernel, in_chan),
        [((rows_6, LANES), BF16)] * 3 + [((8, LANES), F32), ((devices * piece, LANES), BF16)],
        sides, stats_in, sums_in, params, own_hidden, ring_hidden, own_pre, ring_pre, acts_wide,
        stack, raw_down,
        scratch=[
            (stats_shape, F32),
            ring,
            ring,
            ((40, size_z), F32),
            ((rows_64 // 8 * 6 * 3, size_z), BF16),
            ((4 * out_chan, LANES), F32),
            ((3, 24 * in_chan, 4 * out_chan), F32),
            ((rows_6, LANES), BF16),
        ],
        smem=(0,), hbm=(1, 5, 7, 8, 9, 10), hbm_outs=(2,), copies=25, moved=2e7,
    )
    grad_before, grad_after = z_exchange(grad_low, grad_high, grad_swap)
    parts = everyone(parts.reshape(devices, piece, LANES))

    points = local_call(
        functools.partial(point_grad_kernel, only_two, halves, in_chan),
        [((chunks, halves * in_chan, LANES), BF16)],
        sides, grad_low, grad_high, grad_before, grad_after, back_bands, acts, tags,
        scratch=[
            (back_shape, BF16),
            ((groups, size_z), F32),
            ((chunks, 8, LANES), F32),
            ((3 * rows_6, size_z), BF16),
            ((groups * in_chan, size_z), BF16),
        ],
        smem=(0,), hbm=(5, 6, 7), copies=3, moved=2e7,
    )[0]
    parts, points = lax.optimization_barrier((parts, points))
    shapes = [((out_chan, 27 * in_chan), F32), ((out_chan, 8 * out_chan), F32)]
    flat = [((devices * piece, LANES), F32)]
    if aligned:
        both = local_call(
            piece_kernel,
            [((devices, halves * in_chan + piece, LANES), BF16)],
            parts, points, moved=2e6,
        )[0]
        returned, raw_sub, raw_down = local_call(
            functools.partial(last_kernel, halves, in_chan),
            [((in_chan, slot_total), BF16)] + shapes,
            everyone(both), small, scratch=flat, moved=2e6,
        )
    else:
        points = points.reshape(chunks, in_chan, together, slot_cap).transpose(0, 2, 1, 3)
        returned = everyone(points.reshape(devices, in_chan, slot_cap))
        returned = returned.transpose(1, 0, 2).reshape(in_chan, slot_total)
        whole = local_call(sum_kernel, [((devices, piece, LANES), BF16)], parts)[0]
        raw_sub, raw_down = local_call(
            functools.partial(weights_kernel, in_chan), shapes, everyone(whole), small, scratch=flat
        )
    return (
        coarse_out,
        returned,
        raw_sub,
        raw_down,
        small[1, :out_chan],
        small[0, :out_chan],
    )


def solution(mesh):
    in_specs = (
        P(None, AXES),
        P(AXES),
        P(AXES, None),
        P("gx", "gy", "gz"),
        P(),
        P(),
        P(),
        P(),
        P(None, "gx", "gy", "gz"),
    )
    out_specs = (P(None, "gx", "gy", "gz"), P(None, AXES), P(), P(), P(), P())
    return jax.shard_map(
        on_device, mesh=mesh, in_specs=in_specs, out_specs=out_specs, check_vma=False
    )
```
